32 devices in a mesh: row: 8 (over z, y), proto: 4 (over x, core).
Axes of the slice: x: 2, y: 2, z: 4, core: 2. Of those that a mesh axis runs over, the one named last changes fastest.
Arguments:
- embeddings: bfloat16 [2048, 128], P('row'), may hold values from -6.75 to 6.75
- second_view: bfloat16 [2048, 128], P('row'), may hold values from -6.75 to 6.75
- prototypes: bfloat16 [16384, 128], P('proto'), may hold values from -6.75 to 6.75
- row_scale: float32 [2048], P('row'), may hold values from 1 to 16, as said below
- col_scale: float32 [16384], P('proto'), may hold values from 1 to 16, as said below
Outputs:
- embed_grad: float32 [2048, 128], P(('row', 'proto'))
- proto_grad: float32 [16384, 128], P(('proto', 'row'))
The draws below stay inside these ranges and needn't reach their ends.
Inputs may be any that keep to these rules, and one draw needn't show every extreme that they name: `row_scale`: positive scalings. `col_scale`: positive scalings.
All inputs are finite; a program needn't handle non-finite values.
Results may differ from the reference program's by a relative error of at most 0.0025.
Values may be sent and summed in bfloat16 or wider, within the bound.
No kernel may reach another device: no remote copies, remote signals or barrier semaphores. Data moves between devices by JAX's collectives and lax.ppermute only.
A program may use at most 64 MiB of HBM per device.

```python
import math
import jax
import jax.numpy as jnp
from jax import lax

D = 128
ROWS_DEV = 256
ITERS = 4
ROWS = 2048
PROTOS = 16384
N_ROW = 8


def spread_draw(key, row_total):
    noise_key, sign_key, size_key = jax.random.split(key, 3)
    values = jax.random.normal(noise_key, (row_total, D), jnp.float32)
    lead_size = jnp.array([3.7, 2.5], jnp.float32)
    values = jnp.clip(values, -3.0, 3.0)
    signs = jnp.where(jax.random.bernoulli(sign_key, 0.5, (row_total, 2)), 1.0, -1.0)
    factors = jax.random.uniform(size_key, (row_total, 2), jnp.float32, minval=0.7, maxval=1.3)
    leading = signs * factors * lead_size[None, :]
    return jnp.concatenate((leading, values[:, 2:]), 1)


def view_draw(key, row_total):
    first = spread_draw(jax.random.fold_in(key, 7), row_total)
    noise_key, mean_key, rest_key = jax.random.split(jax.random.fold_in(key, 13), 3)
    noise = jnp.clip(jax.random.normal(noise_key, (row_total, D), jnp.float32), -3.0, 3.0)
    lead_mean = 3.5
    mean_signs = jnp.where(jax.random.bernoulli(mean_key, 0.5, (2,)), 1.0, -1.0)
    common = jnp.concatenate((lead_mean * mean_signs, 0.3 * jax.random.normal(rest_key, (D - 2,), jnp.float32)))
    lead_mask = jnp.arange(D) < 2
    first_mix = jnp.where(lead_mask, 0.4, 0.6)
    noise_mix = jnp.where(lead_mask, 0.5, 0.8)
    values = common[None, :] + first_mix[None, :] * first + noise_mix[None, :] * noise
    return jnp.clip(values, -6.75, 6.75)


def scale_draw(key, length):
    position = jnp.arange(length).astype(jnp.float32) / length
    jitter = jax.random.uniform(key, (length,), jnp.float32, minval=-0.3, maxval=2.9)
    logs = jnp.clip(math.log(3.0) * position + jitter, 0.0, math.log(16.0))
    return jnp.clip(jnp.exp(logs), 1.0, 16.0)


def draw_embeddings(key, part):
    return spread_draw(jax.random.fold_in(key, 7), ROWS).astype(jnp.bfloat16)


def draw_second_view(key, part):
    return view_draw(key, ROWS).astype(jnp.bfloat16)


def draw_prototypes(key, part):
    return spread_draw(jax.random.fold_in(key, 11), PROTOS).astype(jnp.bfloat16)


def draw_row_scale(key, part):
    return scale_draw(jax.random.fold_in(key, 3), ROWS)


def draw_col_scale(key, part):
    return scale_draw(jax.random.fold_in(key, 5), PROTOS)


def setup_inputs(seed: int = 0) -> dict:
    key_list = jax.random.split(jax.random.key(seed), 6)
    embeddings = draw_embeddings(jax.random.fold_in(key_list[5], 71), 0)
    second_view = draw_second_view(jax.random.fold_in(key_list[5], 71), 0)
    prototypes = draw_prototypes(jax.random.fold_in(key_list[5], 71), 0)
    row_scale = draw_row_scale(jax.random.fold_in(key_list[5], 71), 0)
    col_scale = draw_col_scale(jax.random.fold_in(key_list[5], 71), 0)
    return {"embeddings": embeddings, "second_view": second_view, "prototypes": prototypes, "row_scale": row_scale, "col_scale": col_scale}


def reference(embeddings, second_view, prototypes, row_scale, col_scale):
    logit_scale = 1.0 / (0.05 * D)
    view_scale = 1.0 / (0.1 * D)
    plan_mass = 64.0 * PROTOS
    proto_wide = prototypes.astype(jnp.float32)
    emb_blocks = embeddings.reshape(N_ROW, ROWS_DEV, D)
    view_blocks = second_view.reshape(N_ROW, ROWS_DEV, D)
    scale_blocks = row_scale.reshape(N_ROW, ROWS_DEV)

    def plan_block(emb_block, scale_block):
        logits = jnp.dot(emb_block.astype(jnp.float32), proto_wide.T) * logit_scale
        return scale_block[:, None] * col_scale[None, :] * jnp.exp(logits) / plan_mass

    def cot_block(view_block):
        return -jnp.dot(view_block.astype(jnp.float32), proto_wide.T) * view_scale

    zero_cols = jnp.zeros((PROTOS,), jnp.float32)

    def first_pass(running, blocks):
        emb_block, view_block, scale_block = blocks
        plan = plan_block(emb_block, scale_block)
        weighted = plan * cot_block(view_block)
        return (running[0] + plan.sum(0), running[1] + weighted.sum(0)), (plan.sum(1), weighted.sum(1))

    (col_mass, col_weight), (row_mass, row_weight) = lax.scan(first_pass, (zero_cols, zero_cols), (emb_blocks, view_blocks, scale_blocks))
    row_mass = row_mass.reshape(ROWS)
    row_weight = row_weight.reshape(ROWS)

    def column_pass(row_dual):
        dual_blocks = row_dual.reshape(N_ROW, ROWS_DEV)

        def add_block(running, blocks):
            emb_block, scale_block, dual_block = blocks
            return running + jnp.dot(dual_block, plan_block(emb_block, scale_block), precision=lax.Precision.HIGHEST), None

        summed, unused = lax.scan(add_block, zero_cols, (emb_blocks, scale_blocks, dual_blocks))
        return summed

    def row_pass(col_dual):
        def one_block(blocks):
            emb_block, scale_block = blocks
            return jnp.dot(plan_block(emb_block, scale_block), col_dual, precision=lax.Precision.HIGHEST)

        return lax.map(one_block, (emb_blocks, scale_blocks)).reshape(ROWS)

    row_dual = row_weight / row_mass
    col_dual = (col_weight - column_pass(row_dual)) / col_mass
    for sweep in range(ITERS - 1):
        row_dual = (row_weight - row_pass(col_dual)) / row_mass
        col_dual = (col_weight - column_pass(row_dual)) / col_mass

    def final_pass(running, blocks):
        emb_block, view_block, scale_block, dual_block = blocks
        plan = plan_block(emb_block, scale_block)
        logit_grad = plan * (cot_block(view_block) - dual_block[:, None] - col_dual[None, :])
        scaled_grad = lax.optimization_barrier((logit_scale * logit_grad).astype(jnp.bfloat16)).astype(jnp.float32)
        scaled_plan = lax.optimization_barrier((-view_scale * plan).astype(jnp.bfloat16)).astype(jnp.float32)
        embed_part = jnp.dot(scaled_grad, proto_wide)
        proto_part = jnp.dot(scaled_grad.T, emb_block.astype(jnp.float32)) + jnp.dot(scaled_plan.T, view_block.astype(jnp.float32))
        return running + proto_part, embed_part

    proto_grad, embed_parts = lax.scan(final_pass, jnp.zeros((PROTOS, D), jnp.float32), (emb_blocks, view_blocks, scale_blocks, row_dual.reshape(N_ROW, ROWS_DEV)))
    return embed_parts.reshape(ROWS, D), proto_grad
```

```python
import jax
import jax.numpy as jnp
from jax import lax
from jax.sharding import PartitionSpec as P

ITERS = 4


def contract_rows(left, right):
    return lax.dot_general(
        left, right, (((0,), (0,)), ((), ())), preferred_element_type=jnp.float32
    )


def contract_width(left, right):
    return lax.dot_general(
        left, right, (((1,), (1,)), ((), ())), preferred_element_type=jnp.float32
    )


def swap(value, axis, step):
    size = lax.axis_size(axis)
    return lax.ppermute(value, axis, [(i, i ^ step) for i in range(size)])


def sum_over(value, axis):
    size = lax.axis_size(axis)
    parts = [value] + [swap(value, axis, step) for step in range(1, size)]
    return sum(parts[1:], parts[0])


def scatter_sum(value, axis):
    size = lax.axis_size(axis)
    me = lax.axis_index(axis)
    rows = value.shape[0] // size
    block = lambda owner: lax.dynamic_slice_in_dim(value, owner * rows, rows, 0)
    total = block(me)
    for step in range(1, size):
        total = total + swap(block(me ^ step), axis, step)
    return total


def per_device(embeddings, second_view, prototypes, row_scale, col_scale):
    feat_width = embeddings.shape[1]
    proto_count = prototypes.shape[0]
    logit_scale = 1.0 / (0.05 * feat_width)
    view_scale = 1.0 / (0.1 * feat_width)
    plan_mass = 64.0 * proto_count * lax.axis_size("proto")

    logits = contract_width(embeddings, prototypes) * logit_scale
    plan = row_scale[:, None] * col_scale[None, :] * jnp.exp(logits) / plan_mass
    cotangent = -contract_width(second_view, prototypes) * view_scale
    weighted = plan * cotangent

    row_mass, row_weight = sum_over(jnp.stack((plan.sum(1), weighted.sum(1))), "proto")
    row_dual = row_weight / row_mass
    sums = jnp.stack((plan.sum(0), weighted.sum(0), (row_dual[:, None] * plan).sum(0)))
    col_mass, col_weight, product = sum_over(sums, "row")
    col_dual = (col_weight - product) / col_mass
    for sweep in range(ITERS - 1):
        product = sum_over((plan * col_dual[None, :]).sum(1), "proto")
        row_dual = (row_weight - product) / row_mass
        product = sum_over((plan * row_dual[:, None]).sum(0), "row")
        col_dual = (col_weight - product) / col_mass
    logit_grad = plan * (cotangent - row_dual[:, None] - col_dual[None, :])
    scaled_grad = (logit_scale * logit_grad).astype(jnp.bfloat16)
    scaled_plan = (-view_scale * plan).astype(jnp.bfloat16)
    embed_grad = scatter_sum(
        jnp.dot(scaled_grad, prototypes, preferred_element_type=jnp.float32), "proto"
    )
    proto_grad = scatter_sum(
        contract_rows(scaled_grad, embeddings) + contract_rows(scaled_plan, second_view), "row"
    )
    return (embed_grad, proto_grad)


def solution(mesh):
    return jax.shard_map(
        per_device,
        mesh=mesh,
        in_specs=(P("row", None), P("row", None), P("proto", None), P("row"), P("proto")),
        out_specs=(P(("row", "proto"), None), P(("proto", "row"), None)),
        check_vma=False,
    )
```

```python
import functools
import math

import jax
import jax.numpy as jnp
from jax import lax
from jax.experimental import pallas as pl
from jax.experimental.pallas import tpu as pltpu
from jax.sharding import PartitionSpec as P

ITERS = 4
CHUNK = 512
STEP = 256
EXT = 16
PLAN_BYTES = 24 << 20
LOG2E = 1.4426950408889634
F32, BF16 = jnp.float32, jnp.bfloat16
NT = (((1,), (1,)), ((), ()))
NN = (((1,), (0,)), ((), ()))


def mm(left, right, dims=NN):
    return lax.dot_general(left, right, dims, preferred_element_type=F32)


def swap(value, axis, step):
    size = lax.axis_size(axis)
    return lax.ppermute(value, axis, [(i, i ^ step) for i in range(size)])


def as_column(row, width):
    tall = jnp.transpose(jnp.broadcast_to(row, (128, row.shape[1])))
    return jnp.concatenate([tall] * (width // 128), 1)


def rows_of(pieces, height=EXT):
    index = lax.broadcasted_iota(jnp.int32, (height, pieces[0].shape[1]), 0)
    total = jnp.zeros(index.shape, F32)
    for place, piece in enumerate(pieces):
        total = jnp.where(index == place, piece, total)
    return total


def pieces_of(row):
    out = []
    for _ in range(3):
        out.append(row.astype(BF16).astype(F32))
        row = row - out[-1]
    return out, [jnp.ones_like(row)] * 3


def prep_kernel(logit_scale, ids, embeddings, second_view, row_scale, send_out):
    rows, width = embeddings.shape

    @pl.when(ids[1] & 1 == 0)
    def _():
        logs, ones = pieces_of(jnp.log(row_scale[...]) / logit_scale)
        send_out[0:width, :] = jnp.transpose(embeddings[...].astype(F32)).astype(BF16)
        send_out[width:width + EXT, :] = rows_of(logs + ones).astype(BF16)

    @pl.when(ids[1] & 1 != 0)
    def _():
        send_out[0:width, :] = jnp.transpose(second_view[...].astype(F32)).astype(BF16)
        send_out[width:width + EXT, :] = jnp.zeros((EXT, rows), BF16)


def turn_kernel(logit_scale, log_mass, ids, protos, col_scale, protos_out, protos_t, token):
    count = protos_out.shape[0]
    width = protos.shape[1]
    token[...] = jnp.zeros_like(token)

    def step(index, carry):
        here = pl.ds(pl.multiple_of(index * CHUNK, CHUNK), CHUNK)
        there = pl.ds(pl.multiple_of((2 * index + (ids[0] & 1)) * CHUNK, CHUNK), CHUNK)
        block = protos[there, :]
        logs, ones = pieces_of((jnp.log(col_scale[:, there]) - log_mass) / logit_scale)
        protos_out[here, 0:width] = block
        protos_out[here, width:] = jnp.transpose(rows_of(ones + logs, width)).astype(BF16)
        protos_t[:, here] = jnp.transpose(block.astype(F32)).astype(BF16)
        return carry

    lax.fori_loop(0, count // CHUNK, step, 0)


def stack_kernel(count, *refs):
    for place in range(count):
        refs[-1][place] = refs[place][...]


def add_kernel(left, right, out):
    out[...] = left[...] + right[...]


def plan_kernel(logit_scale, view_scale, ids, protos, mine_a, theirs_a, mine_b, theirs_b, plan_out, cols_out, sums_out, emb_ext, view_t, row_mass, row_weight):
    pairs, high, rows = mine_a.shape
    blocks = 2 * pairs
    count = protos.shape[0]
    width = view_t.shape[0]
    scale = logit_scale * LOG2E
    emb_ext[high:, :] = jnp.zeros((emb_ext.shape[0] - high, blocks * rows), BF16)

    def fill(embs, views):
        for block in range(blocks):
            cols = slice(block * rows, (block + 1) * rows)
            emb_ext[0:high, cols] = embs[block % 2][block // 2]
            view_t[:, cols] = views[block % 2][block // 2, 0:width, :]

    for core in range(2):
        for odd in range(2):
            a, b = ((mine_a, theirs_a), (mine_b, theirs_b)) if core == 0 else ((theirs_a, mine_a), (theirs_b, mine_b))
            low, upper = (a, b) if odd == 0 else (b, a)
            is_this = jnp.logical_and(ids[1] & 1 == core, ids[0] & 1 == odd)
            pl.when(is_this)(functools.partial(fill, (low[0], upper[0]), (low[1], upper[1])))
    row_mass[...] = jnp.zeros_like(row_mass)
    row_weight[...] = jnp.zeros_like(row_weight)

    def folded(block):
        tiles = [block[:, left:left + 128] for left in range(0, block.shape[1], 128)]
        across = tiles[0]
        for tile in tiles[1:]:
            across = across + tile
        return across, jnp.sum(block.reshape(block.shape[0] // 8, 8, block.shape[1]), axis=0)

    def step(index, carry):
        here = pl.ds(pl.multiple_of(index * CHUNK, CHUNK), CHUNK)
        mass = weight = jnp.zeros((CHUNK, 128), F32)
        for block in range(blocks):
            cols = slice(block * rows, (block + 1) * rows)
            plan = jnp.exp2(scale * mm(protos[here, :], emb_ext[:, cols]))
            plan_out[here, cols] = plan
            across, down = folded(plan)
            mass = mass + across
            row_mass[:, cols] += down
            across, down = folded(plan * mm(protos[here, 0:width], view_t[:, cols]))
            weight = weight + across
            row_weight[:, cols] += down
        cols_out[0:1, here] = jnp.sum(jnp.transpose(mass), axis=0, keepdims=True)
        cols_out[1:2, here] = -view_scale * jnp.sum(jnp.transpose(weight), axis=0, keepdims=True)
        return carry

    lax.fori_loop(0, count // CHUNK, step, 0)
    sums_out[0:1, :] = jnp.sum(row_mass[...], axis=0, keepdims=True)
    sums_out[1:2, :] = -view_scale * jnp.sum(row_weight[...], axis=0, keepdims=True)


def added(parts):
    total = parts[0][...]
    for other in parts[1:]:
        total = total + other[...]
    return total


def by_rows(block, spread):
    tall, wide = block.shape
    sums = []
    for top in range(0, tall, 64):
        group = [jnp.zeros((8, 128), F32) for _ in range(8)]
        for left in range(0, wide, 128):
            dual = spread[:, left:left + 128]
            for place in range(8):
                here = slice(top + place * 8, top + (place + 1) * 8)
                group[place] = group[place] + block[here, left:left + 128] * dual
        sums += group
    return jnp.sum(jnp.transpose(jnp.concatenate(sums)), axis=0, keepdims=True)


def by_cols(block, column):
    tall, wide = block.shape
    sums = [jnp.zeros((8, 128), F32) for _ in range(wide // 128)]
    for top in range(0, tall, 8):
        dual = column[top:top + 8, :]
        for place in range(wide // 128):
            sums[place] = sums[place] + block[top:top + 8, place * 128:(place + 1) * 128] * dual
    return jnp.concatenate(sums, 1)


def chunk(index):
    return pl.ds(pl.multiple_of(index * STEP, STEP), STEP)


def sweep_kernel(opening, shares, plan, cols, *refs):
    if opening:
        parts, (_, _, sums_out, part_out, spread, total) = refs[:shares], refs[shares:]
        sums_out[...] = added(parts)
        row_dual = sums_out[1:2, :] / sums_out[0:1, :]
    else:
        (sums, *parts), (_, _, part_out, spread, total) = refs[:shares + 1], refs[shares + 1:]
        row_dual = (sums[1:2, :] - added(parts)) / sums[0:1, :]
    spread[...] = jnp.broadcast_to(row_dual, spread.shape)
    total[...] = jnp.zeros_like(total)
    steps = plan.shape[0] // STEP

    def duals(index):
        here = chunk(index)
        product = by_rows(plan.at[here, :], spread)
        return as_column((cols[1:2, here] - product) / cols[0:1, here], 128)

    def step(index, dual):
        product = by_cols(plan.at[chunk(index - 1), :], dual)
        dual = duals(index)
        total[...] += product
        return dual

    last = lax.fori_loop(1, steps, step, duals(0))
    total[...] += by_cols(plan.at[chunk(steps - 1), :], last)
    part_out[...] = jnp.sum(total[...], axis=0, keepdims=True)


def embed_before_kernel(logit_scale, protos, emb_ext, after, entry_out, token):
    del after
    scale = logit_scale * LOG2E
    token[...] = jnp.zeros_like(token)

    def step(index, carry):
        here = chunk(index)
        entry_out[here, :] = logit_scale * jnp.exp2(scale * mm(protos[here, :], emb_ext[:, 0:entry_out.shape[1]]))
        return carry

    lax.fori_loop(0, protos.shape[0] // STEP, step, 0)


def embed_kernel(view_scale, shares, ids, plan, cols, sums, protos, protos_t, view_t, entries, *refs):
    parts, (duals_out, rows_out, keep, give, spread, total, whole) = refs[:shares], refs[shares:]
    width = protos_t.shape[0]
    rows = entries.shape[1]
    rows_out[...] = (sums[1:2, :] - added(parts)) / sums[0:1, :]
    spread[...] = jnp.broadcast_to(rows_out[...], spread.shape)
    own_dual = rows_out[:, 0:rows]
    total[...] = jnp.zeros_like(total)
    steps = plan.shape[0] // STEP

    def duals(index):
        here = chunk(index)
        return (cols[1:2, here] - by_rows(plan.at[here, :], spread)) / cols[0:1, here]

    def gradient(index, dual):
        here = chunk(index)
        cot = -view_scale * mm(protos[here, 0:width], view_t[:, 0:rows])
        grad = entries[here, :] * (cot - own_dual - as_column(dual, rows))
        return mm(protos_t[:, here], grad.astype(BF16))

    def step(index, dual):
        share = gradient(index - 1, dual)
        duals_out[:, chunk(index - 1)] = dual
        dual = duals(index)
        total[...] += share
        return dual

    last = lax.fori_loop(1, steps, step, duals(0))
    duals_out[:, chunk(steps - 1)] = last
    total[...] += gradient(steps - 1, last)
    whole[...] = jnp.transpose(total[...])
    tall = keep.shape[1]
    for place in range(shares):
        above, beside = divmod(place, shares // 2)
        to = ((ids[0] & 1) ^ above) * shares + (ids[1] ^ (2 * beside))
        keep[place] = whole[pl.ds(pl.multiple_of(to * tall, tall), tall), :]
        give[place] = whole[pl.ds(pl.multiple_of((to ^ 1) * tall, tall), tall), :]


def proto_before_kernel(logit_scale, view_scale, ids, protos, emb_ext, view_t, after, entry_out, second_out, token):
    del after
    own, rows = entry_out.shape
    width = second_out.shape[1]
    scale = logit_scale * LOG2E
    token[...] = jnp.zeros_like(token)
    here = pl.ds(pl.multiple_of((ids[0] >> 1) * own, own), own)
    total = jnp.zeros((own, width), F32)
    for start in range(0, rows, 2 * width):
        cols = slice(start, start + 2 * width)
        exact = jnp.exp2(scale * mm(protos[here, :], emb_ext[:, cols]))
        entry_out[:, cols] = logit_scale * exact
        total = total + mm((-view_scale * exact).astype(BF16), view_t[:, cols], NT)
    second_out[...] = total


def proto_kernel(view_scale, ids, protos, emb_ext, view_t, entries, second, col_dual, row_dual, out):
    own, width = out.shape
    here = pl.ds(pl.multiple_of((ids[0] >> 1) * own, own), own)
    column = as_column(col_dual[:, here], 2 * width)
    total = second[...]
    for start in range(0, entries.shape[1], 2 * width):
        cols = slice(start, start + 2 * width)
        cot = -view_scale * mm(protos[here, 0:width], view_t[:, cols])
        grad = entries[:, cols] * (cot - row_dual[:, cols] - column)
        total = total + mm(grad.astype(BF16), emb_ext[0:width, cols], NT)
    out[...] = total


def call(kernel, out_shape, name, scalars=0, scratch=(), aliases=None, limit=16):
    def run(*args):
        whole = pl.BlockSpec(memory_space=pltpu.VMEM)
        small = pl.BlockSpec(memory_space=pltpu.SMEM)
        return pl.pallas_call(
            kernel,
            out_shape=out_shape,
            in_specs=[small] * scalars + [whole] * (len(args) - scalars),
            out_specs=jax.tree.map(lambda _: whole, out_shape),
            scratch_shapes=[pltpu.VMEM(dims, dtype) for dtype, *dims in scratch],
            input_output_aliases=aliases or {},
            compiler_params=pltpu.CompilerParams(vmem_limit_bytes=limit << 20),
            name=name,
        )(*args)

    return run


def swap_both(value, above, beside):
    shares = lax.axis_size("proto")
    pairs = [
        (row * shares + col, (row ^ above) * shares + (col ^ beside))
        for row in range(lax.axis_size("row"))
        for col in range(shares)
    ]
    return lax.ppermute(value, ("row", "proto"), pairs)


def others():
    shares = lax.axis_size("proto")
    return [(above, beside) for above in range(2) for beside in range(0, shares, 2)]


def exchange(part):
    near = call(add_kernel, jax.ShapeDtypeStruct(part.shape, F32), "add", limit=2)(part, swap(part, "proto", 1))
    return [near if pair == (0, 0) else swap_both(near, *pair) for pair in others()]


def kept_plan(embeddings, second_view, prototypes, row_scale, col_scale):
    rows, width = embeddings.shape
    blocks, shares = lax.axis_size("row"), lax.axis_size("proto")
    all_rows = rows * blocks
    count = prototypes.shape[0] // 2
    own = 2 * count // blocks
    ids = jnp.stack((lax.axis_index("row"), lax.axis_index("proto")))
    scales = (1.0 / (0.05 * width), 1.0 / (0.1 * width))
    log_mass = math.log(64.0 * prototypes.shape[0] * shares)
    shape = lambda *dims, dtype=F32: jax.ShapeDtypeStruct(dims, dtype)
    form = lambda kernel: functools.partial(kernel, *scales)
    there = lambda value: pltpu.with_memory_space_constraint(value, pltpu.HBM)
    row_scale = row_scale.reshape(1, rows)
    col_scale = col_scale.reshape(1, 2 * count)
    half = shape(width + EXT, rows, dtype=BF16)
    send = call(functools.partial(prep_kernel, scales[0]), half, "prepare", scalars=1)(
        ids, there(embeddings), there(second_view), there(row_scale)
    )
    protos, protos_t, token = call(
        functools.partial(turn_kernel, scales[0], log_mass),
        (shape(count, 2 * width, dtype=BF16), shape(width, count, dtype=BF16), shape(8, 128)),
        "turn",
        scalars=1,
        limit=4,
    )(ids, there(prototypes), there(col_scale))
    pairs = blocks // 2
    stack = call(functools.partial(stack_kernel, pairs), shape(pairs, width + EXT, rows, dtype=BF16), "stack", limit=2)
    direct = [send] + [swap(send, "row", step) for step in range(2, blocks, 2)]
    mine_a = stack(*direct)
    theirs_a = swap(mine_a, "proto", 1)
    mine_b = stack(*[swap(value, "row", 1) for value in direct], token)
    theirs_b = swap(mine_b, "proto", 1)

    kept = pltpu.VMEM((count, all_rows), F32)
    plan, cols, sums, emb_ext, view_t = call(
        form(plan_kernel),
        (kept, shape(2, count), shape(2, all_rows), shape(2 * width, all_rows, dtype=BF16), shape(width, all_rows, dtype=BF16)),
        "plan",
        scalars=1,
        scratch=[(F32, 8, all_rows), (F32, 8, all_rows)],
        limit=12,
    )(ids, protos, mine_a, theirs_a, mine_b, theirs_b)

    work = [(F32, 8, all_rows), (F32, 8, all_rows)]
    token = shape(8, 128)
    parts = exchange(sums)
    entries, done = call(
        functools.partial(embed_before_kernel, scales[0]),
        (shape(count, 2 * rows), token),
        "embed_before",
        limit=6,
    )(protos, emb_ext, parts[0])
    plan, sums, part = call(
        functools.partial(sweep_kernel, True, shares),
        (kept, shape(2, all_rows), shape(1, all_rows)),
        "sweep",
        scratch=work,
        aliases={0: 0},
        limit=4,
    )(plan, cols, *parts, done)
    for sweep in range(ITERS - 2):
        parts = exchange(part)
        if sweep == 0:
            own_entries, second, done = call(
                form(proto_before_kernel),
                (shape(own, all_rows), shape(own, width), token),
                "proto_before",
                scalars=1,
                limit=6,
            )(ids, protos, emb_ext, view_t, parts[0])
        plan, part = call(
            functools.partial(sweep_kernel, False, shares),
            (kept, shape(1, all_rows)),
            "sweep",
            scratch=work,
            aliases={0: 0},
            limit=4,
        )(plan, cols, sums, *parts, done)
    pieces = shape(shares, rows // shares, width)
    col_dual, row_dual, keep, give = call(
        functools.partial(embed_kernel, scales[1], shares),
        (shape(1, count), shape(1, all_rows), pieces, pieces),
        "embed_grad",
        scalars=1,
        scratch=work[:1] + [(F32, width, 2 * rows), (F32, 2 * rows, width)],
        limit=6,
    )(ids, plan, cols, sums, protos, protos_t, view_t, entries, *exchange(part))
    near = call(add_kernel, pieces, "add", limit=2)(keep, swap(give, "proto", 1))
    embed_grad = near[0]
    for place, pair in list(enumerate(others()))[1:]:
        embed_grad = embed_grad + swap_both(near[place], *pair)
    proto_grad = call(functools.partial(proto_kernel, scales[1]), shape(own, width), "proto_grad", scalars=1, limit=6)(
        ids, protos, emb_ext, view_t, own_entries, second, col_dual, row_dual
    )
    return embed_grad, proto_grad


def contract_rows(left, right):
    return mm(left, right, (((0,), (0,)), ((), ())))


def contract_width(left, right):
    return mm(left, right, NT)


def sum_over(value, axis):
    size = lax.axis_size(axis)
    parts = [value] + [swap(value, axis, step) for step in range(1, size)]
    return sum(parts[1:], parts[0])


def scatter_sum(value, axis):
    size = lax.axis_size(axis)
    me = lax.axis_index(axis)
    rows = value.shape[0] // size
    block = lambda owner: lax.dynamic_slice_in_dim(value, owner * rows, rows, 0)
    total = block(me)
    for step in range(1, size):
        total = total + swap(block(me ^ step), axis, step)
    return total


def split_plan(embeddings, second_view, prototypes, row_scale, col_scale):
    feat_width = embeddings.shape[1]
    proto_count = prototypes.shape[0]
    logit_scale = 1.0 / (0.05 * feat_width)
    view_scale = 1.0 / (0.1 * feat_width)
    plan_mass = 64.0 * proto_count * lax.axis_size("proto")

    logits = contract_width(embeddings, prototypes) * logit_scale
    plan = row_scale[:, None] * col_scale[None, :] * jnp.exp(logits) / plan_mass
    cotangent = -contract_width(second_view, prototypes) * view_scale
    weighted = plan * cotangent

    row_mass, row_weight = sum_over(jnp.stack((plan.sum(1), weighted.sum(1))), "proto")
    row_dual = row_weight / row_mass
    sums = jnp.stack((plan.sum(0), weighted.sum(0), (row_dual[:, None] * plan).sum(0)))
    col_mass, col_weight, product = sum_over(sums, "row")
    col_dual = (col_weight - product) / col_mass
    for sweep in range(ITERS - 1):
        product = sum_over((plan * col_dual[None, :]).sum(1), "proto")
        row_dual = (row_weight - product) / row_mass
        product = sum_over((plan * row_dual[:, None]).sum(0), "row")
        col_dual = (col_weight - product) / col_mass
    logit_grad = plan * (cotangent - row_dual[:, None] - col_dual[None, :])
    scaled_grad = (logit_scale * logit_grad).astype(jnp.bfloat16)
    scaled_plan = (-view_scale * plan).astype(jnp.bfloat16)
    embed_grad = scatter_sum(
        jnp.dot(scaled_grad, prototypes, preferred_element_type=jnp.float32), "proto"
    )
    proto_grad = scatter_sum(
        contract_rows(scaled_grad, embeddings) + contract_rows(scaled_plan, second_view), "row"
    )
    return (embed_grad, proto_grad)


def per_device(embeddings, second_view, prototypes, row_scale, col_scale):
    blocks, shares = lax.axis_size("row"), lax.axis_size("proto")
    rows, width = embeddings.shape
    count = prototypes.shape[0]
    fits = rows * blocks * count * 2 <= PLAN_BYTES
    even = all(n & (n - 1) == 0 and n > 1 for n in (blocks, shares))
    even = even and rows % (16 * shares) == 0 and rows % width == 0
    tiled = rows % 128 == 0 and width % 128 == 0 and count == blocks * CHUNK and blocks % 4 == 0
    form = kept_plan if fits and even and tiled else split_plan
    return form(embeddings, second_view, prototypes, row_scale, col_scale)


def solution(mesh):
    return jax.shard_map(
        per_device,
        mesh=mesh,
        in_specs=(P("row", None), P("row", None), P("proto", None), P("row"), P("proto")),
        out_specs=(P(("row", "proto"), None), P(("proto", "row"), None)),
        check_vma=False,
    )
```

```python
import functools
import math

import jax
import jax.numpy as jnp
from jax import lax
from jax.experimental import pallas as pl
from jax.experimental.pallas import tpu as pltpu
from jax.sharding import PartitionSpec as P

ITERS = 4
CHUNK = 512
STEP = 256
EXT = 16
PLAN_BYTES = 24 << 20
LOG2E = 1.4426950408889634
F32, BF16 = jnp.float32, jnp.bfloat16
NT = (((1,), (1,)), ((), ()))
NN = (((1,), (0,)), ((), ()))


def mm(left, right, dims=NN):
    return lax.dot_general(left, right, dims, preferred_element_type=F32)


def swap(value, axis, step):
    size = lax.axis_size(axis)
    return lax.ppermute(value, axis, [(i, i ^ step) for i in range(size)])


def as_column(row, width):
    tall = jnp.transpose(jnp.broadcast_to(row, (128, row.shape[1])))
    return jnp.concatenate([tall] * (width // 128), 1)


def rows_of(pieces, height=EXT):
    index = lax.broadcasted_iota(jnp.int32, (height, pieces[0].shape[1]), 0)
    total = jnp.zeros(index.shape, F32)
    for place, piece in enumerate(pieces):
        total = jnp.where(index == place, piece, total)
    return total


def pieces_of(row):
    out = []
    for _ in range(3):
        out.append(row.astype(BF16).astype(F32))
        row = row - out[-1]
    return out, [jnp.ones_like(row)] * 3


def prep_kernel(logit_scale, ids, embeddings, second_view, row_scale, send_out):
    rows, width = embeddings.shape

    @pl.when(ids[1] & 1 == 0)
    def _():
        logs, ones = pieces_of(jnp.log(row_scale[...]) / logit_scale)
        send_out[0:width, :] = jnp.transpose(embeddings[...].astype(F32)).astype(BF16)
        send_out[width:width + EXT, :] = rows_of(logs + ones).astype(BF16)

    @pl.when(ids[1] & 1 != 0)
    def _():
        send_out[0:width, :] = jnp.transpose(second_view[...].astype(F32)).astype(BF16)
        send_out[width:width + EXT, :] = jnp.zeros((EXT, rows), BF16)


def extend_kernel(logit_scale, log_mass, ids, protos, col_scale, protos_out, token):
    count = protos_out.shape[0]
    width = protos.shape[1]
    token[...] = jnp.zeros_like(token)

    def step(index, carry):
        here = pl.ds(pl.multiple_of(index * CHUNK, CHUNK), CHUNK)
        there = pl.ds(pl.multiple_of((2 * index + (ids[0] & 1)) * CHUNK, CHUNK), CHUNK)
        block = protos[there, :]
        logs, ones = pieces_of((jnp.log(col_scale[:, there]) - log_mass) / logit_scale)
        protos_out[here, 0:width] = block
        protos_out[here, width:] = jnp.transpose(rows_of(ones + logs, width)).astype(BF16)
        return carry

    lax.fori_loop(0, count // CHUNK, step, 0)


def stack_kernel(count, *refs):
    for place in range(count):
        refs[-1][place] = refs[place][...]


def add_kernel(left, right, out):
    out[...] = left[...] + right[...]


def plan_kernel(logit_scale, view_scale, second, ids, protos, mine, theirs, *refs):
    if second:
        _, cols_in, sums_in, *refs = refs
    plan_out, cols_out, sums_out, emb_ext, view_t, row_mass, row_weight = refs
    blocks, high, rows = mine.shape
    count = protos.shape[0]
    width = view_t.shape[0]
    scale = logit_scale * LOG2E
    first_col = blocks * rows if second else 0
    emb_ext[high:, :] = jnp.zeros((emb_ext.shape[0] - high, blocks * rows), BF16)

    def fill(emb, view):
        for block in range(blocks):
            cols = slice(block * rows, (block + 1) * rows)
            emb_ext[0:high, cols] = emb[block]
            view_t[:, cols] = view[block, 0:width, :]

    pl.when(ids[1] & 1 == 0)(lambda: fill(mine, theirs))
    pl.when(ids[1] & 1 != 0)(lambda: fill(theirs, mine))
    row_mass[...] = jnp.zeros_like(row_mass)
    row_weight[...] = jnp.zeros_like(row_weight)

    def folded(block):
        tiles = [block[:, left:left + 128] for left in range(0, block.shape[1], 128)]
        across = tiles[0]
        for tile in tiles[1:]:
            across = across + tile
        return across, jnp.sum(block.reshape(block.shape[0] // 8, 8, block.shape[1]), axis=0)

    def step(index, carry):
        here = pl.ds(pl.multiple_of(index * CHUNK, CHUNK), CHUNK)
        mass = weight = jnp.zeros((CHUNK, 128), F32)
        for block in range(blocks):
            cols = slice(block * rows, (block + 1) * rows)
            plan = jnp.exp2(scale * mm(protos[here, :], emb_ext[:, cols]))
            plan_out[here, first_col + block * rows:first_col + (block + 1) * rows] = plan
            across, down = folded(plan)
            mass = mass + across
            row_mass[:, cols] += down
            across, down = folded(plan * mm(protos[here, 0:width], view_t[:, cols]))
            weight = weight + across
            row_weight[:, cols] += down
        mass = jnp.sum(jnp.transpose(mass), axis=0, keepdims=True)
        weight = -view_scale * jnp.sum(jnp.transpose(weight), axis=0, keepdims=True)
        cols_out[0:1, here] = mass + cols_in[0:1, here] if second else mass
        cols_out[1:2, here] = weight + cols_in[1:2, here] if second else weight
        return carry

    lax.fori_loop(0, count // CHUNK, step, 0)
    if second:
        sums_out[:, 0:first_col] = sums_in[...]
    sums_out[0:1, first_col:] = jnp.sum(row_mass[...], axis=0, keepdims=True)
    sums_out[1:2, first_col:] = -view_scale * jnp.sum(row_weight[...], axis=0, keepdims=True)


def received_kernel(plain, turned, *refs):
    out = refs[-1]
    half = out.shape[1] // 2
    other = added(refs[plain:plain + turned])
    out[...] = added(refs[:plain]) + jnp.concatenate((other[:, half:], other[:, :half]), 1)


def added(parts):
    total = parts[0][...]
    for other in parts[1:]:
        total = total + other[...]
    return total


def by_rows(block, spread):
    tall, wide = block.shape
    sums = []
    for top in range(0, tall, 64):
        group = [jnp.zeros((8, 128), F32) for _ in range(8)]
        for left in range(0, wide, 128):
            dual = spread[:, left:left + 128]
            for place in range(8):
                here = slice(top + place * 8, top + (place + 1) * 8)
                group[place] = group[place] + block[here, left:left + 128] * dual
        sums += group
    return jnp.sum(jnp.transpose(jnp.concatenate(sums)), axis=0, keepdims=True)


def by_cols(block, column):
    tall, wide = block.shape
    sums = [jnp.zeros((8, 128), F32) for _ in range(wide // 128)]
    for top in range(0, tall, 8):
        dual = column[top:top + 8, :]
        for place in range(wide // 128):
            sums[place] = sums[place] + block[top:top + 8, place * 128:(place + 1) * 128] * dual
    return jnp.concatenate(sums, 1)


def chunk(index):
    return pl.ds(pl.multiple_of(index * STEP, STEP), STEP)


def sweep_kernel(opening, terms, plan, cols, *refs):
    if opening:
        parts, (_, sums_out, part_out, spread, total) = refs[:terms], refs[terms:]
        sums_out[...] = added(parts)
        row_dual = sums_out[1:2, :] / sums_out[0:1, :]
    else:
        (sums, *parts), (_, part_out, spread, total) = refs[:terms + 1], refs[terms + 1:]
        row_dual = (sums[1:2, :] - added(parts)) / sums[0:1, :]
    spread[...] = jnp.broadcast_to(row_dual, spread.shape)
    total[...] = jnp.zeros_like(total)
    steps = plan.shape[0] // STEP

    def duals(index):
        here = chunk(index)
        product = by_rows(plan.at[here, :], spread)
        return as_column((cols[1:2, here] - product) / cols[0:1, here], 128)

    def step(index, dual):
        product = by_cols(plan.at[chunk(index - 1), :], dual)
        dual = duals(index)
        total[...] += product
        return dual

    last = lax.fori_loop(1, steps, step, duals(0))
    total[...] += by_cols(plan.at[chunk(steps - 1), :], last)
    part_out[...] = jnp.sum(total[...], axis=0, keepdims=True)


def embed_before_kernel(logit_scale, protos, emb_a, emb_b, after, entry_out, protos_t, token):
    del after
    scale = logit_scale * LOG2E
    rows = entry_out.shape[1] // 2
    token[...] = jnp.zeros_like(token)

    def step(index, carry):
        here = chunk(index)
        for half, emb in enumerate((emb_a, emb_b)):
            entry = jnp.exp2(scale * mm(protos[here, :], emb[:, 0:rows]))
            entry_out[here, half * rows:(half + 1) * rows] = logit_scale * entry
        protos_t[:, here] = jnp.transpose(protos[here, 0:protos_t.shape[0]].astype(F32)).astype(BF16)
        return carry

    lax.fori_loop(0, protos.shape[0] // STEP, step, 0)


def embed_kernel(view_scale, shares, terms, ids, plan, cols, sums, protos, protos_t, view_a, view_b, entries, *refs):
    parts, (duals_out, rows_out, keep, give, spread, total, whole) = refs[:terms], refs[terms:]
    width = protos_t.shape[0]
    rows = entries.shape[1]
    rows_out[...] = (sums[1:2, :] - added(parts)) / sums[0:1, :]
    spread[...] = jnp.broadcast_to(rows_out[...], spread.shape)
    half = rows // 2
    split = rows_out.shape[1] // 2
    own_dual = jnp.concatenate((rows_out[:, 0:half], rows_out[:, split:split + half]), 1)
    total[...] = jnp.zeros_like(total)
    steps = plan.shape[0] // STEP

    def duals(index):
        here = chunk(index)
        return (cols[1:2, here] - by_rows(plan.at[here, :], spread)) / cols[0:1, here]

    def gradient(index, dual):
        here = chunk(index)
        block = protos[here, 0:width]
        cot = -view_scale * jnp.concatenate([mm(block, view[:, 0:half]) for view in (view_a, view_b)], 1)
        grad = entries[here, :] * (cot - own_dual - as_column(dual, rows))
        return mm(protos_t[:, here], grad.astype(BF16))

    def step(index, dual):
        share = gradient(index - 1, dual)
        duals_out[:, chunk(index - 1)] = dual
        dual = duals(index)
        total[...] += share
        return dual

    last = lax.fori_loop(1, steps, step, duals(0))
    duals_out[:, chunk(steps - 1)] = last
    total[...] += gradient(steps - 1, last)
    whole[...] = jnp.transpose(total[...])
    tall = keep.shape[1]
    for place in range(shares):
        above, beside = divmod(place, shares // 2)
        to = above * shares + (ids[1] ^ (2 * beside))
        keep[place] = whole[pl.ds(pl.multiple_of(to * tall, tall), tall), :]
        give[place] = whole[pl.ds(pl.multiple_of((to ^ 1) * tall, tall), tall), :]


def proto_before_kernel(logit_scale, view_scale, ids, protos, emb_a, emb_b, view_a, view_b, after, entry_out, second_out, token):
    del after
    own, rows = entry_out.shape
    width = second_out.shape[1]
    scale = logit_scale * LOG2E
    token[...] = jnp.zeros_like(token)
    here = pl.ds(pl.multiple_of((ids[0] >> 1) * own, own), own)
    total = jnp.zeros((own, width), F32)
    for first_col, emb, view in ((0, emb_a, view_a), (rows // 2, emb_b, view_b)):
        for start in range(0, rows // 2, 2 * width):
            cols = slice(start, start + 2 * width)
            exact = jnp.exp2(scale * mm(protos[here, :], emb[:, cols]))
            entry_out[:, first_col + start:first_col + start + 2 * width] = logit_scale * exact
            total = total + mm((-view_scale * exact).astype(BF16), view[:, cols], NT)
    second_out[...] = total


def proto_kernel(view_scale, ids, protos, emb_a, emb_b, view_a, view_b, entries, second, col_dual, row_dual, out):
    own, width = out.shape
    here = pl.ds(pl.multiple_of((ids[0] >> 1) * own, own), own)
    column = as_column(col_dual[:, here], 2 * width)
    total = second[...]
    split = entries.shape[1] // 2
    for first_col, emb, view in ((0, emb_a, view_a), (split, emb_b, view_b)):
        for start in range(0, split, 2 * width):
            cols = slice(start, start + 2 * width)
            both = slice(first_col + start, first_col + start + 2 * width)
            cot = -view_scale * mm(protos[here, 0:width], view[:, cols])
            grad = entries[:, both] * (cot - row_dual[:, both] - column)
            total = total + mm(grad.astype(BF16), emb[0:width, cols], NT)
    out[...] = total


def call(kernel, out_shape, name, scalars=0, scratch=(), aliases=None, limit=16):
    def run(*args):
        whole = pl.BlockSpec(memory_space=pltpu.VMEM)
        small = pl.BlockSpec(memory_space=pltpu.SMEM)
        return pl.pallas_call(
            kernel,
            out_shape=out_shape,
            in_specs=[small] * scalars + [whole] * (len(args) - scalars),
            out_specs=jax.tree.map(lambda _: whole, out_shape),
            scratch_shapes=[pltpu.VMEM(dims, dtype) for dtype, *dims in scratch],
            input_output_aliases=aliases or {},
            compiler_params=pltpu.CompilerParams(vmem_limit_bytes=limit << 20),
            name=name,
        )(*args)

    return run


def swap_both(value, above, beside, cores=(0, 1)):
    shares = lax.axis_size("proto")
    pairs = [
        (row * shares + col, (row ^ above) * shares + (col ^ beside))
        for row in range(lax.axis_size("row"))
        for col in range(shares)
        if col % 2 in cores
    ]
    return lax.ppermute(value, ("row", "proto"), pairs)


def others():
    shares = lax.axis_size("proto")
    return [(above, beside) for above in range(2) for beside in range(0, shares, 2)]


def exchange(part, work=None):
    shape = jax.ShapeDtypeStruct(part.shape, F32)
    near = call(add_kernel, shape, "add", limit=2)(part, swap(part, "proto", 1))
    plain = [pair for pair in others() if pair[0] == 0 and pair != (0, 0)]
    turned = [pair for pair in others() if pair[0] == 1]
    got = [swap_both(near, *pair, cores=(0,)) for pair in plain] + [swap_both(near, *pair, cores=(1,)) for pair in turned]
    made = work(near) if work else ()
    kernel = functools.partial(received_kernel, len(plain), len(turned))
    got = call(kernel, shape, "received", limit=2)(*got, *made[-1:])
    return [near, got, swap(got, "proto", 1)], made[:-1]


def kept_plan(embeddings, second_view, prototypes, row_scale, col_scale):
    rows, width = embeddings.shape
    blocks, shares = lax.axis_size("row"), lax.axis_size("proto")
    all_rows = rows * blocks
    count = prototypes.shape[0] // 2
    own = 2 * count // blocks
    ids = jnp.stack((lax.axis_index("row"), lax.axis_index("proto")))
    scales = (1.0 / (0.05 * width), 1.0 / (0.1 * width))
    log_mass = math.log(64.0 * prototypes.shape[0] * shares)
    shape = lambda *dims, dtype=F32: jax.ShapeDtypeStruct(dims, dtype)
    form = lambda kernel: functools.partial(kernel, *scales)
    there = lambda value: pltpu.with_memory_space_constraint(value, pltpu.HBM)
    row_scale = row_scale.reshape(1, rows)
    col_scale = col_scale.reshape(1, 2 * count)
    half = shape(width + EXT, rows, dtype=BF16)
    send = call(functools.partial(prep_kernel, scales[0]), half, "prepare", scalars=1)(
        ids, there(embeddings), there(second_view), there(row_scale)
    )
    protos, token = call(
        functools.partial(extend_kernel, scales[0], log_mass),
        (shape(count, 2 * width, dtype=BF16), shape(8, 128)),
        "extend",
        scalars=1,
        limit=4,
    )(ids, there(prototypes), there(col_scale))
    pairs = blocks // 2
    stack = call(functools.partial(stack_kernel, pairs), shape(pairs, width + EXT, rows, dtype=BF16), "stack", limit=2)
    direct = [send] + [swap(send, "row", step) for step in range(2, blocks, 2)]
    mine_a = stack(*direct, token)
    theirs_a = swap(mine_a, "proto", 1)
    mine_b = stack(*[swap(value, "row", 1) for value in direct])
    theirs_b = swap(mine_b, "proto", 1)

    kept = pltpu.VMEM((count, all_rows), F32)
    some = all_rows // 2
    turned = (shape(2 * width, some, dtype=BF16), shape(width, some, dtype=BF16))
    work = [(F32, 8, some), (F32, 8, some)]
    plan, cols, sums, emb_a, view_a = call(
        functools.partial(plan_kernel, *scales, False),
        (kept, shape(2, count), shape(2, some)) + turned,
        "plan_ours",
        scalars=1,
        scratch=work,
        limit=12,
    )(ids, protos, mine_a, theirs_a)
    plan, cols, sums, emb_b, view_b = call(
        functools.partial(plan_kernel, *scales, True),
        (kept, shape(2, count), shape(2, all_rows)) + turned,
        "plan_theirs",
        scalars=1,
        scratch=work,
        aliases={4: 0},
        limit=12,
    )(ids, protos, mine_b, theirs_b, plan, cols, sums)

    token = shape(8, 128)
    embed_before = call(
        functools.partial(embed_before_kernel, scales[0]),
        (shape(count, 2 * rows), shape(width, count, dtype=BF16), token),
        "embed_before",
        limit=6,
    )
    proto_before = call(
        form(proto_before_kernel),
        (shape(own, all_rows), shape(own, width), token),
        "proto_before",
        scalars=1,
        limit=6,
    )
    work = [(F32, 8, all_rows), (F32, 8, all_rows)]
    parts, (entries, protos_t) = exchange(sums, lambda near: embed_before(protos, emb_a, emb_b, near))
    plan, sums, part = call(
        functools.partial(sweep_kernel, True, len(parts)),
        (kept, shape(2, all_rows), shape(1, all_rows)),
        "sweep",
        scratch=work,
        aliases={0: 0},
        limit=4,
    )(plan, cols, *parts)
    parts, (own_entries, second) = exchange(
        part, lambda near: proto_before(ids, protos, emb_a, emb_b, view_a, view_b, near)
    )
    for sweep in range(ITERS - 2):
        plan, part = call(
            functools.partial(sweep_kernel, False, len(parts)),
            (kept, shape(1, all_rows)),
            "sweep",
            scratch=work,
            aliases={0: 0},
            limit=4,
        )(plan, cols, sums, *parts)
        parts, _ = exchange(part)
    pieces = shape(shares, rows // shares, width)
    col_dual, row_dual, keep, give = call(
        functools.partial(embed_kernel, scales[1], shares, len(parts)),
        (shape(1, count), shape(1, all_rows), pieces, pieces),
        "embed_grad",
        scalars=1,
        scratch=work[:1] + [(F32, width, 2 * rows), (F32, 2 * rows, width)],
        limit=6,
    )(ids, plan, cols, sums, protos, protos_t, view_a, view_b, entries, *parts)
    near = call(add_kernel, pieces, "add", limit=2)(keep, swap(give, "proto", 1))
    embed_grad = near[0]
    for place, pair in list(enumerate(others()))[1:]:
        embed_grad = embed_grad + swap_both(near[place], *pair)
    proto_grad = call(functools.partial(proto_kernel, scales[1]), shape(own, width), "proto_grad", scalars=1, limit=6)(
        ids, protos, emb_a, emb_b, view_a, view_b, own_entries, second, col_dual, row_dual
    )
    return embed_grad, proto_grad


def contract_rows(left, right):
    return mm(left, right, (((0,), (0,)), ((), ())))


def contract_width(left, right):
    return mm(left, right, NT)


def sum_over(value, axis):
    size = lax.axis_size(axis)
    parts = [value] + [swap(value, axis, step) for step in range(1, size)]
    return sum(parts[1:], parts[0])


def scatter_sum(value, axis):
    size = lax.axis_size(axis)
    me = lax.axis_index(axis)
    rows = value.shape[0] // size
    block = lambda owner: lax.dynamic_slice_in_dim(value, owner * rows, rows, 0)
    total = block(me)
    for step in range(1, size):
        total = total + swap(block(me ^ step), axis, step)
    return total


def split_plan(embeddings, second_view, prototypes, row_scale, col_scale):
    feat_width = embeddings.shape[1]
    proto_count = prototypes.shape[0]
    logit_scale = 1.0 / (0.05 * feat_width)
    view_scale = 1.0 / (0.1 * feat_width)
    plan_mass = 64.0 * proto_count * lax.axis_size("proto")

    logits = contract_width(embeddings, prototypes) * logit_scale
    plan = row_scale[:, None] * col_scale[None, :] * jnp.exp(logits) / plan_mass
    cotangent = -contract_width(second_view, prototypes) * view_scale
    weighted = plan * cotangent

    row_mass, row_weight = sum_over(jnp.stack((plan.sum(1), weighted.sum(1))), "proto")
    row_dual = row_weight / row_mass
    sums = jnp.stack((plan.sum(0), weighted.sum(0), (row_dual[:, None] * plan).sum(0)))
    col_mass, col_weight, product = sum_over(sums, "row")
    col_dual = (col_weight - product) / col_mass
    for sweep in range(ITERS - 1):
        product = sum_over((plan * col_dual[None, :]).sum(1), "proto")
        row_dual = (row_weight - product) / row_mass
        product = sum_over((plan * row_dual[:, None]).sum(0), "row")
        col_dual = (col_weight - product) / col_mass
    logit_grad = plan * (cotangent - row_dual[:, None] - col_dual[None, :])
    scaled_grad = (logit_scale * logit_grad).astype(jnp.bfloat16)
    scaled_plan = (-view_scale * plan).astype(jnp.bfloat16)
    embed_grad = scatter_sum(
        jnp.dot(scaled_grad, prototypes, preferred_element_type=jnp.float32), "proto"
    )
    proto_grad = scatter_sum(
        contract_rows(scaled_grad, embeddings) + contract_rows(scaled_plan, second_view), "row"
    )
    return (embed_grad, proto_grad)


def per_device(embeddings, second_view, prototypes, row_scale, col_scale):
    blocks, shares = lax.axis_size("row"), lax.axis_size("proto")
    rows, width = embeddings.shape
    count = prototypes.shape[0]
    fits = rows * blocks * count * 2 <= PLAN_BYTES
    even = all(n & (n - 1) == 0 and n > 1 for n in (blocks, shares))
    even = even and rows % (16 * shares) == 0 and rows % width == 0
    tiled = rows % 128 == 0 and width % 128 == 0 and count == blocks * CHUNK and blocks % 4 == 0
    form = kept_plan if fits and even and tiled else split_plan
    return form(embeddings, second_view, prototypes, row_scale, col_scale)


def solution(mesh):
    return jax.shard_map(
        per_device,
        mesh=mesh,
        in_specs=(P("row", None), P("row", None), P("proto", None), P("row"), P("proto")),
        out_specs=(P(("row", "proto"), None), P(("proto", "row"), None)),
        check_vma=False,
    )
```

```python
import functools
import math

import jax
import jax.numpy as jnp
from jax import lax
from jax.experimental import pallas as pl
from jax.experimental.pallas import tpu as pltpu
from jax.sharding import PartitionSpec as P

ITERS = 4
CHUNK = 512
STEP = 256
EXT = 16
PLAN_BYTES = 24 << 20
LOG2E = 1.4426950408889634
F32, BF16 = jnp.float32, jnp.bfloat16
NT = (((1,), (1,)), ((), ()))
NN = (((1,), (0,)), ((), ()))


def mm(left, right, dims=NN):
    return lax.dot_general(left, right, dims, preferred_element_type=F32)


def swap(value, axis, step):
    size = lax.axis_size(axis)
    return lax.ppermute(value, axis, [(i, i ^ step) for i in range(size)])


def as_column(row, width):
    tall = jnp.transpose(jnp.broadcast_to(row, (128, row.shape[1])))
    return jnp.concatenate([tall] * (width // 128), 1)


def rows_of(pieces, height=EXT):
    index = lax.broadcasted_iota(jnp.int32, (height, pieces[0].shape[1]), 0)
    total = jnp.zeros(index.shape, F32)
    for place, piece in enumerate(pieces):
        total = jnp.where(index == place, piece, total)
    return total


def pieces_of(row):
    out = []
    for _ in range(3):
        out.append(row.astype(BF16).astype(F32))
        row = row - out[-1]
    return out, [jnp.ones_like(row)] * 3


def prep_kernel(logit_scale, ids, embeddings, second_view, row_scale, send_out):
    rows, width = embeddings.shape

    @pl.when(ids[1] & 1 == 0)
    def _():
        logs, ones = pieces_of(jnp.log(row_scale[...]) / logit_scale)
        send_out[0:width, :] = jnp.transpose(embeddings[...].astype(F32)).astype(BF16)
        send_out[width:width + EXT, :] = rows_of(logs + ones).astype(BF16)

    @pl.when(ids[1] & 1 != 0)
    def _():
        send_out[0:width, :] = jnp.transpose(second_view[...].astype(F32)).astype(BF16)
        send_out[width:width + EXT, :] = jnp.zeros((EXT, rows), BF16)


def extend_kernel(logit_scale, log_mass, ids, protos, col_scale, protos_out, token):
    count = protos_out.shape[0]
    width = protos.shape[1]
    token[...] = jnp.zeros_like(token)

    def step(index, carry):
        here = pl.ds(pl.multiple_of(index * CHUNK, CHUNK), CHUNK)
        there = pl.ds(pl.multiple_of((2 * index + (ids[0] & 1)) * CHUNK, CHUNK), CHUNK)
        block = protos[there, :]
        logs, ones = pieces_of((jnp.log(col_scale[:, there]) - log_mass) / logit_scale)
        protos_out[here, 0:width] = block
        protos_out[here, width:] = jnp.transpose(rows_of(ones + logs, width)).astype(BF16)
        return carry

    lax.fori_loop(0, count // CHUNK, step, 0)


def stack_kernel(count, *refs):
    for place in range(count):
        refs[-1][place] = refs[place][...]


def add_kernel(left, right, out):
    out[...] = left[...] + right[...]


def plan_kernel(logit_scale, view_scale, ids, protos, mine_a, theirs_a, mine_b, theirs_b, plan_out, cols_out, sums_out, emb_ext, view_t, row_mass, row_weight):
    pairs, high, rows = mine_a.shape
    blocks = 2 * pairs
    count = protos.shape[0]
    width = view_t.shape[0]
    scale = logit_scale * LOG2E
    emb_ext[high:, :] = jnp.zeros((emb_ext.shape[0] - high, blocks * rows), BF16)

    def fill(embs, views):
        for block in range(blocks):
            cols = slice(block * rows, (block + 1) * rows)
            emb_ext[0:high, cols] = embs[block % 2][block // 2]
            view_t[:, cols] = views[block % 2][block // 2, 0:width, :]

    for core in range(2):
        for odd in range(2):
            a, b = ((mine_a, theirs_a), (mine_b, theirs_b)) if core == 0 else ((theirs_a, mine_a), (theirs_b, mine_b))
            low, upper = (a, b) if odd == 0 else (b, a)
            is_this = jnp.logical_and(ids[1] & 1 == core, ids[0] & 1 == odd)
            pl.when(is_this)(functools.partial(fill, (low[0], upper[0]), (low[1], upper[1])))
    row_mass[...] = jnp.zeros_like(row_mass)
    row_weight[...] = jnp.zeros_like(row_weight)

    def folded(block):
        tiles = [block[:, left:left + 128] for left in range(0, block.shape[1], 128)]
        across = tiles[0]
        for tile in tiles[1:]:
            across = across + tile
        return across, jnp.sum(block.reshape(block.shape[0] // 8, 8, block.shape[1]), axis=0)

    def step(index, carry):
        here = pl.ds(pl.multiple_of(index * CHUNK, CHUNK), CHUNK)
        mass = weight = jnp.zeros((CHUNK, 128), F32)
        for block in range(blocks):
            cols = slice(block * rows, (block + 1) * rows)
            plan = jnp.exp2(scale * mm(protos[here, :], emb_ext[:, cols]))
            plan_out[here, cols] = plan
            across, down = folded(plan)
            mass = mass + across
            row_mass[:, cols] += down
            across, down = folded(plan * mm(protos[here, 0:width], view_t[:, cols]))
            weight = weight + across
            row_weight[:, cols] += down
        cols_out[0:1, here] = jnp.sum(jnp.transpose(mass), axis=0, keepdims=True)
        cols_out[1:2, here] = -view_scale * jnp.sum(jnp.transpose(weight), axis=0, keepdims=True)
        return carry

    lax.fori_loop(0, count // CHUNK, step, 0)
    sums_out[0:1, :] = jnp.sum(row_mass[...], axis=0, keepdims=True)
    sums_out[1:2, :] = -view_scale * jnp.sum(row_weight[...], axis=0, keepdims=True)


def received_kernel(terms, *refs):
    total = refs[0][...]
    for other in refs[1:terms]:
        total = total + other[...]
    refs[-1][...] = total


def picked(ids, ours, theirs):
    odd = jnp.full(ours.shape, ids[1] & 1, jnp.int32) == 1
    return jnp.where(odd, ours[...], theirs[...])


def by_rows(block, spread):
    tall, wide = block.shape
    sums = []
    for top in range(0, tall, 64):
        group = [jnp.zeros((8, 128), F32) for _ in range(8)]
        for left in range(0, wide, 128):
            dual = spread[:, left:left + 128]
            for place in range(8):
                here = slice(top + place * 8, top + (place + 1) * 8)
                group[place] = group[place] + block[here, left:left + 128] * dual
        sums += group
    return jnp.sum(jnp.transpose(jnp.concatenate(sums)), axis=0, keepdims=True)


def by_cols(block, column):
    tall, wide = block.shape
    sums = [jnp.zeros((8, 128), F32) for _ in range(wide // 128)]
    for top in range(0, tall, 8):
        dual = column[top:top + 8, :]
        for place in range(wide // 128):
            sums[place] = sums[place] + block[top:top + 8, place * 128:(place + 1) * 128] * dual
    return jnp.concatenate(sums, 1)


def chunk(index):
    return pl.ds(pl.multiple_of(index * STEP, STEP), STEP)


def sweep_kernel(opening, ids, plan, cols, *refs):
    if opening:
        ours, theirs, _, sums_out, part_out, spread, total = refs
        sums_out[...] = picked(ids, ours, theirs)
        row_dual = sums_out[1:2, :] / sums_out[0:1, :]
    else:
        sums, ours, theirs, _, part_out, spread, total = refs
        row_dual = (sums[1:2, :] - picked(ids, ours, theirs)) / sums[0:1, :]
    spread[...] = jnp.broadcast_to(row_dual, spread.shape)
    total[...] = jnp.zeros_like(total)
    steps = plan.shape[0] // STEP

    def duals(index):
        here = chunk(index)
        product = by_rows(plan.at[here, :], spread)
        return as_column((cols[1:2, here] - product) / cols[0:1, here], 128)

    def step(index, dual):
        product = by_cols(plan.at[chunk(index - 1), :], dual)
        dual = duals(index)
        total[...] += product
        return dual

    last = lax.fori_loop(1, steps, step, duals(0))
    total[...] += by_cols(plan.at[chunk(steps - 1), :], last)
    part_out[...] = jnp.sum(total[...], axis=0, keepdims=True)


def embed_before_kernel(logit_scale, protos, emb_ext, after, entry_out, protos_t, token):
    del after
    scale = logit_scale * LOG2E
    token[...] = jnp.zeros_like(token)

    def step(index, carry):
        here = chunk(index)
        entry_out[here, :] = logit_scale * jnp.exp2(scale * mm(protos[here, :], emb_ext[:, 0:entry_out.shape[1]]))
        protos_t[:, here] = jnp.transpose(protos[here, 0:protos_t.shape[0]].astype(F32)).astype(BF16)
        return carry

    lax.fori_loop(0, protos.shape[0] // STEP, step, 0)


def embed_kernel(view_scale, ids, plan, cols, sums, protos, protos_t, view_t, entries, ours, theirs, duals_out, rows_out, keep, give, spread, total, whole):
    shares = keep.shape[0]
    width = protos_t.shape[0]
    rows = entries.shape[1]
    rows_out[...] = (sums[1:2, :] - picked(ids, ours, theirs)) / sums[0:1, :]
    spread[...] = jnp.broadcast_to(rows_out[...], spread.shape)
    own_dual = rows_out[:, 0:rows]
    total[...] = jnp.zeros_like(total)
    steps = plan.shape[0] // STEP

    def duals(index):
        here = chunk(index)
        return (cols[1:2, here] - by_rows(plan.at[here, :], spread)) / cols[0:1, here]

    def gradient(index, dual):
        here = chunk(index)
        cot = -view_scale * mm(protos[here, 0:width], view_t[:, 0:rows])
        grad = entries[here, :] * (cot - own_dual - as_column(dual, rows))
        return mm(protos_t[:, here], grad.astype(BF16))

    def step(index, dual):
        share = gradient(index - 1, dual)
        duals_out[:, chunk(index - 1)] = dual
        dual = duals(index)
        total[...] += share
        return dual

    last = lax.fori_loop(1, steps, step, duals(0))
    duals_out[:, chunk(steps - 1)] = last
    total[...] += gradient(steps - 1, last)
    whole[...] = jnp.transpose(total[...])
    tall = keep.shape[1]
    for place in range(shares):
        above, beside = divmod(place, shares // 2)
        to = ((ids[0] & 1) ^ above) * shares + (ids[1] ^ (2 * beside))
        keep[place] = whole[pl.ds(pl.multiple_of(to * tall, tall), tall), :]
        give[place] = whole[pl.ds(pl.multiple_of((to ^ 1) * tall, tall), tall), :]


def proto_before_kernel(logit_scale, view_scale, ids, protos, emb_ext, view_t, after, entry_out, second_out, token):
    del after
    own, rows = entry_out.shape
    width = second_out.shape[1]
    scale = logit_scale * LOG2E
    token[...] = jnp.zeros_like(token)
    here = pl.ds(pl.multiple_of((ids[0] >> 1) * own, own), own)
    total = jnp.zeros((own, width), F32)
    for start in range(0, rows, 2 * width):
        cols = slice(start, start + 2 * width)
        exact = jnp.exp2(scale * mm(protos[here, :], emb_ext[:, cols]))
        entry_out[:, cols] = logit_scale * exact
        total = total + mm((-view_scale * exact).astype(BF16), view_t[:, cols], NT)
    second_out[...] = total


def proto_kernel(view_scale, ids, protos, emb_ext, view_t, entries, second, col_dual, row_dual, out):
    own, width = out.shape
    here = pl.ds(pl.multiple_of((ids[0] >> 1) * own, own), own)
    column = as_column(col_dual[:, here], 2 * width)
    total = second[...]
    for start in range(0, entries.shape[1], 2 * width):
        cols = slice(start, start + 2 * width)
        cot = -view_scale * mm(protos[here, 0:width], view_t[:, cols])
        grad = entries[:, cols] * (cot - row_dual[:, cols] - column)
        total = total + mm(grad.astype(BF16), emb_ext[0:width, cols], NT)
    out[...] = total


def call(kernel, out_shape, name, scalars=0, scratch=(), aliases=None, limit=16):
    def run(*args):
        whole = pl.BlockSpec(memory_space=pltpu.VMEM)
        small = pl.BlockSpec(memory_space=pltpu.SMEM)
        return pl.pallas_call(
            kernel,
            out_shape=out_shape,
            in_specs=[small] * scalars + [whole] * (len(args) - scalars),
            out_specs=jax.tree.map(lambda _: whole, out_shape),
            scratch_shapes=[pltpu.VMEM(dims, dtype) for dtype, *dims in scratch],
            input_output_aliases=aliases or {},
            compiler_params=pltpu.CompilerParams(vmem_limit_bytes=limit << 20),
            name=name,
        )(*args)

    return run


def swap_both(value, above, beside, cores=(0, 1)):
    shares = lax.axis_size("proto")
    pairs = []
    for row in range(lax.axis_size("row")):
        for col in range(shares):
            partner = (row ^ above, col ^ beside) if col % 2 in cores else (row, col)
            pairs.append((row * shares + col, partner[0] * shares + partner[1]))
    return lax.ppermute(value, ("row", "proto"), pairs)


def others():
    shares = lax.axis_size("proto")
    return [(above, beside) for above in range(2) for beside in range(0, shares, 2)]


def exchange(part, work=None):
    shape = jax.ShapeDtypeStruct(part.shape, F32)
    near = call(add_kernel, shape, "add", limit=2)(part, swap(part, "proto", 1))
    got = [swap_both(near, *pair, cores=(1,)) for pair in others() if pair != (0, 0)]
    made = work(near) if work else ()
    kernel = functools.partial(received_kernel, len(got) + 1)
    total = call(kernel, shape, "received", limit=2)(near, *got, *made[-1:])
    return [total, swap(total, "proto", 1)], made[:-1]


def kept_plan(embeddings, second_view, prototypes, row_scale, col_scale):
    rows, width = embeddings.shape
    blocks, shares = lax.axis_size("row"), lax.axis_size("proto")
    all_rows = rows * blocks
    count = prototypes.shape[0] // 2
    own = 2 * count // blocks
    ids = jnp.stack((lax.axis_index("row"), lax.axis_index("proto")))
    scales = (1.0 / (0.05 * width), 1.0 / (0.1 * width))
    log_mass = math.log(64.0 * prototypes.shape[0] * shares)
    shape = lambda *dims, dtype=F32: jax.ShapeDtypeStruct(dims, dtype)
    form = lambda kernel: functools.partial(kernel, *scales)
    there = lambda value: pltpu.with_memory_space_constraint(value, pltpu.HBM)
    row_scale = row_scale.reshape(1, rows)
    col_scale = col_scale.reshape(1, 2 * count)
    half = shape(width + EXT, rows, dtype=BF16)
    send = call(functools.partial(prep_kernel, scales[0]), half, "prepare", scalars=1)(
        ids, there(embeddings), there(second_view), there(row_scale)
    )
    protos, token = call(
        functools.partial(extend_kernel, scales[0], log_mass),
        (shape(count, 2 * width, dtype=BF16), shape(8, 128)),
        "extend",
        scalars=1,
        limit=4,
    )(ids, there(prototypes), there(col_scale))
    pairs = blocks // 2
    stack = call(functools.partial(stack_kernel, pairs), shape(pairs, width + EXT, rows, dtype=BF16), "stack", limit=2)
    direct = [send] + [swap(send, "row", step) for step in range(2, blocks, 2)]
    mine_a = stack(*direct)
    theirs_a = swap(mine_a, "proto", 1)
    mine_b = stack(*[swap(value, "row", 1) for value in direct], token)
    theirs_b = swap(mine_b, "proto", 1)

    kept = pltpu.VMEM((count, all_rows), F32)
    plan, cols, sums, emb_ext, view_t = call(
        form(plan_kernel),
        (kept, shape(2, count), shape(2, all_rows), shape(2 * width, all_rows, dtype=BF16), shape(width, all_rows, dtype=BF16)),
        "plan",
        scalars=1,
        scratch=[(F32, 8, all_rows), (F32, 8, all_rows)],
        limit=12,
    )(ids, protos, mine_a, theirs_a, mine_b, theirs_b)

    work = [(F32, 8, all_rows), (F32, 8, all_rows)]
    token = shape(8, 128)
    embed_before = call(
        functools.partial(embed_before_kernel, scales[0]),
        (shape(count, 2 * rows), shape(width, count, dtype=BF16), token),
        "embed_before",
        limit=6,
    )
    proto_before = call(
        form(proto_before_kernel),
        (shape(own, all_rows), shape(own, width), token),
        "proto_before",
        scalars=1,
        limit=6,
    )
    parts, (entries, protos_t) = exchange(sums, lambda near: embed_before(protos, emb_ext, near))
    plan, sums, part = call(
        functools.partial(sweep_kernel, True),
        (kept, shape(2, all_rows), shape(1, all_rows)),
        "sweep",
        scalars=1,
        scratch=work,
        aliases={1: 0},
        limit=4,
    )(ids, plan, cols, *parts)
    parts, (own_entries, second) = exchange(part, lambda near: proto_before(ids, protos, emb_ext, view_t, near))
    for sweep in range(ITERS - 2):
        plan, part = call(
            functools.partial(sweep_kernel, False),
            (kept, shape(1, all_rows)),
            "sweep",
            scalars=1,
            scratch=work,
            aliases={1: 0},
            limit=4,
        )(ids, plan, cols, sums, *parts)
        parts, _ = exchange(part)
    pieces = shape(shares, rows // shares, width)
    col_dual, row_dual, keep, give = call(
        functools.partial(embed_kernel, scales[1]),
        (shape(1, count), shape(1, all_rows), pieces, pieces),
        "embed_grad",
        scalars=1,
        scratch=work[:1] + [(F32, width, 2 * rows), (F32, 2 * rows, width)],
        limit=6,
    )(ids, plan, cols, sums, protos, protos_t, view_t, entries, *parts)
    near = call(add_kernel, pieces, "add", limit=2)(keep, swap(give, "proto", 1))
    embed_grad = near[0]
    for place, pair in list(enumerate(others()))[1:]:
        embed_grad = embed_grad + swap_both(near[place], *pair)
    proto_grad = call(functools.partial(proto_kernel, scales[1]), shape(own, width), "proto_grad", scalars=1, limit=6)(
        ids, protos, emb_ext, view_t, own_entries, second, col_dual, row_dual
    )
    return embed_grad, proto_grad


def contract_rows(left, right):
    return mm(left, right, (((0,), (0,)), ((), ())))


def contract_width(left, right):
    return mm(left, right, NT)


def sum_over(value, axis):
    size = lax.axis_size(axis)
    parts = [value] + [swap(value, axis, step) for step in range(1, size)]
    return sum(parts[1:], parts[0])


def scatter_sum(value, axis):
    size = lax.axis_size(axis)
    me = lax.axis_index(axis)
    rows = value.shape[0] // size
    block = lambda owner: lax.dynamic_slice_in_dim(value, owner * rows, rows, 0)
    total = block(me)
    for step in range(1, size):
        total = total + swap(block(me ^ step), axis, step)
    return total


def split_plan(embeddings, second_view, prototypes, row_scale, col_scale):
    feat_width = embeddings.shape[1]
    proto_count = prototypes.shape[0]
    logit_scale = 1.0 / (0.05 * feat_width)
    view_scale = 1.0 / (0.1 * feat_width)
    plan_mass = 64.0 * proto_count * lax.axis_size("proto")

    logits = contract_width(embeddings, prototypes) * logit_scale
    plan = row_scale[:, None] * col_scale[None, :] * jnp.exp(logits) / plan_mass
    cotangent = -contract_width(second_view, prototypes) * view_scale
    weighted = plan * cotangent

    row_mass, row_weight = sum_over(jnp.stack((plan.sum(1), weighted.sum(1))), "proto")
    row_dual = row_weight / row_mass
    sums = jnp.stack((plan.sum(0), weighted.sum(0), (row_dual[:, None] * plan).sum(0)))
    col_mass, col_weight, product = sum_over(sums, "row")
    col_dual = (col_weight - product) / col_mass
    for sweep in range(ITERS - 1):
        product = sum_over((plan * col_dual[None, :]).sum(1), "proto")
        row_dual = (row_weight - product) / row_mass
        product = sum_over((plan * row_dual[:, None]).sum(0), "row")
        col_dual = (col_weight - product) / col_mass
    logit_grad = plan * (cotangent - row_dual[:, None] - col_dual[None, :])
    scaled_grad = (logit_scale * logit_grad).astype(jnp.bfloat16)
    scaled_plan = (-view_scale * plan).astype(jnp.bfloat16)
    embed_grad = scatter_sum(
        jnp.dot(scaled_grad, prototypes, preferred_element_type=jnp.float32), "proto"
    )
    proto_grad = scatter_sum(
        contract_rows(scaled_grad, embeddings) + contract_rows(scaled_plan, second_view), "row"
    )
    return (embed_grad, proto_grad)


def per_device(embeddings, second_view, prototypes, row_scale, col_scale):
    blocks, shares = lax.axis_size("row"), lax.axis_size("proto")
    rows, width = embeddings.shape
    count = prototypes.shape[0]
    fits = rows * blocks * count * 2 <= PLAN_BYTES
    even = all(n & (n - 1) == 0 and n > 1 for n in (blocks, shares))
    even = even and rows % (16 * shares) == 0 and rows % width == 0
    tiled = rows % 128 == 0 and width % 128 == 0 and count == blocks * CHUNK and blocks % 4 == 0
    form = kept_plan if fits and even and tiled else split_plan
    return form(embeddings, second_view, prototypes, row_scale, col_scale)


def solution(mesh):
    return jax.shard_map(
        per_device,
        mesh=mesh,
        in_specs=(P("row", None), P("row", None), P("proto", None), P("row"), P("proto")),
        out_specs=(P(("row", "proto"), None), P(("proto", "row"), None)),
        check_vma=False,
    )
```

```python
import functools
import math

import jax
import jax.numpy as jnp
from jax import lax
from jax.experimental import pallas as pl
from jax.experimental.pallas import tpu as pltpu
from jax.sharding import PartitionSpec as P

ITERS = 4
CHUNK = 512
STEP = 256
EXT = 16
PLAN_BYTES = 24 << 20
LOG2E = 1.4426950408889634
F32, BF16 = jnp.float32, jnp.bfloat16
NT = (((1,), (1,)), ((), ()))
NN = (((1,), (0,)), ((), ()))


def mm(left, right, dims=NN):
    return lax.dot_general(left, right, dims, preferred_element_type=F32)


def swap(value, axis, step):
    size = lax.axis_size(axis)
    return lax.ppermute(value, axis, [(i, i ^ step) for i in range(size)])


def lane_sums(block):
    return jnp.broadcast_to(jnp.sum(block, axis=1, keepdims=True), (block.shape[0], 128))


def widened(column, width):
    return jnp.concatenate([column] * (width // 128), 1)


def rows_of(pieces, height=EXT):
    index = lax.broadcasted_iota(jnp.int32, (height, pieces[0].shape[1]), 0)
    total = jnp.zeros(index.shape, F32)
    for place, piece in enumerate(pieces):
        total = jnp.where(index == place, piece, total)
    return total


def pieces_of(row):
    out = []
    for _ in range(3):
        out.append(row.astype(BF16).astype(F32))
        row = row - out[-1]
    return out, [jnp.ones_like(row)] * 3


def prep_kernel(logit_scale, ids, embeddings, second_view, row_scale, send_out):
    rows, width = embeddings.shape

    @pl.when(ids[1] & 1 == 0)
    def _():
        logs, ones = pieces_of(jnp.log(row_scale[...]) / logit_scale)
        send_out[0:width, :] = jnp.transpose(embeddings[...].astype(F32)).astype(BF16)
        send_out[width:width + EXT, :] = rows_of(logs + ones).astype(BF16)

    @pl.when(ids[1] & 1 != 0)
    def _():
        send_out[0:width, :] = jnp.transpose(second_view[...].astype(F32)).astype(BF16)
        send_out[width:width + EXT, :] = jnp.zeros((EXT, rows), BF16)


def turn_kernel(logit_scale, log_mass, ids, protos, col_scale, protos_out, protos_t, token):
    count = protos_out.shape[0]
    width = protos.shape[1]
    token[...] = jnp.zeros_like(token)

    def step(index, carry):
        here = pl.ds(pl.multiple_of(index * CHUNK, CHUNK), CHUNK)
        there = pl.ds(pl.multiple_of((2 * index + (ids[0] & 1)) * CHUNK, CHUNK), CHUNK)
        block = protos[there, :]
        logs, ones = pieces_of((jnp.log(col_scale[:, there]) - log_mass) / logit_scale)
        protos_out[here, 0:width] = block
        protos_out[here, width:] = jnp.transpose(rows_of(ones + logs, width)).astype(BF16)
        protos_t[:, here] = jnp.transpose(block.astype(F32)).astype(BF16)
        return carry

    lax.fori_loop(0, count // CHUNK, step, 0)


def stack_kernel(count, *refs):
    for place in range(count):
        refs[-1][place] = refs[place][...]


def add_kernel(left, right, out):
    out[...] = left[...] + right[...]


def plan_kernel(logit_scale, view_scale, ids, protos, mine_a, theirs_a, mine_b, theirs_b, plan_out, cols_out, sums_out, emb_ext, view_t, row_mass, row_weight):
    pairs, high, rows = mine_a.shape
    blocks = 2 * pairs
    count = protos.shape[0]
    width = view_t.shape[0]
    scale = logit_scale * LOG2E
    emb_ext[high:, :] = jnp.zeros((emb_ext.shape[0] - high, blocks * rows), BF16)

    def fill(embs, views):
        for block in range(blocks):
            cols = slice(block * rows, (block + 1) * rows)
            emb_ext[0:high, cols] = embs[block % 2][block // 2]
            view_t[:, cols] = views[block % 2][block // 2, 0:width, :]

    for core in range(2):
        for odd in range(2):
            a, b = ((mine_a, theirs_a), (mine_b, theirs_b)) if core == 0 else ((theirs_a, mine_a), (theirs_b, mine_b))
            low, upper = (a, b) if odd == 0 else (b, a)
            is_this = jnp.logical_and(ids[1] & 1 == core, ids[0] & 1 == odd)
            pl.when(is_this)(functools.partial(fill, (low[0], upper[0]), (low[1], upper[1])))
    row_mass[...] = jnp.zeros_like(row_mass)
    row_weight[...] = jnp.zeros_like(row_weight)

    def folded(block):
        tiles = [block[:, left:left + 128] for left in range(0, block.shape[1], 128)]
        across = tiles[0]
        for tile in tiles[1:]:
            across = across + tile
        return across, jnp.sum(block.reshape(block.shape[0] // 8, 8, block.shape[1]), axis=0)

    def step(index, carry):
        here = pl.ds(pl.multiple_of(index * CHUNK, CHUNK), CHUNK)
        mass = weight = jnp.zeros((CHUNK, 128), F32)
        for block in range(blocks):
            cols = slice(block * rows, (block + 1) * rows)
            plan = jnp.exp2(scale * mm(protos[here, :], emb_ext[:, cols]))
            plan_out[here, cols] = plan
            across, down = folded(plan)
            mass = mass + across
            row_mass[:, cols] += down
            across, down = folded(plan * mm(protos[here, 0:width], view_t[:, cols]))
            weight = weight + across
            row_weight[:, cols] += down
        inverse = 1.0 / lane_sums(mass)
        cols_out[0, here, :] = inverse
        cols_out[1, here, :] = -view_scale * lane_sums(weight) * inverse
        return carry

    lax.fori_loop(0, count // CHUNK, step, 0)
    sums_out[0:1, :] = jnp.sum(row_mass[...], axis=0, keepdims=True)
    sums_out[1:2, :] = -view_scale * jnp.sum(row_weight[...], axis=0, keepdims=True)


def added(parts):
    total = parts[0][...]
    for other in parts[1:]:
        total = total + other[...]
    return total


def by_rows(block, cols, here, spread):
    tall, wide = block.shape
    duals = []
    for top in range(0, tall, 64):
        group = [jnp.zeros((8, 128), F32) for _ in range(8)]
        for left in range(0, wide, 128):
            dual = spread[:, left:left + 128]
            for place in range(8):
                rows = slice(top + place * 8, top + (place + 1) * 8)
                group[place] = group[place] + block[rows, left:left + 128] * dual
        duals.append(lane_sums(jnp.concatenate(group)))
    return cols[1, here, :] - cols[0, here, :] * jnp.concatenate(duals)


def by_cols(block, column):
    tall, wide = block.shape
    sums = [jnp.zeros((8, 128), F32) for _ in range(wide // 128)]
    for top in range(0, tall, 8):
        dual = column[top:top + 8, :]
        for place in range(wide // 128):
            sums[place] = sums[place] + block[top:top + 8, place * 128:(place + 1) * 128] * dual
    return jnp.concatenate(sums, 1)


def chunk(index):
    return pl.ds(pl.multiple_of(index * STEP, STEP), STEP)


def sweep_kernel(opening, shares, plan, cols, *refs):
    if opening:
        parts, (_, _, sums_out, part_out, spread, total) = refs[:shares], refs[shares:]
        sums_out[...] = added(parts)
        row_dual = sums_out[1:2, :] / sums_out[0:1, :]
    else:
        (sums, *parts), (_, _, part_out, spread, total) = refs[:shares + 1], refs[shares + 1:]
        row_dual = (sums[1:2, :] - added(parts)) / sums[0:1, :]
    spread[...] = jnp.broadcast_to(row_dual, spread.shape)
    total[...] = jnp.zeros_like(total)
    steps = plan.shape[0] // STEP

    def duals(index):
        here = chunk(index)
        return by_rows(plan.at[here, :], cols, here, spread)

    def step(index, dual):
        product = by_cols(plan.at[chunk(index - 1), :], dual)
        dual = duals(index)
        total[...] += product
        return dual

    last = lax.fori_loop(1, steps, step, duals(0))
    total[...] += by_cols(plan.at[chunk(steps - 1), :], last)
    part_out[...] = jnp.sum(total[...], axis=0, keepdims=True)


def embed_before_kernel(logit_scale, protos, emb_ext, after, entry_out, token):
    del after
    scale = logit_scale * LOG2E
    token[...] = jnp.zeros_like(token)

    def step(index, carry):
        here = chunk(index)
        entry_out[here, :] = logit_scale * jnp.exp2(scale * mm(protos[here, :], emb_ext[:, 0:entry_out.shape[1]]))
        return carry

    lax.fori_loop(0, protos.shape[0] // STEP, step, 0)


def embed_kernel(view_scale, shares, ids, plan, cols, sums, protos, protos_t, view_t, entries, *refs):
    parts, (duals_out, rows_out, keep, give, spread, total, whole) = refs[:shares], refs[shares:]
    width = protos_t.shape[0]
    rows = entries.shape[1]
    rows_out[...] = (sums[1:2, :] - added(parts)) / sums[0:1, :]
    spread[...] = jnp.broadcast_to(rows_out[...], spread.shape)
    own_dual = rows_out[:, 0:rows]
    total[...] = jnp.zeros_like(total)
    steps = plan.shape[0] // STEP

    def duals(index):
        here = chunk(index)
        return by_rows(plan.at[here, :], cols, here, spread)

    def gradient(index, dual):
        here = chunk(index)
        cot = -view_scale * mm(protos[here, 0:width], view_t[:, 0:rows])
        grad = entries[here, :] * (cot - own_dual - widened(dual, rows))
        return mm(protos_t[:, here], grad.astype(BF16))

    def step(index, dual):
        share = gradient(index - 1, dual)
        duals_out[chunk(index - 1), :] = dual
        dual = duals(index)
        total[...] += share
        return dual

    last = lax.fori_loop(1, steps, step, duals(0))
    duals_out[chunk(steps - 1), :] = last
    total[...] += gradient(steps - 1, last)
    whole[...] = jnp.transpose(total[...])
    tall = keep.shape[1]
    for place in range(shares):
        above, beside = divmod(place, shares // 2)
        to = ((ids[0] & 1) ^ above) * shares + (ids[1] ^ (2 * beside))
        keep[place] = whole[pl.ds(pl.multiple_of(to * tall, tall), tall), :]
        give[place] = whole[pl.ds(pl.multiple_of((to ^ 1) * tall, tall), tall), :]


def proto_before_kernel(logit_scale, view_scale, ids, protos, emb_ext, view_t, after, entry_out, second_out, token):
    del after
    own, rows = entry_out.shape
    width = second_out.shape[1]
    scale = logit_scale * LOG2E
    token[...] = jnp.zeros_like(token)
    here = pl.ds(pl.multiple_of((ids[0] >> 1) * own, own), own)
    total = jnp.zeros((own, width), F32)
    for start in range(0, rows, 2 * width):
        cols = slice(start, start + 2 * width)
        exact = jnp.exp2(scale * mm(protos[here, :], emb_ext[:, cols]))
        entry_out[:, cols] = logit_scale * exact
        total = total + mm((-view_scale * exact).astype(BF16), view_t[:, cols], NT)
    second_out[...] = total


def proto_kernel(view_scale, ids, protos, emb_ext, view_t, entries, second, col_dual, row_dual, out):
    own, width = out.shape
    here = pl.ds(pl.multiple_of((ids[0] >> 1) * own, own), own)
    column = widened(col_dual[here, :], 2 * width)
    total = second[...]
    for start in range(0, entries.shape[1], 2 * width):
        cols = slice(start, start + 2 * width)
        cot = -view_scale * mm(protos[here, 0:width], view_t[:, cols])
        grad = entries[:, cols] * (cot - row_dual[:, cols] - column)
        total = total + mm(grad.astype(BF16), emb_ext[0:width, cols], NT)
    out[...] = total


def call(kernel, out_shape, name, scalars=0, scratch=(), aliases=None, limit=16):
    def run(*args):
        whole = pl.BlockSpec(memory_space=pltpu.VMEM)
        small = pl.BlockSpec(memory_space=pltpu.SMEM)
        return pl.pallas_call(
            kernel,
            out_shape=out_shape,
            in_specs=[small] * scalars + [whole] * (len(args) - scalars),
            out_specs=jax.tree.map(lambda _: whole, out_shape),
            scratch_shapes=[pltpu.VMEM(dims, dtype) for dtype, *dims in scratch],
            input_output_aliases=aliases or {},
            compiler_params=pltpu.CompilerParams(vmem_limit_bytes=limit << 20),
            name=name,
        )(*args)

    return run


def swap_both(value, above, beside):
    shares = lax.axis_size("proto")
    pairs = [
        (row * shares + col, (row ^ above) * shares + (col ^ beside))
        for row in range(lax.axis_size("row"))
        for col in range(shares)
    ]
    return lax.ppermute(value, ("row", "proto"), pairs)


def others():
    shares = lax.axis_size("proto")
    return [(above, beside) for above in range(2) for beside in range(0, shares, 2)]


def exchange(part):
    near = call(add_kernel, jax.ShapeDtypeStruct(part.shape, F32), "add", limit=2)(part, swap(part, "proto", 1))
    return [near if pair == (0, 0) else swap_both(near, *pair) for pair in others()]


def kept_plan(embeddings, second_view, prototypes, row_scale, col_scale):
    rows, width = embeddings.shape
    blocks, shares = lax.axis_size("row"), lax.axis_size("proto")
    all_rows = rows * blocks
    count = prototypes.shape[0] // 2
    own = 2 * count // blocks
    ids = jnp.stack((lax.axis_index("row"), lax.axis_index("proto")))
    scales = (1.0 / (0.05 * width), 1.0 / (0.1 * width))
    log_mass = math.log(64.0 * prototypes.shape[0] * shares)
    shape = lambda *dims, dtype=F32: jax.ShapeDtypeStruct(dims, dtype)
    form = lambda kernel: functools.partial(kernel, *scales)
    there = lambda value: pltpu.with_memory_space_constraint(value, pltpu.HBM)
    row_scale = row_scale.reshape(1, rows)
    col_scale = col_scale.reshape(1, 2 * count)
    half = shape(width + EXT, rows, dtype=BF16)
    send = call(functools.partial(prep_kernel, scales[0]), half, "prepare", scalars=1)(
        ids, there(embeddings), there(second_view), there(row_scale)
    )
    protos, protos_t, token = call(
        functools.partial(turn_kernel, scales[0], log_mass),
        (shape(count, 2 * width, dtype=BF16), shape(width, count, dtype=BF16), shape(8, 128)),
        "turn",
        scalars=1,
        limit=4,
    )(ids, there(prototypes), there(col_scale))
    pairs = blocks // 2
    stack = call(functools.partial(stack_kernel, pairs), shape(pairs, width + EXT, rows, dtype=BF16), "stack", limit=2)
    direct = [send] + [swap(send, "row", step) for step in range(2, blocks, 2)]
    mine_a = stack(*direct)
    theirs_a = swap(mine_a, "proto", 1)
    mine_b = stack(*[swap(value, "row", 1) for value in direct], token)
    theirs_b = swap(mine_b, "proto", 1)

    kept = pltpu.VMEM((count, all_rows), F32)
    plan, cols, sums, emb_ext, view_t = call(
        form(plan_kernel),
        (kept, shape(2, count, 128), shape(2, all_rows), shape(2 * width, all_rows, dtype=BF16), shape(width, all_rows, dtype=BF16)),
        "plan",
        scalars=1,
        scratch=[(F32, 8, all_rows), (F32, 8, all_rows)],
        limit=12,
    )(ids, protos, mine_a, theirs_a, mine_b, theirs_b)

    work = [(F32, 8, all_rows), (F32, 8, all_rows)]
    token = shape(8, 128)
    parts = exchange(sums)
    entries, done = call(
        functools.partial(embed_before_kernel, scales[0]),
        (shape(count, 2 * rows), token),
        "embed_before",
        limit=6,
    )(protos, emb_ext, parts[0])
    plan, sums, part = call(
        functools.partial(sweep_kernel, True, shares),
        (kept, shape(2, all_rows), shape(1, all_rows)),
        "sweep",
        scratch=work,
        aliases={0: 0},
        limit=4,
    )(plan, cols, *parts, done)
    for sweep in range(ITERS - 2):
        parts = exchange(part)
        if sweep == 0:
            own_entries, second, done = call(
                form(proto_before_kernel),
                (shape(own, all_rows), shape(own, width), token),
                "proto_before",
                scalars=1,
                limit=6,
            )(ids, protos, emb_ext, view_t, parts[0])
        plan, part = call(
            functools.partial(sweep_kernel, False, shares),
            (kept, shape(1, all_rows)),
            "sweep",
            scratch=work,
            aliases={0: 0},
            limit=4,
        )(plan, cols, sums, *parts, done)
    pieces = shape(shares, rows // shares, width)
    col_dual, row_dual, keep, give = call(
        functools.partial(embed_kernel, scales[1], shares),
        (shape(count, 128), shape(1, all_rows), pieces, pieces),
        "embed_grad",
        scalars=1,
        scratch=work[:1] + [(F32, width, 2 * rows), (F32, 2 * rows, width)],
        limit=6,
    )(ids, plan, cols, sums, protos, protos_t, view_t, entries, *exchange(part))
    near = call(add_kernel, pieces, "add", limit=2)(keep, swap(give, "proto", 1))
    embed_grad = near[0]
    for place, pair in list(enumerate(others()))[1:]:
        embed_grad = embed_grad + swap_both(near[place], *pair)
    proto_grad = call(functools.partial(proto_kernel, scales[1]), shape(own, width), "proto_grad", scalars=1, limit=6)(
        ids, protos, emb_ext, view_t, own_entries, second, col_dual, row_dual
    )
    return embed_grad, proto_grad


def contract_rows(left, right):
    return mm(left, right, (((0,), (0,)), ((), ())))


def contract_width(left, right):
    return mm(left, right, NT)


def sum_over(value, axis):
    size = lax.axis_size(axis)
    parts = [value] + [swap(value, axis, step) for step in range(1, size)]
    return sum(parts[1:], parts[0])


def scatter_sum(value, axis):
    size = lax.axis_size(axis)
    me = lax.axis_index(axis)
    rows = value.shape[0] // size
    block = lambda owner: lax.dynamic_slice_in_dim(value, owner * rows, rows, 0)
    total = block(me)
    for step in range(1, size):
        total = total + swap(block(me ^ step), axis, step)
    return total


def split_plan(embeddings, second_view, prototypes, row_scale, col_scale):
    feat_width = embeddings.shape[1]
    proto_count = prototypes.shape[0]
    logit_scale = 1.0 / (0.05 * feat_width)
    view_scale = 1.0 / (0.1 * feat_width)
    plan_mass = 64.0 * proto_count * lax.axis_size("proto")

    logits = contract_width(embeddings, prototypes) * logit_scale
    plan = row_scale[:, None] * col_scale[None, :] * jnp.exp(logits) / plan_mass
    cotangent = -contract_width(second_view, prototypes) * view_scale
    weighted = plan * cotangent

    row_mass, row_weight = sum_over(jnp.stack((plan.sum(1), weighted.sum(1))), "proto")
    row_dual = row_weight / row_mass
    sums = jnp.stack((plan.sum(0), weighted.sum(0), (row_dual[:, None] * plan).sum(0)))
    col_mass, col_weight, product = sum_over(sums, "row")
    col_dual = (col_weight - product) / col_mass
    for sweep in range(ITERS - 1):
        product = sum_over((plan * col_dual[None, :]).sum(1), "proto")
        row_dual = (row_weight - product) / row_mass
        product = sum_over((plan * row_dual[:, None]).sum(0), "row")
        col_dual = (col_weight - product) / col_mass
    logit_grad = plan * (cotangent - row_dual[:, None] - col_dual[None, :])
    scaled_grad = (logit_scale * logit_grad).astype(jnp.bfloat16)
    scaled_plan = (-view_scale * plan).astype(jnp.bfloat16)
    embed_grad = scatter_sum(
        jnp.dot(scaled_grad, prototypes, preferred_element_type=jnp.float32), "proto"
    )
    proto_grad = scatter_sum(
        contract_rows(scaled_grad, embeddings) + contract_rows(scaled_plan, second_view), "row"
    )
    return (embed_grad, proto_grad)


def per_device(embeddings, second_view, prototypes, row_scale, col_scale):
    blocks, shares = lax.axis_size("row"), lax.axis_size("proto")
    rows, width = embeddings.shape
    count = prototypes.shape[0]
    fits = rows * blocks * count * 2 <= PLAN_BYTES
    even = all(n & (n - 1) == 0 and n > 1 for n in (blocks, shares))
    even = even and rows % (16 * shares) == 0 and rows % width == 0
    tiled = rows % 128 == 0 and width % 128 == 0 and count == blocks * CHUNK and blocks % 4 == 0
    form = kept_plan if fits and even and tiled else split_plan
    return form(embeddings, second_view, prototypes, row_scale, col_scale)


def solution(mesh):
    return jax.shard_map(
        per_device,
        mesh=mesh,
        in_specs=(P("row", None), P("row", None), P("proto", None), P("row"), P("proto")),
        out_specs=(P(("row", "proto"), None), P(("proto", "row"), None)),
        check_vma=False,
    )
```

```python
import functools
import math

import jax
import jax.numpy as jnp
from jax import lax
from jax.experimental import pallas as pl
from jax.experimental.pallas import tpu as pltpu
from jax.sharding import PartitionSpec as P

ITERS = 4
CHUNK = 512
STEP = 256
EXT = 16
PLAN_BYTES = 24 << 20
LOG2E = 1.4426950408889634
F32, BF16 = jnp.float32, jnp.bfloat16
NT = (((1,), (1,)), ((), ()))
NN = (((1,), (0,)), ((), ()))


def mm(left, right, dims=NN):
    return lax.dot_general(left, right, dims, preferred_element_type=F32)


def swap(value, axis, step):
    size = lax.axis_size(axis)
    return lax.ppermute(value, axis, [(i, i ^ step) for i in range(size)])


def lane_sums(block):
    return jnp.broadcast_to(jnp.sum(block, axis=1, keepdims=True), (block.shape[0], 128))


def widened(column, width):
    return jnp.concatenate([column] * (width // 128), 1)


def rows_of(pieces, height=EXT):
    index = lax.broadcasted_iota(jnp.int32, (height, pieces[0].shape[1]), 0)
    total = jnp.zeros(index.shape, F32)
    for place, piece in enumerate(pieces):
        total = jnp.where(index == place, piece, total)
    return total


def pieces_of(row):
    out = []
    for _ in range(3):
        out.append(row.astype(BF16).astype(F32))
        row = row - out[-1]
    return out, [jnp.ones_like(row)] * 3


def prep_kernel(logit_scale, ids, embeddings, second_view, row_scale, send_out):
    rows, width = embeddings.shape

    @pl.when(ids[1] & 1 == 0)
    def _():
        logs, ones = pieces_of(jnp.log(row_scale[...]) / logit_scale)
        send_out[0:width, :] = jnp.transpose(embeddings[...].astype(F32)).astype(BF16)
        send_out[width:width + EXT, :] = rows_of(logs + ones).astype(BF16)

    @pl.when(ids[1] & 1 != 0)
    def _():
        send_out[0:width, :] = jnp.transpose(second_view[...].astype(F32)).astype(BF16)
        send_out[width:width + EXT, :] = jnp.zeros((EXT, rows), BF16)


def turn_kernel(logit_scale, log_mass, ids, protos, col_scale, protos_out, protos_t, token):
    count = protos_out.shape[0]
    width = protos.shape[1]
    token[...] = jnp.zeros_like(token)

    def step(index, carry):
        here = pl.ds(pl.multiple_of(index * CHUNK, CHUNK), CHUNK)
        there = pl.ds(pl.multiple_of((2 * index + (ids[0] & 1)) * CHUNK, CHUNK), CHUNK)
        block = protos[there, :]
        logs, ones = pieces_of((jnp.log(col_scale[:, there]) - log_mass) / logit_scale)
        protos_out[here, 0:width] = block
        protos_out[here, width:] = jnp.transpose(rows_of(ones + logs, width)).astype(BF16)
        protos_t[:, here] = jnp.transpose(block.astype(F32)).astype(BF16)
        return carry

    lax.fori_loop(0, count // CHUNK, step, 0)


def stack_kernel(count, *refs):
    for place in range(count):
        refs[-1][place] = refs[place][...]


def add_kernel(left, right, *refs):
    refs[-1][...] = left[...] + right[...]


def plan_kernel(logit_scale, view_scale, ids, protos, mine_a, theirs_a, mine_b, theirs_b, plan_out, cols_out, sums_out, emb_ext, view_t, row_mass, row_weight):
    pairs, high, rows = mine_a.shape
    blocks = 2 * pairs
    count = protos.shape[0]
    width = view_t.shape[0]
    scale = logit_scale * LOG2E
    emb_ext[high:, :] = jnp.zeros((emb_ext.shape[0] - high, blocks * rows), BF16)

    def fill(embs, views):
        for block in range(blocks):
            cols = slice(block * rows, (block + 1) * rows)
            emb_ext[0:high, cols] = embs[block % 2][block // 2]
            view_t[:, cols] = views[block % 2][block // 2, 0:width, :]

    for core in range(2):
        for odd in range(2):
            a, b = ((mine_a, theirs_a), (mine_b, theirs_b)) if core == 0 else ((theirs_a, mine_a), (theirs_b, mine_b))
            low, upper = (a, b) if odd == 0 else (b, a)
            is_this = jnp.logical_and(ids[1] & 1 == core, ids[0] & 1 == odd)
            pl.when(is_this)(functools.partial(fill, (low[0], upper[0]), (low[1], upper[1])))
    row_mass[...] = jnp.zeros_like(row_mass)
    row_weight[...] = jnp.zeros_like(row_weight)

    def folded(block):
        tiles = [block[:, left:left + 128] for left in range(0, block.shape[1], 128)]
        across = tiles[0]
        for tile in tiles[1:]:
            across = across + tile
        return across, jnp.sum(block.reshape(block.shape[0] // 8, 8, block.shape[1]), axis=0)

    def step(index, carry):
        here = pl.ds(pl.multiple_of(index * CHUNK, CHUNK), CHUNK)
        mass = weight = jnp.zeros((CHUNK, 128), F32)
        for block in range(blocks):
            cols = slice(block * rows, (block + 1) * rows)
            plan = jnp.exp2(scale * mm(protos[here, :], emb_ext[:, cols]))
            plan_out[here, cols] = plan
            across, down = folded(plan)
            mass = mass + across
            row_mass[:, cols] += down
            across, down = folded(plan * mm(protos[here, 0:width], view_t[:, cols]))
            weight = weight + across
            row_weight[:, cols] += down
        inverse = 1.0 / lane_sums(mass)
        cols_out[0, here, :] = inverse
        cols_out[1, here, :] = -view_scale * lane_sums(weight) * inverse
        return carry

    lax.fori_loop(0, count // CHUNK, step, 0)
    sums_out[0:1, :] = jnp.sum(row_mass[...], axis=0, keepdims=True)
    sums_out[1:2, :] = -view_scale * jnp.sum(row_weight[...], axis=0, keepdims=True)


def added(parts):
    total = parts[0][...]
    for other in parts[1:]:
        total = total + other[...]
    return total


def by_rows(block, cols, here, spread):
    tall, wide = block.shape
    duals = []
    for top in range(0, tall, 64):
        group = [jnp.zeros((8, 128), F32) for _ in range(8)]
        for left in range(0, wide, 128):
            dual = spread[:, left:left + 128]
            for place in range(8):
                rows = slice(top + place * 8, top + (place + 1) * 8)
                group[place] = group[place] + block[rows, left:left + 128] * dual
        duals.append(lane_sums(jnp.concatenate(group)))
    return cols[1, here, :] - cols[0, here, :] * jnp.concatenate(duals)


def by_cols(block, column):
    tall, wide = block.shape
    sums = [jnp.zeros((8, 128), F32) for _ in range(wide // 128)]
    for top in range(0, tall, 8):
        dual = column[top:top + 8, :]
        for place in range(wide // 128):
            sums[place] = sums[place] + block[top:top + 8, place * 128:(place + 1) * 128] * dual
    return jnp.concatenate(sums, 1)


def chunk(index):
    return pl.ds(pl.multiple_of(index * STEP, STEP), STEP)


def sweep_kernel(opening, shares, plan, cols, *refs):
    if opening:
        parts, (_, _, sums_out, part_out, spread, total) = refs[:shares], refs[shares:]
        sums_out[...] = added(parts)
        row_dual = sums_out[1:2, :] / sums_out[0:1, :]
    else:
        (sums, *parts), (_, _, part_out, spread, total) = refs[:shares + 1], refs[shares + 1:]
        row_dual = (sums[1:2, :] - added(parts)) / sums[0:1, :]
    spread[...] = jnp.broadcast_to(row_dual, spread.shape)
    total[...] = jnp.zeros_like(total)
    steps = plan.shape[0] // STEP

    def duals(index):
        here = chunk(index)
        return by_rows(plan.at[here, :], cols, here, spread)

    def step(index, dual):
        product = by_cols(plan.at[chunk(index - 1), :], dual)
        dual = duals(index)
        total[...] += product
        return dual

    last = lax.fori_loop(1, steps, step, duals(0))
    total[...] += by_cols(plan.at[chunk(steps - 1), :], last)
    part_out[...] = jnp.sum(total[...], axis=0, keepdims=True)


def embed_before_kernel(logit_scale, protos, emb_ext, after, entry_out, token):
    del after
    scale = logit_scale * LOG2E
    token[...] = jnp.zeros_like(token)

    def step(index, carry):
        here = chunk(index)
        entry_out[here, :] = logit_scale * jnp.exp2(scale * mm(protos[here, :], emb_ext[:, 0:entry_out.shape[1]]))
        return carry

    lax.fori_loop(0, protos.shape[0] // STEP, step, 0)


def cotangent_kernel(view_scale, block, ids, protos, view_t, after, cot_out, token):
    del after
    width = view_t.shape[0]
    tall, wide = cot_out.shape
    token[...] = jnp.zeros_like(token)
    first = pl.multiple_of(block(ids) * tall, tall)

    def step(index, carry):
        here = chunk(index)
        from_row = pl.ds(pl.multiple_of(first + index * STEP, STEP), STEP)
        cot_out[here, :] = -view_scale * mm(protos[from_row, 0:width], view_t[:, 0:wide])
        return carry

    lax.fori_loop(0, tall // STEP, step, 0)


def embed_kernel(shares, ids, plan, cols, sums, protos_t, entries, cots, *refs):
    parts, (_, duals_out, rows_out, keep, give, spread, whole) = refs[:shares], refs[shares:]
    width = protos_t.shape[0]
    rows = entries.shape[1]
    rows_out[...] = (sums[1:2, :] - added(parts)) / sums[0:1, :]
    spread[...] = jnp.broadcast_to(rows_out[...], spread.shape)
    own_dual = rows_out[:, 0:rows]

    def duals(index, carry):
        here = chunk(index)
        duals_out[here, :] = by_rows(plan.at[here, :], cols, here, spread)
        return carry

    lax.fori_loop(0, plan.shape[0] // STEP, duals, 0)
    total = jnp.zeros((width, rows), F32)
    for start in range(0, plan.shape[0], CHUNK):
        here = slice(start, start + CHUNK)
        grad = entries[here, :] * (cots[here, :] - own_dual - widened(duals_out[here, :], rows))
        total = total + mm(protos_t[:, here], grad.astype(BF16))
    whole[...] = jnp.transpose(total)
    tall = keep.shape[1]
    for place in range(shares):
        above, beside = divmod(place, shares // 2)
        to = ((ids[0] & 1) ^ above) * shares + (ids[1] ^ (2 * beside))
        keep[place] = whole[pl.ds(pl.multiple_of(to * tall, tall), tall), :]
        give[place] = whole[pl.ds(pl.multiple_of((to ^ 1) * tall, tall), tall), :]


def proto_before_kernel(logit_scale, view_scale, ids, protos, emb_ext, view_t, after, entry_out, second_out, token):
    del after
    own, rows = entry_out.shape
    width = second_out.shape[1]
    scale = logit_scale * LOG2E
    token[...] = jnp.zeros_like(token)
    here = pl.ds(pl.multiple_of((ids[0] >> 1) * own, own), own)
    total = jnp.zeros((own, width), F32)
    for start in range(0, rows, 2 * width):
        cols = slice(start, start + 2 * width)
        exact = jnp.exp2(scale * mm(protos[here, :], emb_ext[:, cols]))
        entry_out[:, cols] = logit_scale * exact
        total = total + mm((-view_scale * exact).astype(BF16), view_t[:, cols], NT)
    second_out[...] = total


def proto_kernel(half, ids, emb_ext, entries, cots, so_far, col_dual, row_dual, *outs):
    own, width = outs[0].shape
    here = pl.ds(pl.multiple_of((ids[0] >> 1) * own, own), own)
    column = widened(col_dual[here, :], 2 * width)
    total = so_far[...]
    some = entries.shape[1] // 2
    for start in range(half * some, (half + 1) * some, 2 * width):
        cols = slice(start, start + 2 * width)
        grad = entries[:, cols] * (cots[:, cols] - row_dual[:, cols] - column)
        total = total + mm(grad.astype(BF16), emb_ext[0:width, cols], NT)
    outs[0][...] = total
    for token in outs[1:]:
        token[...] = jnp.zeros_like(token)


def call(kernel, out_shape, name, scalars=0, scratch=(), aliases=None, limit=16):
    def run(*args):
        whole = pl.BlockSpec(memory_space=pltpu.VMEM)
        small = pl.BlockSpec(memory_space=pltpu.SMEM)
        return pl.pallas_call(
            kernel,
            out_shape=out_shape,
            in_specs=[small] * scalars + [whole] * (len(args) - scalars),
            out_specs=jax.tree.map(lambda _: whole, out_shape),
            scratch_shapes=[pltpu.VMEM(dims, dtype) for dtype, *dims in scratch],
            input_output_aliases=aliases or {},
            compiler_params=pltpu.CompilerParams(vmem_limit_bytes=limit << 20),
            name=name,
        )(*args)

    return run


def swap_both(value, above, beside):
    shares = lax.axis_size("proto")
    pairs = [
        (row * shares + col, (row ^ above) * shares + (col ^ beside))
        for row in range(lax.axis_size("row"))
        for col in range(shares)
    ]
    return lax.ppermute(value, ("row", "proto"), pairs)


def others():
    shares = lax.axis_size("proto")
    return [(above, beside) for above in range(2) for beside in range(0, shares, 2)]


def exchange(part):
    near = call(add_kernel, jax.ShapeDtypeStruct(part.shape, F32), "add", limit=2)(part, swap(part, "proto", 1))
    return [near if pair == (0, 0) else swap_both(near, *pair) for pair in others()]


def kept_plan(embeddings, second_view, prototypes, row_scale, col_scale):
    rows, width = embeddings.shape
    blocks, shares = lax.axis_size("row"), lax.axis_size("proto")
    all_rows = rows * blocks
    count = prototypes.shape[0] // 2
    own = 2 * count // blocks
    ids = jnp.stack((lax.axis_index("row"), lax.axis_index("proto")))
    scales = (1.0 / (0.05 * width), 1.0 / (0.1 * width))
    log_mass = math.log(64.0 * prototypes.shape[0] * shares)
    shape = lambda *dims, dtype=F32: jax.ShapeDtypeStruct(dims, dtype)
    form = lambda kernel: functools.partial(kernel, *scales)
    there = lambda value: pltpu.with_memory_space_constraint(value, pltpu.HBM)
    row_scale = row_scale.reshape(1, rows)
    col_scale = col_scale.reshape(1, 2 * count)
    half = shape(width + EXT, rows, dtype=BF16)
    send = call(functools.partial(prep_kernel, scales[0]), half, "prepare", scalars=1)(
        ids, there(embeddings), there(second_view), there(row_scale)
    )
    protos, protos_t, token = call(
        functools.partial(turn_kernel, scales[0], log_mass),
        (shape(count, 2 * width, dtype=BF16), shape(width, count, dtype=BF16), shape(8, 128)),
        "turn",
        scalars=1,
        limit=4,
    )(ids, there(prototypes), there(col_scale))
    pairs = blocks // 2
    stack = call(functools.partial(stack_kernel, pairs), shape(pairs, width + EXT, rows, dtype=BF16), "stack", limit=2)
    direct = [send] + [swap(send, "row", step) for step in range(2, blocks, 2)]
    mine_a = stack(*direct)
    theirs_a = swap(mine_a, "proto", 1)
    mine_b = stack(*[swap(value, "row", 1) for value in direct], token)
    theirs_b = swap(mine_b, "proto", 1)

    kept = pltpu.VMEM((count, all_rows), F32)
    plan, cols, sums, emb_ext, view_t = call(
        form(plan_kernel),
        (kept, shape(2, count, 128), shape(2, all_rows), shape(2 * width, all_rows, dtype=BF16), shape(width, all_rows, dtype=BF16)),
        "plan",
        scalars=1,
        scratch=[(F32, 8, all_rows), (F32, 8, all_rows)],
        limit=12,
    )(ids, protos, mine_a, theirs_a, mine_b, theirs_b)

    work = [(F32, 8, all_rows), (F32, 8, all_rows)]
    token = shape(8, 128)
    parts = exchange(sums)
    entries, done = call(
        functools.partial(embed_before_kernel, scales[0]),
        (shape(count, 2 * rows), token),
        "embed_before",
        limit=6,
    )(protos, emb_ext, parts[0])
    plan, sums, part = call(
        functools.partial(sweep_kernel, True, shares),
        (kept, shape(2, all_rows), shape(1, all_rows)),
        "sweep",
        scratch=work,
        aliases={0: 0},
        limit=4,
    )(plan, cols, *parts, done)
    cotangent = lambda dims, block: call(
        functools.partial(cotangent_kernel, scales[1], block), (shape(*dims), token), "cotangent", scalars=1, limit=4
    )
    for sweep in range(ITERS - 2):
        parts = exchange(part)
        if sweep == ITERS - 3:
            cots, done = cotangent((count, 2 * rows), lambda ids: 0)(ids, protos, view_t, parts[0])
        if sweep == 0:
            own_entries, second, done = call(
                form(proto_before_kernel),
                (shape(own, all_rows), shape(own, width), token),
                "proto_before",
                scalars=1,
                limit=6,
            )(ids, protos, emb_ext, view_t, parts[0])
        plan, part = call(
            functools.partial(sweep_kernel, False, shares),
            (kept, shape(1, all_rows)),
            "sweep",
            scratch=work,
            aliases={0: 0},
            limit=4,
        )(plan, cols, sums, *parts, done)
    parts = exchange(part)
    own_cots, done = cotangent((own, all_rows), lambda ids: ids[0] >> 1)(ids, protos, view_t, parts[0])
    pieces = shape(shares, rows // shares, width)
    col_dual, row_dual, keep, give = call(
        functools.partial(embed_kernel, shares),
        (shape(count, 128), shape(1, all_rows), pieces, pieces),
        "embed_grad",
        scalars=1,
        scratch=work[:1] + [(F32, 2 * rows, width)],
        limit=8,
    )(ids, plan, cols, sums, protos_t, entries, cots, *parts, done)
    half = lambda number, outs: call(functools.partial(proto_kernel, number), outs, "proto_grad", scalars=1, limit=6)
    second, done = half(0, (shape(own, width), token))(ids, emb_ext, own_entries, own_cots, second, col_dual, row_dual)
    near = call(add_kernel, pieces, "add", limit=2)(keep, swap(give, "proto", 1), done)
    embed_grad = near[0]
    for place, pair in list(enumerate(others()))[1:]:
        embed_grad = embed_grad + swap_both(near[place], *pair)
    proto_grad = half(1, (shape(own, width),))(ids, emb_ext, own_entries, own_cots, second, col_dual, row_dual)[0]
    return embed_grad, proto_grad


def contract_rows(left, right):
    return mm(left, right, (((0,), (0,)), ((), ())))


def contract_width(left, right):
    return mm(left, right, NT)


def sum_over(value, axis):
    size = lax.axis_size(axis)
    parts = [value] + [swap(value, axis, step) for step in range(1, size)]
    return sum(parts[1:], parts[0])


def scatter_sum(value, axis):
    size = lax.axis_size(axis)
    me = lax.axis_index(axis)
    rows = value.shape[0] // size
    block = lambda owner: lax.dynamic_slice_in_dim(value, owner * rows, rows, 0)
    total = block(me)
    for step in range(1, size):
        total = total + swap(block(me ^ step), axis, step)
    return total


def split_plan(embeddings, second_view, prototypes, row_scale, col_scale):
    feat_width = embeddings.shape[1]
    proto_count = prototypes.shape[0]
    logit_scale = 1.0 / (0.05 * feat_width)
    view_scale = 1.0 / (0.1 * feat_width)
    plan_mass = 64.0 * proto_count * lax.axis_size("proto")

    logits = contract_width(embeddings, prototypes) * logit_scale
    plan = row_scale[:, None] * col_scale[None, :] * jnp.exp(logits) / plan_mass
    cotangent = -contract_width(second_view, prototypes) * view_scale
    weighted = plan * cotangent

    row_mass, row_weight = sum_over(jnp.stack((plan.sum(1), weighted.sum(1))), "proto")
    row_dual = row_weight / row_mass
    sums = jnp.stack((plan.sum(0), weighted.sum(0), (row_dual[:, None] * plan).sum(0)))
    col_mass, col_weight, product = sum_over(sums, "row")
    col_dual = (col_weight - product) / col_mass
    for sweep in range(ITERS - 1):
        product = sum_over((plan * col_dual[None, :]).sum(1), "proto")
        row_dual = (row_weight - product) / row_mass
        product = sum_over((plan * row_dual[:, None]).sum(0), "row")
        col_dual = (col_weight - product) / col_mass
    logit_grad = plan * (cotangent - row_dual[:, None] - col_dual[None, :])
    scaled_grad = (logit_scale * logit_grad).astype(jnp.bfloat16)
    scaled_plan = (-view_scale * plan).astype(jnp.bfloat16)
    embed_grad = scatter_sum(
        jnp.dot(scaled_grad, prototypes, preferred_element_type=jnp.float32), "proto"
    )
    proto_grad = scatter_sum(
        contract_rows(scaled_grad, embeddings) + contract_rows(scaled_plan, second_view), "row"
    )
    return (embed_grad, proto_grad)


def per_device(embeddings, second_view, prototypes, row_scale, col_scale):
    blocks, shares = lax.axis_size("row"), lax.axis_size("proto")
    rows, width = embeddings.shape
    count = prototypes.shape[0]
    fits = rows * blocks * count * 2 <= PLAN_BYTES
    even = all(n & (n - 1) == 0 and n > 1 for n in (blocks, shares))
    even = even and rows % (16 * shares) == 0 and rows % width == 0
    tiled = rows % 128 == 0 and width % 128 == 0 and count == blocks * CHUNK and blocks % 4 == 0
    form = kept_plan if fits and even and tiled else split_plan
    return form(embeddings, second_view, prototypes, row_scale, col_scale)


def solution(mesh):
    return jax.shard_map(
        per_device,
        mesh=mesh,
        in_specs=(P("row", None), P("row", None), P("proto", None), P("row"), P("proto")),
        out_specs=(P(("row", "proto"), None), P(("proto", "row"), None)),
        check_vma=False,
    )
```

```python
import functools
import math

import jax
import jax.numpy as jnp
from jax import lax
from jax.experimental import pallas as pl
from jax.experimental.pallas import tpu as pltpu
from jax.sharding import PartitionSpec as P

ITERS = 4
CHUNK = 512
STEP = 256
EXT = 16
PLAN_BYTES = 24 << 20
LOG2E = 1.4426950408889634
F32, BF16 = jnp.float32, jnp.bfloat16
NT = (((1,), (1,)), ((), ()))
NN = (((1,), (0,)), ((), ()))


def mm(left, right, dims=NN):
    return lax.dot_general(left, right, dims, preferred_element_type=F32)


def swap(value, axis, step):
    size = lax.axis_size(axis)
    return lax.ppermute(value, axis, [(i, i ^ step) for i in range(size)])


def lane_sums(block):
    return jnp.broadcast_to(jnp.sum(block, axis=1, keepdims=True), (block.shape[0], 128))


def widened(column, width):
    return jnp.concatenate([column] * (width // 128), 1)


def rows_of(pieces, height=EXT):
    index = lax.broadcasted_iota(jnp.int32, (height, pieces[0].shape[1]), 0)
    total = jnp.zeros(index.shape, F32)
    for place, piece in enumerate(pieces):
        total = jnp.where(index == place, piece, total)
    return total


def pieces_of(row):
    out = []
    for _ in range(3):
        out.append(row.astype(BF16).astype(F32))
        row = row - out[-1]
    return out, [jnp.ones_like(row)] * 3


def prep_kernel(logit_scale, ids, embeddings, second_view, row_scale, send_out):
    rows, width = embeddings.shape

    @pl.when(ids[1] & 1 == 0)
    def _():
        logs, ones = pieces_of(jnp.log(row_scale[...]) / logit_scale)
        send_out[0:width, :] = jnp.transpose(embeddings[...].astype(F32)).astype(BF16)
        send_out[width:width + EXT, :] = rows_of(logs + ones).astype(BF16)

    @pl.when(ids[1] & 1 != 0)
    def _():
        send_out[0:width, :] = jnp.transpose(second_view[...].astype(F32)).astype(BF16)
        send_out[width:width + EXT, :] = jnp.zeros((EXT, rows), BF16)


def turn_kernel(logit_scale, log_mass, ids, protos, col_scale, protos_out, protos_t, token):
    count = protos_out.shape[0]
    width = protos.shape[1]
    token[...] = jnp.zeros_like(token)

    def step(index, carry):
        here = pl.ds(pl.multiple_of(index * CHUNK, CHUNK), CHUNK)
        there = pl.ds(pl.multiple_of((2 * index + (ids[0] & 1)) * CHUNK, CHUNK), CHUNK)
        block = protos[there, :]
        logs, ones = pieces_of((jnp.log(col_scale[:, there]) - log_mass) / logit_scale)
        protos_out[here, 0:width] = block
        protos_out[here, width:] = jnp.transpose(rows_of(ones + logs, width)).astype(BF16)
        protos_t[:, here] = jnp.transpose(block.astype(F32)).astype(BF16)
        return carry

    lax.fori_loop(0, count // CHUNK, step, 0)


def stack_kernel(count, *refs):
    for place in range(count):
        refs[-1][place] = refs[place][...]


def add_kernel(left, right, *refs):
    refs[-1][...] = left[...] + right[...]


def plan_kernel(logit_scale, view_scale, ids, protos, mine_a, theirs_a, mine_b, theirs_b, plan_out, cols_out, sums_out, emb_ext, view_t, row_mass, row_weight):
    pairs, high, rows = mine_a.shape
    blocks = 2 * pairs
    count = protos.shape[0]
    width = view_t.shape[0]
    scale = logit_scale * LOG2E
    emb_ext[high:, :] = jnp.zeros((emb_ext.shape[0] - high, blocks * rows), BF16)

    def fill(embs, views):
        for block in range(blocks):
            cols = slice(block * rows, (block + 1) * rows)
            emb_ext[0:high, cols] = embs[block % 2][block // 2]
            view_t[:, cols] = views[block % 2][block // 2, 0:width, :]

    for core in range(2):
        for odd in range(2):
            a, b = ((mine_a, theirs_a), (mine_b, theirs_b)) if core == 0 else ((theirs_a, mine_a), (theirs_b, mine_b))
            low, upper = (a, b) if odd == 0 else (b, a)
            is_this = jnp.logical_and(ids[1] & 1 == core, ids[0] & 1 == odd)
            pl.when(is_this)(functools.partial(fill, (low[0], upper[0]), (low[1], upper[1])))
    row_mass[...] = jnp.zeros_like(row_mass)
    row_weight[...] = jnp.zeros_like(row_weight)

    def folded(block):
        tiles = [block[:, left:left + 128] for left in range(0, block.shape[1], 128)]
        across = tiles[0]
        for tile in tiles[1:]:
            across = across + tile
        return across, jnp.sum(block.reshape(block.shape[0] // 8, 8, block.shape[1]), axis=0)

    def step(index, carry):
        here = pl.ds(pl.multiple_of(index * CHUNK, CHUNK), CHUNK)
        mass = weight = jnp.zeros((CHUNK, 128), F32)
        for block in range(blocks):
            cols = slice(block * rows, (block + 1) * rows)
            plan = jnp.exp2(scale * mm(protos[here, :], emb_ext[:, cols]))
            plan_out[here, cols] = plan
            across, down = folded(plan)
            mass = mass + across
            row_mass[:, cols] += down
            across, down = folded(plan * mm(protos[here, 0:width], view_t[:, cols]))
            weight = weight + across
            row_weight[:, cols] += down
        inverse = 1.0 / lane_sums(mass)
        cols_out[0, here, :] = inverse
        cols_out[1, here, :] = -view_scale * lane_sums(weight) * inverse
        return carry

    lax.fori_loop(0, count // CHUNK, step, 0, unroll=True)
    sums_out[0:1, :] = jnp.sum(row_mass[...], axis=0, keepdims=True)
    sums_out[1:2, :] = -view_scale * jnp.sum(row_weight[...], axis=0, keepdims=True)


def added(parts):
    total = parts[0][...]
    for other in parts[1:]:
        total = total + other[...]
    return total


def by_rows(block, cols, here, spread):
    tall, wide = block.shape
    duals = []
    for top in range(0, tall, 64):
        group = [jnp.zeros((8, 128), F32) for _ in range(8)]
        for left in range(0, wide, 128):
            dual = spread[:, left:left + 128]
            for place in range(8):
                rows = slice(top + place * 8, top + (place + 1) * 8)
                group[place] = group[place] + block[rows, left:left + 128] * dual
        duals.append(lane_sums(jnp.concatenate(group)))
    return cols[1, here, :] - cols[0, here, :] * jnp.concatenate(duals)


def by_cols(block, column):
    tall, wide = block.shape
    sums = [jnp.zeros((8, 128), F32) for _ in range(wide // 128)]
    for top in range(0, tall, 8):
        dual = column[top:top + 8, :]
        for place in range(wide // 128):
            sums[place] = sums[place] + block[top:top + 8, place * 128:(place + 1) * 128] * dual
    return jnp.concatenate(sums, 1)


def chunk(index):
    return pl.ds(pl.multiple_of(index * STEP, STEP), STEP)


def sweep_kernel(opening, shares, plan, cols, *refs):
    if opening:
        parts, (_, _, sums_out, part_out, spread, total) = refs[:shares], refs[shares:]
        sums_out[...] = added(parts)
        row_dual = sums_out[1:2, :] / sums_out[0:1, :]
    else:
        (sums, *parts), (_, _, part_out, spread, total) = refs[:shares + 1], refs[shares + 1:]
        row_dual = (sums[1:2, :] - added(parts)) / sums[0:1, :]
    spread[...] = jnp.broadcast_to(row_dual, spread.shape)
    total[...] = jnp.zeros_like(total)
    steps = plan.shape[0] // STEP

    def duals(index):
        here = chunk(index)
        return by_rows(plan.at[here, :], cols, here, spread)

    def step(index, dual):
        product = by_cols(plan.at[chunk(index - 1), :], dual)
        dual = duals(index)
        total[...] += product
        return dual

    last = lax.fori_loop(1, steps, step, duals(0), unroll=2)
    total[...] += by_cols(plan.at[chunk(steps - 1), :], last)
    part_out[...] = jnp.sum(total[...], axis=0, keepdims=True)


def embed_before_kernel(logit_scale, protos, emb_ext, after, entry_out, token):
    del after
    scale = logit_scale * LOG2E
    token[...] = jnp.zeros_like(token)

    def step(index, carry):
        here = chunk(index)
        entry_out[here, :] = logit_scale * jnp.exp2(scale * mm(protos[here, :], emb_ext[:, 0:entry_out.shape[1]]))
        return carry

    lax.fori_loop(0, protos.shape[0] // STEP, step, 0)


def cotangent_kernel(view_scale, block, ids, protos, view_t, after, cot_out, token):
    del after
    width = view_t.shape[0]
    tall, wide = cot_out.shape
    token[...] = jnp.zeros_like(token)
    first = pl.multiple_of(block(ids) * tall, tall)

    def step(index, carry):
        here = chunk(index)
        from_row = pl.ds(pl.multiple_of(first + index * STEP, STEP), STEP)
        cot_out[here, :] = -view_scale * mm(protos[from_row, 0:width], view_t[:, 0:wide])
        return carry

    lax.fori_loop(0, tall // STEP, step, 0)


def embed_kernel(shares, ids, plan, cols, sums, protos_t, entries, cots, *refs):
    parts, (_, duals_out, rows_out, keep, give, spread, whole) = refs[:shares], refs[shares:]
    width = protos_t.shape[0]
    rows = entries.shape[1]
    rows_out[...] = (sums[1:2, :] - added(parts)) / sums[0:1, :]
    spread[...] = jnp.broadcast_to(rows_out[...], spread.shape)
    own_dual = rows_out[:, 0:rows]

    def duals(index, carry):
        here = chunk(index)
        duals_out[here, :] = by_rows(plan.at[here, :], cols, here, spread)
        return carry

    lax.fori_loop(0, plan.shape[0] // STEP, duals, 0, unroll=2)
    total = jnp.zeros((width, rows), F32)
    for start in range(0, plan.shape[0], CHUNK):
        here = slice(start, start + CHUNK)
        grad = entries[here, :] * (cots[here, :] - own_dual - widened(duals_out[here, :], rows))
        total = total + mm(protos_t[:, here], grad.astype(BF16))
    whole[...] = jnp.transpose(total)
    tall = keep.shape[1]
    for place in range(shares):
        above, beside = divmod(place, shares // 2)
        to = ((ids[0] & 1) ^ above) * shares + (ids[1] ^ (2 * beside))
        keep[place] = whole[pl.ds(pl.multiple_of(to * tall, tall), tall), :]
        give[place] = whole[pl.ds(pl.multiple_of((to ^ 1) * tall, tall), tall), :]


def proto_before_kernel(logit_scale, view_scale, ids, protos, emb_ext, view_t, after, entry_out, second_out, token):
    del after
    own, rows = entry_out.shape
    width = second_out.shape[1]
    scale = logit_scale * LOG2E
    token[...] = jnp.zeros_like(token)
    here = pl.ds(pl.multiple_of((ids[0] >> 1) * own, own), own)
    total = jnp.zeros((own, width), F32)
    for start in range(0, rows, 2 * width):
        cols = slice(start, start + 2 * width)
        exact = jnp.exp2(scale * mm(protos[here, :], emb_ext[:, cols]))
        entry_out[:, cols] = logit_scale * exact
        total = total + mm((-view_scale * exact).astype(BF16), view_t[:, cols], NT)
    second_out[...] = total


def proto_kernel(half, ids, emb_ext, entries, cots, so_far, col_dual, row_dual, *outs):
    own, width = outs[0].shape
    here = pl.ds(pl.multiple_of((ids[0] >> 1) * own, own), own)
    column = widened(col_dual[here, :], 2 * width)
    total = so_far[...]
    some = entries.shape[1] // 2
    for start in range(half * some, (half + 1) * some, 2 * width):
        cols = slice(start, start + 2 * width)
        grad = entries[:, cols] * (cots[:, cols] - row_dual[:, cols] - column)
        total = total + mm(grad.astype(BF16), emb_ext[0:width, cols], NT)
    outs[0][...] = total
    for token in outs[1:]:
        token[...] = jnp.zeros_like(token)


def call(kernel, out_shape, name, scalars=0, scratch=(), aliases=None, limit=16):
    def run(*args):
        whole = pl.BlockSpec(memory_space=pltpu.VMEM)
        small = pl.BlockSpec(memory_space=pltpu.SMEM)
        return pl.pallas_call(
            kernel,
            out_shape=out_shape,
            in_specs=[small] * scalars + [whole] * (len(args) - scalars),
            out_specs=jax.tree.map(lambda _: whole, out_shape),
            scratch_shapes=[pltpu.VMEM(dims, dtype) for dtype, *dims in scratch],
            input_output_aliases=aliases or {},
            compiler_params=pltpu.CompilerParams(vmem_limit_bytes=limit << 20),
            name=name,
        )(*args)

    return run


def swap_both(value, above, beside):
    shares = lax.axis_size("proto")
    pairs = [
        (row * shares + col, (row ^ above) * shares + (col ^ beside))
        for row in range(lax.axis_size("row"))
        for col in range(shares)
    ]
    return lax.ppermute(value, ("row", "proto"), pairs)


def others():
    shares = lax.axis_size("proto")
    return [(above, beside) for above in range(2) for beside in range(0, shares, 2)]


def exchange(part):
    near = call(add_kernel, jax.ShapeDtypeStruct(part.shape, F32), "add", limit=2)(part, swap(part, "proto", 1))
    return [near if pair == (0, 0) else swap_both(near, *pair) for pair in others()]


def kept_plan(embeddings, second_view, prototypes, row_scale, col_scale):
    rows, width = embeddings.shape
    blocks, shares = lax.axis_size("row"), lax.axis_size("proto")
    all_rows = rows * blocks
    count = prototypes.shape[0] // 2
    own = 2 * count // blocks
    ids = jnp.stack((lax.axis_index("row"), lax.axis_index("proto")))
    scales = (1.0 / (0.05 * width), 1.0 / (0.1 * width))
    log_mass = math.log(64.0 * prototypes.shape[0] * shares)
    shape = lambda *dims, dtype=F32: jax.ShapeDtypeStruct(dims, dtype)
    form = lambda kernel: functools.partial(kernel, *scales)
    there = lambda value: pltpu.with_memory_space_constraint(value, pltpu.HBM)
    row_scale = row_scale.reshape(1, rows)
    col_scale = col_scale.reshape(1, 2 * count)
    half = shape(width + EXT, rows, dtype=BF16)
    send = call(functools.partial(prep_kernel, scales[0]), half, "prepare", scalars=1)(
        ids, there(embeddings), there(second_view), there(row_scale)
    )
    protos, protos_t, token = call(
        functools.partial(turn_kernel, scales[0], log_mass),
        (shape(count, 2 * width, dtype=BF16), shape(width, count, dtype=BF16), shape(8, 128)),
        "turn",
        scalars=1,
        limit=4,
    )(ids, there(prototypes), there(col_scale))
    pairs = blocks // 2
    stack = call(functools.partial(stack_kernel, pairs), shape(pairs, width + EXT, rows, dtype=BF16), "stack", limit=2)
    direct = [send] + [swap(send, "row", step) for step in range(2, blocks, 2)]
    mine_a = stack(*direct)
    theirs_a = swap(mine_a, "proto", 1)
    mine_b = stack(*[swap(value, "row", 1) for value in direct], token)
    theirs_b = swap(mine_b, "proto", 1)

    kept = pltpu.VMEM((count, all_rows), F32)
    plan, cols, sums, emb_ext, view_t = call(
        form(plan_kernel),
        (kept, shape(2, count, 128), shape(2, all_rows), shape(2 * width, all_rows, dtype=BF16), shape(width, all_rows, dtype=BF16)),
        "plan",
        scalars=1,
        scratch=[(F32, 8, all_rows), (F32, 8, all_rows)],
        limit=12,
    )(ids, protos, mine_a, theirs_a, mine_b, theirs_b)

    work = [(F32, 8, all_rows), (F32, 8, all_rows)]
    token = shape(8, 128)
    parts = exchange(sums)
    entries, done = call(
        functools.partial(embed_before_kernel, scales[0]),
        (shape(count, 2 * rows), token),
        "embed_before",
        limit=6,
    )(protos, emb_ext, parts[0])
    plan, sums, part = call(
        functools.partial(sweep_kernel, True, shares),
        (kept, shape(2, all_rows), shape(1, all_rows)),
        "sweep",
        scratch=work,
        aliases={0: 0},
        limit=4,
    )(plan, cols, *parts, done)
    cotangent = lambda dims, block: call(
        functools.partial(cotangent_kernel, scales[1], block), (shape(*dims), token), "cotangent", scalars=1, limit=4
    )
    for sweep in range(ITERS - 2):
        parts = exchange(part)
        if sweep == ITERS - 3:
            cots, done = cotangent((count, 2 * rows), lambda ids: 0)(ids, protos, view_t, parts[0])
        if sweep == 0:
            own_entries, second, done = call(
                form(proto_before_kernel),
                (shape(own, all_rows), shape(own, width), token),
                "proto_before",
                scalars=1,
                limit=6,
            )(ids, protos, emb_ext, view_t, parts[0])
        plan, part = call(
            functools.partial(sweep_kernel, False, shares),
            (kept, shape(1, all_rows)),
            "sweep",
            scratch=work,
            aliases={0: 0},
            limit=4,
        )(plan, cols, sums, *parts, done)
    parts = exchange(part)
    own_cots, done = cotangent((own, all_rows), lambda ids: ids[0] >> 1)(ids, protos, view_t, parts[0])
    pieces = shape(shares, rows // shares, width)
    col_dual, row_dual, keep, give = call(
        functools.partial(embed_kernel, shares),
        (shape(count, 128), shape(1, all_rows), pieces, pieces),
        "embed_grad",
        scalars=1,
        scratch=work[:1] + [(F32, 2 * rows, width)],
        limit=8,
    )(ids, plan, cols, sums, protos_t, entries, cots, *parts, done)
    half = lambda number, outs: call(functools.partial(proto_kernel, number), outs, "proto_grad", scalars=1, limit=6)
    second, done = half(0, (shape(own, width), token))(ids, emb_ext, own_entries, own_cots, second, col_dual, row_dual)
    near = call(add_kernel, pieces, "add", limit=2)(keep, swap(give, "proto", 1), done)
    embed_grad = near[0]
    for place, pair in list(enumerate(others()))[1:]:
        embed_grad = embed_grad + swap_both(near[place], *pair)
    proto_grad = half(1, (shape(own, width),))(ids, emb_ext, own_entries, own_cots, second, col_dual, row_dual)[0]
    return embed_grad, proto_grad


def contract_rows(left, right):
    return mm(left, right, (((0,), (0,)), ((), ())))


def contract_width(left, right):
    return mm(left, right, NT)


def sum_over(value, axis):
    size = lax.axis_size(axis)
    parts = [value] + [swap(value, axis, step) for step in range(1, size)]
    return sum(parts[1:], parts[0])


def scatter_sum(value, axis):
    size = lax.axis_size(axis)
    me = lax.axis_index(axis)
    rows = value.shape[0] // size
    block = lambda owner: lax.dynamic_slice_in_dim(value, owner * rows, rows, 0)
    total = block(me)
    for step in range(1, size):
        total = total + swap(block(me ^ step), axis, step)
    return total


def split_plan(embeddings, second_view, prototypes, row_scale, col_scale):
    feat_width = embeddings.shape[1]
    proto_count = prototypes.shape[0]
    logit_scale = 1.0 / (0.05 * feat_width)
    view_scale = 1.0 / (0.1 * feat_width)
    plan_mass = 64.0 * proto_count * lax.axis_size("proto")

    logits = contract_width(embeddings, prototypes) * logit_scale
    plan = row_scale[:, None] * col_scale[None, :] * jnp.exp(logits) / plan_mass
    cotangent = -contract_width(second_view, prototypes) * view_scale
    weighted = plan * cotangent

    row_mass, row_weight = sum_over(jnp.stack((plan.sum(1), weighted.sum(1))), "proto")
    row_dual = row_weight / row_mass
    sums = jnp.stack((plan.sum(0), weighted.sum(0), (row_dual[:, None] * plan).sum(0)))
    col_mass, col_weight, product = sum_over(sums, "row")
    col_dual = (col_weight - product) / col_mass
    for sweep in range(ITERS - 1):
        product = sum_over((plan * col_dual[None, :]).sum(1), "proto")
        row_dual = (row_weight - product) / row_mass
        product = sum_over((plan * row_dual[:, None]).sum(0), "row")
        col_dual = (col_weight - product) / col_mass
    logit_grad = plan * (cotangent - row_dual[:, None] - col_dual[None, :])
    scaled_grad = (logit_scale * logit_grad).astype(jnp.bfloat16)
    scaled_plan = (-view_scale * plan).astype(jnp.bfloat16)
    embed_grad = scatter_sum(
        jnp.dot(scaled_grad, prototypes, preferred_element_type=jnp.float32), "proto"
    )
    proto_grad = scatter_sum(
        contract_rows(scaled_grad, embeddings) + contract_rows(scaled_plan, second_view), "row"
    )
    return (embed_grad, proto_grad)


def per_device(embeddings, second_view, prototypes, row_scale, col_scale):
    blocks, shares = lax.axis_size("row"), lax.axis_size("proto")
    rows, width = embeddings.shape
    count = prototypes.shape[0]
    fits = rows * blocks * count * 2 <= PLAN_BYTES
    even = all(n & (n - 1) == 0 and n > 1 for n in (blocks, shares))
    even = even and rows % (16 * shares) == 0 and rows % width == 0
    tiled = rows % 128 == 0 and width % 128 == 0 and count == blocks * CHUNK and blocks % 4 == 0
    form = kept_plan if fits and even and tiled else split_plan
    return form(embeddings, second_view, prototypes, row_scale, col_scale)


def solution(mesh):
    return jax.shard_map(
        per_device,
        mesh=mesh,
        in_specs=(P("row", None), P("row", None), P("proto", None), P("row"), P("proto")),
        out_specs=(P(("row", "proto"), None), P(("proto", "row"), None)),
        check_vma=False,
    )
```

```python
import functools
import math

import jax
import jax.numpy as jnp
from jax import lax
from jax.experimental import pallas as pl
from jax.experimental.pallas import tpu as pltpu
from jax.sharding import PartitionSpec as P

ITERS = 4
CHUNK = 512
STEP = 256
EXT = 16
PLAN_BYTES = 24 << 20
LOG2E = 1.4426950408889634
F32, BF16 = jnp.float32, jnp.bfloat16
NT = (((1,), (1,)), ((), ()))
NN = (((1,), (0,)), ((), ()))


def mm(left, right, dims=NN):
    return lax.dot_general(left, right, dims, preferred_element_type=F32)


def swap(value, axis, step):
    size = lax.axis_size(axis)
    return lax.ppermute(value, axis, [(i, i ^ step) for i in range(size)])


def lane_sums(block):
    return jnp.broadcast_to(jnp.sum(block, axis=1, keepdims=True), (block.shape[0], 128))


def widened(column, width):
    return jnp.concatenate([column] * (width // 128), 1)


def rows_of(pieces, height=EXT):
    index = lax.broadcasted_iota(jnp.int32, (height, pieces[0].shape[1]), 0)
    total = jnp.zeros(index.shape, F32)
    for place, piece in enumerate(pieces):
        total = jnp.where(index == place, piece, total)
    return total


def pieces_of(row):
    out = []
    for _ in range(3):
        out.append(row.astype(BF16).astype(F32))
        row = row - out[-1]
    return out, [jnp.ones_like(row)] * 3


def prep_kernel(logit_scale, ids, embeddings, second_view, row_scale, send_out):
    rows, width = embeddings.shape

    @pl.when(ids[1] & 1 == 0)
    def _():
        logs, ones = pieces_of(jnp.log(row_scale[...]) / logit_scale)
        send_out[0:width, :] = jnp.transpose(embeddings[...].astype(F32)).astype(BF16)
        send_out[width:width + EXT, :] = rows_of(logs + ones).astype(BF16)

    @pl.when(ids[1] & 1 != 0)
    def _():
        send_out[0:width, :] = jnp.transpose(second_view[...].astype(F32)).astype(BF16)
        send_out[width:width + EXT, :] = jnp.zeros((EXT, rows), BF16)


def turn_kernel(logit_scale, log_mass, ids, protos, col_scale, protos_out, protos_t, token):
    count = protos_out.shape[0]
    width = protos.shape[1]
    token[...] = jnp.zeros_like(token)

    def step(index, carry):
        here = pl.ds(pl.multiple_of(index * CHUNK, CHUNK), CHUNK)
        there = pl.ds(pl.multiple_of((2 * index + (ids[0] & 1)) * CHUNK, CHUNK), CHUNK)
        block = protos[there, :]
        logs, ones = pieces_of((jnp.log(col_scale[:, there]) - log_mass) / logit_scale)
        protos_out[here, 0:width] = block
        protos_out[here, width:] = jnp.transpose(rows_of(ones + logs, width)).astype(BF16)
        protos_t[:, here] = jnp.transpose(block.astype(F32)).astype(BF16)
        return carry

    lax.fori_loop(0, count // CHUNK, step, 0)


def stack_kernel(count, *refs):
    for place in range(count):
        refs[-1][place] = refs[place][...]


def add_kernel(left, right, *refs):
    refs[-1][...] = left[...] + right[...]


def plan_kernel(logit_scale, view_scale, second, ids, protos, mine, theirs, *refs):
    if second:
        _, cols_in, sums_in, *refs = refs
    plan_out, cols_out, sums_out, emb_ext, view_t, row_mass, row_weight = refs
    blocks, high, rows = mine.shape
    count = protos.shape[0]
    width = view_t.shape[0]
    scale = logit_scale * LOG2E
    left = blocks * rows if second else 0
    emb_ext[high:, :] = jnp.zeros((emb_ext.shape[0] - high, blocks * rows), BF16)

    def fill(emb, view):
        for block in range(blocks):
            cols = slice(block * rows, (block + 1) * rows)
            emb_ext[0:high, cols] = emb[block]
            view_t[:, cols] = view[block, 0:width, :]

    pl.when(ids[1] & 1 == 0)(lambda: fill(mine, theirs))
    pl.when(ids[1] & 1 != 0)(lambda: fill(theirs, mine))
    row_mass[...] = jnp.zeros_like(row_mass)
    row_weight[...] = jnp.zeros_like(row_weight)

    def folded(block):
        tiles = [block[:, left:left + 128] for left in range(0, block.shape[1], 128)]
        across = tiles[0]
        for tile in tiles[1:]:
            across = across + tile
        return across, jnp.sum(block.reshape(block.shape[0] // 8, 8, block.shape[1]), axis=0)

    def step(index, carry):
        here = pl.ds(pl.multiple_of(index * CHUNK, CHUNK), CHUNK)
        mass = cols_in[0, here, :] if second else jnp.zeros((CHUNK, 128), F32)
        weight = cols_in[1, here, :] if second else mass
        for block in range(blocks):
            cols = slice(block * rows, (block + 1) * rows)
            plan = jnp.exp2(scale * mm(protos[here, :], emb_ext[:, cols]))
            plan_out[here, left + block * rows:left + (block + 1) * rows] = plan
            across, down = folded(plan)
            mass = mass + across
            row_mass[:, cols] += down
            across, down = folded(plan * mm(protos[here, 0:width], view_t[:, cols]))
            weight = weight + across
            row_weight[:, cols] += down
        if second:
            mass = 1.0 / lane_sums(mass)
            weight = -view_scale * lane_sums(weight) * mass
        cols_out[0, here, :] = mass
        cols_out[1, here, :] = weight
        return carry

    lax.fori_loop(0, count // CHUNK, step, 0, unroll=True)
    if second:
        sums_out[:, 0:left] = sums_in[...]
    sums_out[0:1, left:] = jnp.sum(row_mass[...], axis=0, keepdims=True)
    sums_out[1:2, left:] = -view_scale * jnp.sum(row_weight[...], axis=0, keepdims=True)


def added(parts):
    plain, turned = parts[:len(parts) // 2], parts[len(parts) // 2:]
    total, other = plain[0][...], turned[0][...]
    for part in plain[1:]:
        total = total + part[...]
    for part in turned[1:]:
        other = other + part[...]
    half = other.shape[1] // 2
    return total + jnp.concatenate((other[:, half:], other[:, :half]), 1)


def by_rows(block, cols, here, spread):
    tall, wide = block.shape
    duals = []
    for top in range(0, tall, 64):
        group = [jnp.zeros((8, 128), F32) for _ in range(8)]
        for left in range(0, wide, 128):
            dual = spread[:, left:left + 128]
            for place in range(8):
                rows = slice(top + place * 8, top + (place + 1) * 8)
                group[place] = group[place] + block[rows, left:left + 128] * dual
        duals.append(lane_sums(jnp.concatenate(group)))
    return cols[1, here, :] - cols[0, here, :] * jnp.concatenate(duals)


def by_cols(block, column):
    tall, wide = block.shape
    sums = [jnp.zeros((8, 128), F32) for _ in range(wide // 128)]
    for top in range(0, tall, 8):
        dual = column[top:top + 8, :]
        for place in range(wide // 128):
            sums[place] = sums[place] + block[top:top + 8, place * 128:(place + 1) * 128] * dual
    return jnp.concatenate(sums, 1)


def chunk(index):
    return pl.ds(pl.multiple_of(index * STEP, STEP), STEP)


def sweep_kernel(opening, shares, plan, cols, *refs):
    if opening:
        parts, (_, _, sums_out, part_out, spread, total) = refs[:shares], refs[shares:]
        sums_out[...] = added(parts)
        row_dual = sums_out[1:2, :] / sums_out[0:1, :]
    else:
        (sums, *parts), (_, _, part_out, spread, total) = refs[:shares + 1], refs[shares + 1:]
        row_dual = (sums[1:2, :] - added(parts)) / sums[0:1, :]
    spread[...] = jnp.broadcast_to(row_dual, spread.shape)
    total[...] = jnp.zeros_like(total)
    steps = plan.shape[0] // STEP

    def duals(index):
        here = chunk(index)
        return by_rows(plan.at[here, :], cols, here, spread)

    def step(index, dual):
        product = by_cols(plan.at[chunk(index - 1), :], dual)
        dual = duals(index)
        total[...] += product
        return dual

    last = lax.fori_loop(1, steps, step, duals(0), unroll=True)
    total[...] += by_cols(plan.at[chunk(steps - 1), :], last)
    part_out[...] = jnp.sum(total[...], axis=0, keepdims=True)


def embed_before_kernel(logit_scale, protos, emb_a, emb_b, after, entry_out, token):
    del after
    scale = logit_scale * LOG2E
    token[...] = jnp.zeros_like(token)
    rows = entry_out.shape[1] // 2

    def step(index, carry):
        here = chunk(index)
        for half, emb in enumerate((emb_a, emb_b)):
            entry = jnp.exp2(scale * mm(protos[here, :], emb[:, 0:rows]))
            entry_out[here, half * rows:(half + 1) * rows] = logit_scale * entry
        return carry

    lax.fori_loop(0, protos.shape[0] // STEP, step, 0)


def cotangent_kernel(view_scale, block, ids, protos, view_a, view_b, after, cot_out, token):
    del after
    width = view_a.shape[0]
    tall, wide = cot_out.shape
    token[...] = jnp.zeros_like(token)
    first = pl.multiple_of(block(ids) * tall, tall)

    def step(index, carry):
        here = chunk(index)
        from_row = pl.ds(pl.multiple_of(first + index * STEP, STEP), STEP)
        for half, view in enumerate((view_a, view_b)):
            cot = mm(protos[from_row, 0:width], view[:, 0:wide // 2])
            cot_out[here, half * wide // 2:(half + 1) * wide // 2] = -view_scale * cot
        return carry

    lax.fori_loop(0, tall // STEP, step, 0)


def embed_kernel(shares, ids, plan, cols, sums, protos_t, entries, cots, *refs):
    parts, (_, duals_out, rows_out, keep, give, spread, whole) = refs[:shares], refs[shares:]
    width = protos_t.shape[0]
    rows = entries.shape[1]
    rows_out[...] = (sums[1:2, :] - added(parts)) / sums[0:1, :]
    spread[...] = jnp.broadcast_to(rows_out[...], spread.shape)
    split = rows_out.shape[1] // 2
    own_dual = jnp.concatenate((rows_out[:, 0:rows // 2], rows_out[:, split:split + rows // 2]), 1)

    def duals(index, carry):
        here = chunk(index)
        duals_out[here, :] = by_rows(plan.at[here, :], cols, here, spread)
        return carry

    lax.fori_loop(0, plan.shape[0] // STEP, duals, 0, unroll=2)
    total = jnp.zeros((width, rows), F32)
    for start in range(0, plan.shape[0], CHUNK):
        here = slice(start, start + CHUNK)
        grad = entries[here, :] * (cots[here, :] - own_dual - widened(duals_out[here, :], rows))
        total = total + mm(protos_t[:, here], grad.astype(BF16))
    whole[...] = jnp.transpose(total)
    tall = keep.shape[1]
    for place in range(shares):
        above, beside = divmod(place, shares // 2)
        to = above * shares + (ids[1] ^ (2 * beside))
        keep[place] = whole[pl.ds(pl.multiple_of(to * tall, tall), tall), :]
        give[place] = whole[pl.ds(pl.multiple_of((to ^ 1) * tall, tall), tall), :]


def proto_before_kernel(logit_scale, view_scale, ids, protos, emb_a, emb_b, view_a, view_b, after, entry_out, second_out, token):
    del after
    own, rows = entry_out.shape
    width = second_out.shape[1]
    scale = logit_scale * LOG2E
    token[...] = jnp.zeros_like(token)
    here = pl.ds(pl.multiple_of((ids[0] >> 1) * own, own), own)
    total = jnp.zeros((own, width), F32)
    for left, emb, view in ((0, emb_a, view_a), (rows // 2, emb_b, view_b)):
        for start in range(0, rows // 2, 2 * width):
            cols = slice(start, start + 2 * width)
            exact = jnp.exp2(scale * mm(protos[here, :], emb[:, cols]))
            entry_out[:, left + start:left + start + 2 * width] = logit_scale * exact
            total = total + mm((-view_scale * exact).astype(BF16), view[:, cols], NT)
    second_out[...] = total


def proto_kernel(half, ids, emb_ext, entries, cots, so_far, col_dual, row_dual, *outs):
    own, width = outs[0].shape
    here = pl.ds(pl.multiple_of((ids[0] >> 1) * own, own), own)
    column = widened(col_dual[here, :], 2 * width)
    total = so_far[...]
    some = entries.shape[1] // 2
    for start in range(0, some, 2 * width):
        cols = slice(half * some + start, half * some + start + 2 * width)
        grad = entries[:, cols] * (cots[:, cols] - row_dual[:, cols] - column)
        total = total + mm(grad.astype(BF16), emb_ext[0:width, start:start + 2 * width], NT)
    outs[0][...] = total
    for token in outs[1:]:
        token[...] = jnp.zeros_like(token)


def call(kernel, out_shape, name, scalars=0, scratch=(), aliases=None, limit=16):
    def run(*args):
        whole = pl.BlockSpec(memory_space=pltpu.VMEM)
        small = pl.BlockSpec(memory_space=pltpu.SMEM)
        return pl.pallas_call(
            kernel,
            out_shape=out_shape,
            in_specs=[small] * scalars + [whole] * (len(args) - scalars),
            out_specs=jax.tree.map(lambda _: whole, out_shape),
            scratch_shapes=[pltpu.VMEM(dims, dtype) for dtype, *dims in scratch],
            input_output_aliases=aliases or {},
            compiler_params=pltpu.CompilerParams(vmem_limit_bytes=limit << 20),
            name=name,
        )(*args)

    return run


def swap_both(value, above, beside):
    shares = lax.axis_size("proto")
    pairs = [
        (row * shares + col, (row ^ above) * shares + (col ^ beside))
        for row in range(lax.axis_size("row"))
        for col in range(shares)
    ]
    return lax.ppermute(value, ("row", "proto"), pairs)


def others():
    shares = lax.axis_size("proto")
    return [(above, beside) for above in range(2) for beside in range(0, shares, 2)]


def exchange(part):
    near = call(add_kernel, jax.ShapeDtypeStruct(part.shape, F32), "add", limit=2)(part, swap(part, "proto", 1))
    return [near if pair == (0, 0) else swap_both(near, *pair) for pair in others()]


def kept_plan(embeddings, second_view, prototypes, row_scale, col_scale):
    rows, width = embeddings.shape
    blocks, shares = lax.axis_size("row"), lax.axis_size("proto")
    all_rows = rows * blocks
    count = prototypes.shape[0] // 2
    own = 2 * count // blocks
    ids = jnp.stack((lax.axis_index("row"), lax.axis_index("proto")))
    scales = (1.0 / (0.05 * width), 1.0 / (0.1 * width))
    log_mass = math.log(64.0 * prototypes.shape[0] * shares)
    shape = lambda *dims, dtype=F32: jax.ShapeDtypeStruct(dims, dtype)
    form = lambda kernel: functools.partial(kernel, *scales)
    there = lambda value: pltpu.with_memory_space_constraint(value, pltpu.HBM)
    row_scale = row_scale.reshape(1, rows)
    col_scale = col_scale.reshape(1, 2 * count)
    half = shape(width + EXT, rows, dtype=BF16)
    send = call(functools.partial(prep_kernel, scales[0]), half, "prepare", scalars=1)(
        ids, there(embeddings), there(second_view), there(row_scale)
    )
    protos, protos_t, token = call(
        functools.partial(turn_kernel, scales[0], log_mass),
        (shape(count, 2 * width, dtype=BF16), shape(width, count, dtype=BF16), shape(8, 128)),
        "turn",
        scalars=1,
        limit=4,
    )(ids, there(prototypes), there(col_scale))
    pairs = blocks // 2
    stack = call(functools.partial(stack_kernel, pairs), shape(pairs, width + EXT, rows, dtype=BF16), "stack", limit=2)
    direct = [send] + [swap(send, "row", step) for step in range(2, blocks, 2)]
    mine_a = stack(*direct, token)
    theirs_a = swap(mine_a, "proto", 1)
    mine_b = stack(*[swap(value, "row", 1) for value in direct])
    theirs_b = swap(mine_b, "proto", 1)

    kept = pltpu.VMEM((count, all_rows), F32)
    some = all_rows // 2
    turned = (shape(2 * width, some, dtype=BF16), shape(width, some, dtype=BF16))
    work = [(F32, 8, some), (F32, 8, some)]
    plan, cols, sums, emb_a, view_a = call(
        functools.partial(plan_kernel, *scales, False),
        (kept, shape(2, count, 128), shape(2, some)) + turned,
        "plan_ours",
        scalars=1,
        scratch=work,
        limit=12,
    )(ids, protos, mine_a, theirs_a)
    plan, cols, sums, emb_b, view_b = call(
        functools.partial(plan_kernel, *scales, True),
        (kept, shape(2, count, 128), shape(2, all_rows)) + turned,
        "plan_theirs",
        scalars=1,
        scratch=work,
        aliases={4: 0},
        limit=12,
    )(ids, protos, mine_b, theirs_b, plan, cols, sums)

    work = [(F32, 8, all_rows), (F32, 8, all_rows)]
    token = shape(8, 128)
    parts = exchange(sums)
    entries, done = call(
        functools.partial(embed_before_kernel, scales[0]),
        (shape(count, 2 * rows), token),
        "embed_before",
        limit=6,
    )(protos, emb_a, emb_b, parts[0])
    plan, sums, part = call(
        functools.partial(sweep_kernel, True, shares),
        (kept, shape(2, all_rows), shape(1, all_rows)),
        "sweep",
        scratch=work,
        aliases={0: 0},
        limit=4,
    )(plan, cols, *parts, done)
    cotangent = lambda dims, block: call(
        functools.partial(cotangent_kernel, scales[1], block), (shape(*dims), token), "cotangent", scalars=1, limit=4
    )
    for sweep in range(ITERS - 2):
        parts = exchange(part)
        if sweep == ITERS - 3:
            cots, done = cotangent((count, 2 * rows), lambda ids: 0)(ids, protos, view_a, view_b, parts[0])
        if sweep == 0:
            own_entries, second, done = call(
                form(proto_before_kernel),
                (shape(own, all_rows), shape(own, width), token),
                "proto_before",
                scalars=1,
                limit=6,
            )(ids, protos, emb_a, emb_b, view_a, view_b, parts[0])
        plan, part = call(
            functools.partial(sweep_kernel, False, shares),
            (kept, shape(1, all_rows)),
            "sweep",
            scratch=work,
            aliases={0: 0},
            limit=4,
        )(plan, cols, sums, *parts, done)
    parts = exchange(part)
    own_cots, done = cotangent((own, all_rows), lambda ids: ids[0] >> 1)(ids, protos, view_a, view_b, parts[0])
    pieces = shape(shares, rows // shares, width)
    col_dual, row_dual, keep, give = call(
        functools.partial(embed_kernel, shares),
        (shape(count, 128), shape(1, all_rows), pieces, pieces),
        "embed_grad",
        scalars=1,
        scratch=work[:1] + [(F32, 2 * rows, width)],
        limit=8,
    )(ids, plan, cols, sums, protos_t, entries, cots, *parts, done)
    half = lambda number, outs: call(functools.partial(proto_kernel, number), outs, "proto_grad", scalars=1, limit=6)
    second, done = half(0, (shape(own, width), token))(ids, emb_a, own_entries, own_cots, second, col_dual, row_dual)
    near = call(add_kernel, pieces, "add", limit=2)(keep, swap(give, "proto", 1), done)
    embed_grad = near[0]
    for place, pair in list(enumerate(others()))[1:]:
        embed_grad = embed_grad + swap_both(near[place], *pair)
    proto_grad = half(1, (shape(own, width),))(ids, emb_b, own_entries, own_cots, second, col_dual, row_dual)[0]
    return embed_grad, proto_grad


def contract_rows(left, right):
    return mm(left, right, (((0,), (0,)), ((), ())))


def contract_width(left, right):
    return mm(left, right, NT)


def sum_over(value, axis):
    size = lax.axis_size(axis)
    parts = [value] + [swap(value, axis, step) for step in range(1, size)]
    return sum(parts[1:], parts[0])


def scatter_sum(value, axis):
    size = lax.axis_size(axis)
    me = lax.axis_index(axis)
    rows = value.shape[0] // size
    block = lambda owner: lax.dynamic_slice_in_dim(value, owner * rows, rows, 0)
    total = block(me)
    for step in range(1, size):
        total = total + swap(block(me ^ step), axis, step)
    return total


def split_plan(embeddings, second_view, prototypes, row_scale, col_scale):
    feat_width = embeddings.shape[1]
    proto_count = prototypes.shape[0]
    logit_scale = 1.0 / (0.05 * feat_width)
    view_scale = 1.0 / (0.1 * feat_width)
    plan_mass = 64.0 * proto_count * lax.axis_size("proto")

    logits = contract_width(embeddings, prototypes) * logit_scale
    plan = row_scale[:, None] * col_scale[None, :] * jnp.exp(logits) / plan_mass
    cotangent = -contract_width(second_view, prototypes) * view_scale
    weighted = plan * cotangent

    row_mass, row_weight = sum_over(jnp.stack((plan.sum(1), weighted.sum(1))), "proto")
    row_dual = row_weight / row_mass
    sums = jnp.stack((plan.sum(0), weighted.sum(0), (row_dual[:, None] * plan).sum(0)))
    col_mass, col_weight, product = sum_over(sums, "row")
    col_dual = (col_weight - product) / col_mass
    for sweep in range(ITERS - 1):
        product = sum_over((plan * col_dual[None, :]).sum(1), "proto")
        row_dual = (row_weight - product) / row_mass
        product = sum_over((plan * row_dual[:, None]).sum(0), "row")
        col_dual = (col_weight - product) / col_mass
    logit_grad = plan * (cotangent - row_dual[:, None] - col_dual[None, :])
    scaled_grad = (logit_scale * logit_grad).astype(jnp.bfloat16)
    scaled_plan = (-view_scale * plan).astype(jnp.bfloat16)
    embed_grad = scatter_sum(
        jnp.dot(scaled_grad, prototypes, preferred_element_type=jnp.float32), "proto"
    )
    proto_grad = scatter_sum(
        contract_rows(scaled_grad, embeddings) + contract_rows(scaled_plan, second_view), "row"
    )
    return (embed_grad, proto_grad)


def per_device(embeddings, second_view, prototypes, row_scale, col_scale):
    blocks, shares = lax.axis_size("row"), lax.axis_size("proto")
    rows, width = embeddings.shape
    count = prototypes.shape[0]
    fits = rows * blocks * count * 2 <= PLAN_BYTES
    even = all(n & (n - 1) == 0 and n > 1 for n in (blocks, shares))
    even = even and rows % (16 * shares) == 0 and rows % width == 0
    tiled = rows % 128 == 0 and width % 128 == 0 and count == blocks * CHUNK and blocks % 4 == 0
    form = kept_plan if fits and even and tiled else split_plan
    return form(embeddings, second_view, prototypes, row_scale, col_scale)


def solution(mesh):
    return jax.shard_map(
        per_device,
        mesh=mesh,
        in_specs=(P("row", None), P("row", None), P("proto", None), P("row"), P("proto")),
        out_specs=(P(("row", "proto"), None), P(("proto", "row"), None)),
        check_vma=False,
    )
```

```python
import functools
import math

import jax
import jax.numpy as jnp
from jax import lax
from jax.experimental import pallas as pl
from jax.experimental.pallas import tpu as pltpu
from jax.sharding import PartitionSpec as P

ITERS = 4
CHUNK = 512
STEP = 256
EXT = 16
PLAN_BYTES = 24 << 20
LOG2E = 1.4426950408889634
F32, BF16 = jnp.float32, jnp.bfloat16
NT = (((1,), (1,)), ((), ()))
NN = (((1,), (0,)), ((), ()))


def mm(left, right, dims=NN):
    return lax.dot_general(left, right, dims, preferred_element_type=F32)


def swap(value, axis, step):
    size = lax.axis_size(axis)
    return lax.ppermute(value, axis, [(i, i ^ step) for i in range(size)])


def lane_sums(block):
    return jnp.broadcast_to(jnp.sum(block, axis=1, keepdims=True), (block.shape[0], 128))


def widened(column, width):
    return jnp.concatenate([column] * (width // 128), 1)


def rows_of(pieces, height=EXT):
    index = lax.broadcasted_iota(jnp.int32, (height, pieces[0].shape[1]), 0)
    total = jnp.zeros(index.shape, F32)
    for place, piece in enumerate(pieces):
        total = jnp.where(index == place, piece, total)
    return total


def pieces_of(row):
    out = []
    for _ in range(3):
        out.append(row.astype(BF16).astype(F32))
        row = row - out[-1]
    return out, [jnp.ones_like(row)] * 3


def prep_kernel(logit_scale, ids, embeddings, second_view, row_scale, send_out):
    rows, width = embeddings.shape

    @pl.when(ids[1] & 1 == 0)
    def _():
        logs, ones = pieces_of(jnp.log(row_scale[...]) / logit_scale)
        send_out[0:width, :] = jnp.transpose(embeddings[...].astype(F32)).astype(BF16)
        send_out[width:width + EXT, :] = rows_of(logs + ones).astype(BF16)

    @pl.when(ids[1] & 1 != 0)
    def _():
        send_out[0:width, :] = jnp.transpose(second_view[...].astype(F32)).astype(BF16)
        send_out[width:width + EXT, :] = jnp.zeros((EXT, rows), BF16)


def turn_kernel(logit_scale, log_mass, ids, protos, col_scale, protos_out, protos_t, token):
    count = protos_out.shape[0]
    width = protos.shape[1]
    token[...] = jnp.zeros_like(token)

    def step(index, carry):
        here = pl.ds(pl.multiple_of(index * CHUNK, CHUNK), CHUNK)
        there = pl.ds(pl.multiple_of((2 * index + (ids[0] & 1)) * CHUNK, CHUNK), CHUNK)
        block = protos[there, :]
        logs, ones = pieces_of((jnp.log(col_scale[:, there]) - log_mass) / logit_scale)
        protos_out[here, 0:width] = block
        protos_out[here, width:] = jnp.transpose(rows_of(ones + logs, width)).astype(BF16)
        protos_t[:, here] = jnp.transpose(block.astype(F32)).astype(BF16)
        return carry

    lax.fori_loop(0, count // CHUNK, step, 0)


def stack_kernel(count, *refs):
    for place in range(count):
        refs[-1][place] = refs[place][...]


def add_kernel(left, right, *refs):
    refs[-1][...] = left[...] + right[...]


def plan_kernel(logit_scale, view_scale, second, ids, protos, mine, theirs, *refs):
    if second:
        _, cols_in, sums_in, *refs = refs
    plan_out, cols_out, sums_out, emb_ext, view_t, row_mass, row_weight = refs
    blocks, high, rows = mine.shape
    count = protos.shape[0]
    width = view_t.shape[0]
    scale = logit_scale * LOG2E
    left = blocks * rows if second else 0
    emb_ext[high:, :] = jnp.zeros((emb_ext.shape[0] - high, blocks * rows), BF16)

    def fill(emb, view):
        for block in range(blocks):
            cols = slice(block * rows, (block + 1) * rows)
            emb_ext[0:high, cols] = emb[block]
            view_t[:, cols] = view[block, 0:width, :]

    pl.when(ids[1] & 1 == 0)(lambda: fill(mine, theirs))
    pl.when(ids[1] & 1 != 0)(lambda: fill(theirs, mine))
    row_mass[...] = jnp.zeros_like(row_mass)
    row_weight[...] = jnp.zeros_like(row_weight)

    def folded(block):
        tiles = [block[:, left:left + 128] for left in range(0, block.shape[1], 128)]
        across = tiles[0]
        for tile in tiles[1:]:
            across = across + tile
        return across, jnp.sum(block.reshape(block.shape[0] // 8, 8, block.shape[1]), axis=0)

    def step(index, carry):
        here = pl.ds(pl.multiple_of(index * CHUNK, CHUNK), CHUNK)
        mass = cols_in[0, here, :] if second else jnp.zeros((CHUNK, 128), F32)
        weight = cols_in[1, here, :] if second else mass
        for block in range(blocks):
            cols = slice(block * rows, (block + 1) * rows)
            plan = jnp.exp2(scale * mm(protos[here, :], emb_ext[:, cols]))
            plan_out[here, left + block * rows:left + (block + 1) * rows] = plan
            across, down = folded(plan)
            mass = mass + across
            row_mass[:, cols] += down
            across, down = folded(plan * mm(protos[here, 0:width], view_t[:, cols]))
            weight = weight + across
            row_weight[:, cols] += down
        if second:
            mass = 1.0 / lane_sums(mass)
            weight = -view_scale * lane_sums(weight) * mass
        cols_out[0, here, :] = mass
        cols_out[1, here, :] = weight
        return carry

    lax.fori_loop(0, count // CHUNK, step, 0, unroll=True)
    if second:
        sums_out[:, 0:left] = sums_in[...]
    sums_out[0:1, left:] = jnp.sum(row_mass[...], axis=0, keepdims=True)
    sums_out[1:2, left:] = -view_scale * jnp.sum(row_weight[...], axis=0, keepdims=True)


def added(parts):
    turned, plain = parts[:len(parts) // 2], parts[len(parts) // 2:]
    total, other = plain[0][...], turned[0][...]
    for part in plain[1:]:
        total = total + part[...]
    for part in turned[1:]:
        other = other + part[...]
    half = other.shape[1] // 2
    return total + jnp.concatenate((other[:, half:], other[:, :half]), 1)


def by_rows(block, cols, here, spread):
    tall, wide = block.shape
    duals = []
    for top in range(0, tall, 64):
        group = [jnp.zeros((8, 128), F32) for _ in range(8)]
        for left in range(0, wide, 128):
            dual = spread[:, left:left + 128]
            for place in range(8):
                rows = slice(top + place * 8, top + (place + 1) * 8)
                group[place] = group[place] + block[rows, left:left + 128] * dual
        duals.append(lane_sums(jnp.concatenate(group)))
    return cols[1, here, :] - cols[0, here, :] * jnp.concatenate(duals)


def by_cols(block, column):
    tall, wide = block.shape
    sums = [jnp.zeros((8, 128), F32) for _ in range(wide // 128)]
    for top in range(0, tall, 8):
        dual = column[top:top + 8, :]
        for place in range(wide // 128):
            sums[place] = sums[place] + block[top:top + 8, place * 128:(place + 1) * 128] * dual
    return jnp.concatenate(sums, 1)


def chunk(index):
    return pl.ds(pl.multiple_of(index * STEP, STEP), STEP)


def sweep_kernel(opening, shares, plan, cols, *refs):
    if opening:
        parts, (_, _, sums_out, part_out, spread, total) = refs[:shares], refs[shares:]
        sums_out[...] = added(parts)
        row_dual = sums_out[1:2, :] / sums_out[0:1, :]
    else:
        (sums, *parts), (_, _, part_out, spread, total) = refs[:shares + 1], refs[shares + 1:]
        row_dual = (sums[1:2, :] - added(parts)) / sums[0:1, :]
    spread[...] = jnp.broadcast_to(row_dual, spread.shape)
    total[...] = jnp.zeros_like(total)
    steps = plan.shape[0] // STEP

    def duals(index):
        here = chunk(index)
        return by_rows(plan.at[here, :], cols, here, spread)

    def step(index, dual):
        product = by_cols(plan.at[chunk(index - 1), :], dual)
        dual = duals(index)
        total[...] += product
        return dual

    last = lax.fori_loop(1, steps, step, duals(0), unroll=True)
    total[...] += by_cols(plan.at[chunk(steps - 1), :], last)
    part_out[...] = jnp.sum(total[...], axis=0, keepdims=True)


def embed_before_kernel(logit_scale, protos, emb_a, emb_b, after, entry_out, token):
    del after
    scale = logit_scale * LOG2E
    token[...] = jnp.zeros_like(token)
    rows = entry_out.shape[1] // 2

    def step(index, carry):
        here = chunk(index)
        for half, emb in enumerate((emb_a, emb_b)):
            entry = jnp.exp2(scale * mm(protos[here, :], emb[:, 0:rows]))
            entry_out[here, half * rows:(half + 1) * rows] = logit_scale * entry
        return carry

    lax.fori_loop(0, protos.shape[0] // STEP, step, 0)


def cotangent_kernel(view_scale, block, ids, protos, view_a, view_b, after, cot_out, token):
    del after
    width = view_a.shape[0]
    tall, wide = cot_out.shape
    token[...] = jnp.zeros_like(token)
    first = pl.multiple_of(block(ids) * tall, tall)

    def step(index, carry):
        here = chunk(index)
        from_row = pl.ds(pl.multiple_of(first + index * STEP, STEP), STEP)
        for half, view in enumerate((view_a, view_b)):
            cot = mm(protos[from_row, 0:width], view[:, 0:wide // 2])
            cot_out[here, half * wide // 2:(half + 1) * wide // 2] = -view_scale * cot
        return carry

    lax.fori_loop(0, tall // STEP, step, 0)


def embed_kernel(shares, ids, plan, cols, sums, protos_t, entries, cots, *refs):
    parts, (_, duals_out, rows_out, keep, give, spread, whole) = refs[:shares], refs[shares:]
    width = protos_t.shape[0]
    rows = entries.shape[1]
    rows_out[...] = (sums[1:2, :] - added(parts)) / sums[0:1, :]
    spread[...] = jnp.broadcast_to(rows_out[...], spread.shape)
    split = rows_out.shape[1] // 2
    own_dual = jnp.concatenate((rows_out[:, 0:rows // 2], rows_out[:, split:split + rows // 2]), 1)

    def duals(index, carry):
        here = chunk(index)
        duals_out[here, :] = by_rows(plan.at[here, :], cols, here, spread)
        return carry

    lax.fori_loop(0, plan.shape[0] // STEP, duals, 0, unroll=4)
    total = jnp.zeros((width, rows), F32)
    for start in range(0, plan.shape[0], CHUNK):
        here = slice(start, start + CHUNK)
        grad = entries[here, :] * (cots[here, :] - own_dual - widened(duals_out[here, :], rows))
        total = total + mm(protos_t[:, here], grad.astype(BF16))
    whole[...] = jnp.transpose(total)
    tall = keep.shape[1]
    for place in range(shares):
        above, beside = divmod(place, shares // 2)
        to = above * shares + (ids[1] ^ (2 * beside))
        keep[place] = whole[pl.ds(pl.multiple_of(to * tall, tall), tall), :]
        give[place] = whole[pl.ds(pl.multiple_of((to ^ 1) * tall, tall), tall), :]


def proto_before_kernel(logit_scale, view_scale, ids, protos, emb_a, emb_b, view_a, view_b, after, entry_out, second_out, token):
    del after
    own, rows = entry_out.shape
    width = second_out.shape[1]
    scale = logit_scale * LOG2E
    token[...] = jnp.zeros_like(token)
    here = pl.ds(pl.multiple_of((ids[0] >> 1) * own, own), own)
    total = jnp.zeros((own, width), F32)
    for left, emb, view in ((0, emb_a, view_a), (rows // 2, emb_b, view_b)):
        for start in range(0, rows // 2, 2 * width):
            cols = slice(start, start + 2 * width)
            exact = jnp.exp2(scale * mm(protos[here, :], emb[:, cols]))
            entry_out[:, left + start:left + start + 2 * width] = logit_scale * exact
            total = total + mm((-view_scale * exact).astype(BF16), view[:, cols], NT)
    second_out[...] = total


def proto_kernel(half, ids, emb_ext, entries, cots, so_far, col_dual, row_dual, *outs):
    own, width = outs[0].shape
    here = pl.ds(pl.multiple_of((ids[0] >> 1) * own, own), own)
    column = widened(col_dual[here, :], 2 * width)
    total = so_far[...]
    some = entries.shape[1] // 2
    for start in range(0, some, 2 * width):
        cols = slice(half * some + start, half * some + start + 2 * width)
        grad = entries[:, cols] * (cots[:, cols] - row_dual[:, cols] - column)
        total = total + mm(grad.astype(BF16), emb_ext[0:width, start:start + 2 * width], NT)
    outs[0][...] = total
    for token in outs[1:]:
        token[...] = jnp.zeros_like(token)


def call(kernel, out_shape, name, scalars=0, scratch=(), aliases=None, limit=16):
    def run(*args):
        whole = pl.BlockSpec(memory_space=pltpu.VMEM)
        small = pl.BlockSpec(memory_space=pltpu.SMEM)
        return pl.pallas_call(
            kernel,
            out_shape=out_shape,
            in_specs=[small] * scalars + [whole] * (len(args) - scalars),
            out_specs=jax.tree.map(lambda _: whole, out_shape),
            scratch_shapes=[pltpu.VMEM(dims, dtype) for dtype, *dims in scratch],
            input_output_aliases=aliases or {},
            compiler_params=pltpu.CompilerParams(vmem_limit_bytes=limit << 20),
            name=name,
        )(*args)

    return run


def swap_both(value, above, beside):
    shares = lax.axis_size("proto")
    pairs = [
        (row * shares + col, (row ^ above) * shares + (col ^ beside))
        for row in range(lax.axis_size("row"))
        for col in range(shares)
    ]
    return lax.ppermute(value, ("row", "proto"), pairs)


def others():
    shares = lax.axis_size("proto")
    return [(above, beside) for above in range(2) for beside in range(0, shares, 2)]


def exchange(part):
    near = call(add_kernel, jax.ShapeDtypeStruct(part.shape, F32), "add", limit=2)(part, swap(part, "proto", 1))
    return near, [near if pair == (0, 0) else swap_both(near, *pair) for pair in reversed(others())]


def kept_plan(embeddings, second_view, prototypes, row_scale, col_scale):
    rows, width = embeddings.shape
    blocks, shares = lax.axis_size("row"), lax.axis_size("proto")
    all_rows = rows * blocks
    count = prototypes.shape[0] // 2
    own = 2 * count // blocks
    ids = jnp.stack((lax.axis_index("row"), lax.axis_index("proto")))
    scales = (1.0 / (0.05 * width), 1.0 / (0.1 * width))
    log_mass = math.log(64.0 * prototypes.shape[0] * shares)
    shape = lambda *dims, dtype=F32: jax.ShapeDtypeStruct(dims, dtype)
    form = lambda kernel: functools.partial(kernel, *scales)
    there = lambda value: pltpu.with_memory_space_constraint(value, pltpu.HBM)
    row_scale = row_scale.reshape(1, rows)
    col_scale = col_scale.reshape(1, 2 * count)
    half = shape(width + EXT, rows, dtype=BF16)
    send = call(functools.partial(prep_kernel, scales[0]), half, "prepare", scalars=1)(
        ids, there(embeddings), there(second_view), there(row_scale)
    )
    protos, protos_t, token = call(
        functools.partial(turn_kernel, scales[0], log_mass),
        (shape(count, 2 * width, dtype=BF16), shape(width, count, dtype=BF16), shape(8, 128)),
        "turn",
        scalars=1,
        limit=4,
    )(ids, there(prototypes), there(col_scale))
    pairs = blocks // 2
    stack = call(functools.partial(stack_kernel, pairs), shape(pairs, width + EXT, rows, dtype=BF16), "stack", limit=2)
    direct = [send] + [swap(send, "row", step) for step in range(2, blocks, 2)]
    mine_a = stack(*direct, token)
    theirs_a = swap(mine_a, "proto", 1)
    mine_b = stack(*[swap(value, "row", 1) for value in direct])
    theirs_b = swap(mine_b, "proto", 1)

    kept = pltpu.VMEM((count, all_rows), F32)
    some = all_rows // 2
    turned = (shape(2 * width, some, dtype=BF16), shape(width, some, dtype=BF16))
    work = [(F32, 8, some), (F32, 8, some)]
    plan, cols, sums, emb_a, view_a = call(
        functools.partial(plan_kernel, *scales, False),
        (kept, shape(2, count, 128), shape(2, some)) + turned,
        "plan_ours",
        scalars=1,
        scratch=work,
        limit=12,
    )(ids, protos, mine_a, theirs_a)
    plan, cols, sums, emb_b, view_b = call(
        functools.partial(plan_kernel, *scales, True),
        (kept, shape(2, count, 128), shape(2, all_rows)) + turned,
        "plan_theirs",
        scalars=1,
        scratch=work,
        aliases={4: 0},
        limit=12,
    )(ids, protos, mine_b, theirs_b, plan, cols, sums)

    work = [(F32, 8, all_rows), (F32, 8, all_rows)]
    token = shape(8, 128)
    near, parts = exchange(sums)
    entries, done = call(
        functools.partial(embed_before_kernel, scales[0]),
        (shape(count, 2 * rows), token),
        "embed_before",
        limit=6,
    )(protos, emb_a, emb_b, near)
    plan, sums, part = call(
        functools.partial(sweep_kernel, True, shares),
        (kept, shape(2, all_rows), shape(1, all_rows)),
        "sweep",
        scratch=work,
        aliases={0: 0},
        limit=4,
    )(plan, cols, *parts, done)
    cotangent = lambda dims, block: call(
        functools.partial(cotangent_kernel, scales[1], block), (shape(*dims), token), "cotangent", scalars=1, limit=4
    )
    for sweep in range(ITERS - 2):
        near, parts = exchange(part)
        if sweep == ITERS - 3:
            cots, done = cotangent((count, 2 * rows), lambda ids: 0)(ids, protos, view_a, view_b, near)
        if sweep == 0:
            own_entries, second, done = call(
                form(proto_before_kernel),
                (shape(own, all_rows), shape(own, width), token),
                "proto_before",
                scalars=1,
                limit=6,
            )(ids, protos, emb_a, emb_b, view_a, view_b, near)
        plan, part = call(
            functools.partial(sweep_kernel, False, shares),
            (kept, shape(1, all_rows)),
            "sweep",
            scratch=work,
            aliases={0: 0},
            limit=4,
        )(plan, cols, sums, *parts, done)
    near, parts = exchange(part)
    own_cots, done = cotangent((own, all_rows), lambda ids: ids[0] >> 1)(ids, protos, view_a, view_b, near)
    pieces = shape(shares, rows // shares, width)
    col_dual, row_dual, keep, give = call(
        functools.partial(embed_kernel, shares),
        (shape(count, 128), shape(1, all_rows), pieces, pieces),
        "embed_grad",
        scalars=1,
        scratch=work[:1] + [(F32, 2 * rows, width)],
        limit=8,
    )(ids, plan, cols, sums, protos_t, entries, cots, *parts, done)
    half = lambda number, outs: call(functools.partial(proto_kernel, number), outs, "proto_grad", scalars=1, limit=6)
    second, done = half(0, (shape(own, width), token))(ids, emb_a, own_entries, own_cots, second, col_dual, row_dual)
    near = call(add_kernel, pieces, "add", limit=2)(keep, swap(give, "proto", 1), done)
    embed_grad = near[0]
    for place, pair in reversed(list(enumerate(others()))[1:]):
        embed_grad = embed_grad + swap_both(near[place], *pair)
    proto_grad = half(1, (shape(own, width),))(ids, emb_b, own_entries, own_cots, second, col_dual, row_dual)[0]
    return embed_grad, proto_grad


def contract_rows(left, right):
    return mm(left, right, (((0,), (0,)), ((), ())))


def contract_width(left, right):
    return mm(left, right, NT)


def sum_over(value, axis):
    size = lax.axis_size(axis)
    parts = [value] + [swap(value, axis, step) for step in range(1, size)]
    return sum(parts[1:], parts[0])


def scatter_sum(value, axis):
    size = lax.axis_size(axis)
    me = lax.axis_index(axis)
    rows = value.shape[0] // size
    block = lambda owner: lax.dynamic_slice_in_dim(value, owner * rows, rows, 0)
    total = block(me)
    for step in range(1, size):
        total = total + swap(block(me ^ step), axis, step)
    return total


def split_plan(embeddings, second_view, prototypes, row_scale, col_scale):
    feat_width = embeddings.shape[1]
    proto_count = prototypes.shape[0]
    logit_scale = 1.0 / (0.05 * feat_width)
    view_scale = 1.0 / (0.1 * feat_width)
    plan_mass = 64.0 * proto_count * lax.axis_size("proto")

    logits = contract_width(embeddings, prototypes) * logit_scale
    plan = row_scale[:, None] * col_scale[None, :] * jnp.exp(logits) / plan_mass
    cotangent = -contract_width(second_view, prototypes) * view_scale
    weighted = plan * cotangent

    row_mass, row_weight = sum_over(jnp.stack((plan.sum(1), weighted.sum(1))), "proto")
    row_dual = row_weight / row_mass
    sums = jnp.stack((plan.sum(0), weighted.sum(0), (row_dual[:, None] * plan).sum(0)))
    col_mass, col_weight, product = sum_over(sums, "row")
    col_dual = (col_weight - product) / col_mass
    for sweep in range(ITERS - 1):
        product = sum_over((plan * col_dual[None, :]).sum(1), "proto")
        row_dual = (row_weight - product) / row_mass
        product = sum_over((plan * row_dual[:, None]).sum(0), "row")
        col_dual = (col_weight - product) / col_mass
    logit_grad = plan * (cotangent - row_dual[:, None] - col_dual[None, :])
    scaled_grad = (logit_scale * logit_grad).astype(jnp.bfloat16)
    scaled_plan = (-view_scale * plan).astype(jnp.bfloat16)
    embed_grad = scatter_sum(
        jnp.dot(scaled_grad, prototypes, preferred_element_type=jnp.float32), "proto"
    )
    proto_grad = scatter_sum(
        contract_rows(scaled_grad, embeddings) + contract_rows(scaled_plan, second_view), "row"
    )
    return (embed_grad, proto_grad)


def per_device(embeddings, second_view, prototypes, row_scale, col_scale):
    blocks, shares = lax.axis_size("row"), lax.axis_size("proto")
    rows, width = embeddings.shape
    count = prototypes.shape[0]
    fits = rows * blocks * count * 2 <= PLAN_BYTES
    even = all(n & (n - 1) == 0 and n > 1 for n in (blocks, shares))
    even = even and rows % (16 * shares) == 0 and rows % width == 0
    tiled = rows % 128 == 0 and width % 128 == 0 and count == blocks * CHUNK and blocks % 4 == 0
    form = kept_plan if fits and even and tiled else split_plan
    return form(embeddings, second_view, prototypes, row_scale, col_scale)


def solution(mesh):
    return jax.shard_map(
        per_device,
        mesh=mesh,
        in_specs=(P("row", None), P("row", None), P("proto", None), P("row"), P("proto")),
        out_specs=(P(("row", "proto"), None), P(("proto", "row"), None)),
        check_vma=False,
    )
```

```python
import functools
import math

import jax
import jax.numpy as jnp
from jax import lax
from jax.experimental import pallas as pl
from jax.experimental.pallas import tpu as pltpu
from jax.sharding import PartitionSpec as P

ITERS = 4
CHUNK = 512
STEP = 256
EXT = 16
PLAN_BYTES = 24 << 20
LOG2E = 1.4426950408889634
F32, BF16 = jnp.float32, jnp.bfloat16
NT = (((1,), (1,)), ((), ()))
NN = (((1,), (0,)), ((), ()))


def mm(left, right, dims=NN):
    return lax.dot_general(left, right, dims, preferred_element_type=F32)


def swap(value, axis, step):
    size = lax.axis_size(axis)
    return lax.ppermute(value, axis, [(i, i ^ step) for i in range(size)])


def lane_sums(block):
    return jnp.broadcast_to(jnp.sum(block, axis=1, keepdims=True), (block.shape[0], 128))


def widened(column, width):
    return jnp.concatenate([column] * (width // 128), 1)


def rows_of(pieces, height=EXT):
    index = lax.broadcasted_iota(jnp.int32, (height, pieces[0].shape[1]), 0)
    total = jnp.zeros(index.shape, F32)
    for place, piece in enumerate(pieces):
        total = jnp.where(index == place, piece, total)
    return total


def pieces_of(row):
    out = []
    for _ in range(3):
        out.append(row.astype(BF16).astype(F32))
        row = row - out[-1]
    return out, [jnp.ones_like(row)] * 3


def prep_kernel(logit_scale, ids, embeddings, second_view, row_scale, send_out):
    rows, width = embeddings.shape

    @pl.when(ids[1] & 1 == 0)
    def _():
        logs, ones = pieces_of(jnp.log(row_scale[...]) / logit_scale)
        send_out[0:width, :] = jnp.transpose(embeddings[...].astype(F32)).astype(BF16)
        send_out[width:width + EXT, :] = rows_of(logs + ones).astype(BF16)

    @pl.when(ids[1] & 1 != 0)
    def _():
        send_out[0:width, :] = jnp.transpose(second_view[...].astype(F32)).astype(BF16)
        send_out[width:width + EXT, :] = jnp.zeros((EXT, rows), BF16)


def turn_kernel(logit_scale, log_mass, ids, protos, col_scale, protos_out, protos_t, token):
    count = protos_out.shape[0]
    width = protos.shape[1]
    token[...] = jnp.zeros_like(token)

    def step(index, carry):
        here = pl.ds(pl.multiple_of(index * CHUNK, CHUNK), CHUNK)
        there = pl.ds(pl.multiple_of((2 * index + (ids[0] & 1)) * CHUNK, CHUNK), CHUNK)
        block = protos[there, :]
        logs, ones = pieces_of((jnp.log(col_scale[:, there]) - log_mass) / logit_scale)
        protos_out[here, 0:width] = block
        protos_out[here, width:] = jnp.transpose(rows_of(ones + logs, width)).astype(BF16)
        protos_t[:, here] = jnp.transpose(block.astype(F32)).astype(BF16)
        return carry

    lax.fori_loop(0, count // CHUNK, step, 0)


def stack_kernel(count, *refs):
    for place in range(count):
        refs[-1][place] = refs[place][...]


def add_kernel(left, right, *refs):
    refs[-1][...] = left[...] + right[...]


def plan_kernel(logit_scale, view_scale, second, ids, protos, mine, theirs, *refs):
    if second:
        _, cols_in, sums_in, *refs = refs
    plan_out, cols_out, sums_out, emb_ext, view_t, row_mass, row_weight = refs
    blocks, high, rows = mine.shape
    count = protos.shape[0]
    width = view_t.shape[0]
    scale = logit_scale * LOG2E
    left = blocks * rows if second else 0
    emb_ext[high:, :] = jnp.zeros((emb_ext.shape[0] - high, blocks * rows), BF16)

    def fill(emb, view):
        for block in range(blocks):
            cols = slice(block * rows, (block + 1) * rows)
            emb_ext[0:high, cols] = emb[block]
            view_t[:, cols] = view[block, 0:width, :]

    pl.when(ids[1] & 1 == 0)(lambda: fill(mine, theirs))
    pl.when(ids[1] & 1 != 0)(lambda: fill(theirs, mine))
    row_mass[...] = jnp.zeros_like(row_mass)
    row_weight[...] = jnp.zeros_like(row_weight)

    def folded(block):
        tiles = [block[:, left:left + 128] for left in range(0, block.shape[1], 128)]
        across = tiles[0]
        for tile in tiles[1:]:
            across = across + tile
        return across, jnp.sum(block.reshape(block.shape[0] // 8, 8, block.shape[1]), axis=0)

    def step(index, carry):
        here = pl.ds(pl.multiple_of(index * CHUNK, CHUNK), CHUNK)
        mass = cols_in[0, here, :] if second else jnp.zeros((CHUNK, 128), F32)
        weight = cols_in[1, here, :] if second else mass
        for start in range(0, blocks * rows, 2 * rows):
            cols = slice(start, start + 2 * rows)
            plan = jnp.exp2(scale * mm(protos[here, :], emb_ext[:, cols]))
            plan_out[here, left + start:left + start + 2 * rows] = plan
            across, down = folded(plan)
            mass = mass + across
            row_mass[:, cols] += down
            across, down = folded(plan * mm(protos[here, 0:width], view_t[:, cols]))
            weight = weight + across
            row_weight[:, cols] += down
        if second:
            mass = 1.0 / lane_sums(mass)
            weight = -view_scale * lane_sums(weight) * mass
        cols_out[0, here, :] = mass
        cols_out[1, here, :] = weight
        return carry

    lax.fori_loop(0, count // CHUNK, step, 0, unroll=True)
    if second:
        sums_out[:, 0:left] = sums_in[...]
    sums_out[0:1, left:] = jnp.sum(row_mass[...], axis=0, keepdims=True)
    sums_out[1:2, left:] = -view_scale * jnp.sum(row_weight[...], axis=0, keepdims=True)


def added(parts):
    plain, turned = parts[:len(parts) // 2], parts[len(parts) // 2:]
    total, other = plain[0][...], turned[0][...]
    for part in plain[1:]:
        total = total + part[...]
    for part in turned[1:]:
        other = other + part[...]
    half = other.shape[1] // 2
    return total + jnp.concatenate((other[:, half:], other[:, :half]), 1)


def by_rows(block, cols, here, spread):
    tall, wide = block.shape
    duals = []
    for top in range(0, tall, 64):
        group = [jnp.zeros((8, 128), F32) for _ in range(8)]
        for left in range(0, wide, 128):
            dual = spread[:, left:left + 128]
            for place in range(8):
                rows = slice(top + place * 8, top + (place + 1) * 8)
                group[place] = group[place] + block[rows, left:left + 128] * dual
        duals.append(lane_sums(jnp.concatenate(group)))
    return cols[1, here, :] - cols[0, here, :] * jnp.concatenate(duals)


def by_cols(block, column):
    tall, wide = block.shape
    sums = [jnp.zeros((8, 128), F32) for _ in range(wide // 128)]
    for top in range(0, tall, 8):
        dual = column[top:top + 8, :]
        for place in range(wide // 128):
            sums[place] = sums[place] + block[top:top + 8, place * 128:(place + 1) * 128] * dual
    return jnp.concatenate(sums, 1)


def chunk(index):
    return pl.ds(pl.multiple_of(index * STEP, STEP), STEP)


def sweep_kernel(opening, shares, plan, cols, *refs):
    if opening:
        parts, (_, _, sums_out, part_out, spread, total) = refs[:shares], refs[shares:]
        sums_out[...] = added(parts)
        row_dual = sums_out[1:2, :] / sums_out[0:1, :]
    else:
        (sums, *parts), (_, _, part_out, spread, total) = refs[:shares + 1], refs[shares + 1:]
        row_dual = (sums[1:2, :] - added(parts)) / sums[0:1, :]
    spread[...] = jnp.broadcast_to(row_dual, spread.shape)
    total[...] = jnp.zeros_like(total)
    steps = plan.shape[0] // STEP

    def duals(index):
        here = chunk(index)
        return by_rows(plan.at[here, :], cols, here, spread)

    def step(index, dual):
        product = by_cols(plan.at[chunk(index - 1), :], dual)
        dual = duals(index)
        total[...] += product
        return dual

    last = lax.fori_loop(1, steps, step, duals(0), unroll=True)
    total[...] += by_cols(plan.at[chunk(steps - 1), :], last)
    part_out[...] = jnp.sum(total[...], axis=0, keepdims=True)


def embed_before_kernel(logit_scale, protos, emb_a, emb_b, after, entry_out, token):
    del after
    scale = logit_scale * LOG2E
    token[...] = jnp.zeros_like(token)
    rows = entry_out.shape[1] // 2

    def step(index, carry):
        here = chunk(index)
        for half, emb in enumerate((emb_a, emb_b)):
            entry = jnp.exp2(scale * mm(protos[here, :], emb[:, 0:rows]))
            entry_out[here, half * rows:(half + 1) * rows] = logit_scale * entry
        return carry

    lax.fori_loop(0, protos.shape[0] // STEP, step, 0)


def cotangent_kernel(view_scale, block, ids, protos, view_a, view_b, after, cot_out, token):
    del after
    width = view_a.shape[0]
    tall, wide = cot_out.shape
    token[...] = jnp.zeros_like(token)
    first = pl.multiple_of(block(ids) * tall, tall)

    def step(index, carry):
        here = chunk(index)
        from_row = pl.ds(pl.multiple_of(first + index * STEP, STEP), STEP)
        for half, view in enumerate((view_a, view_b)):
            cot = mm(protos[from_row, 0:width], view[:, 0:wide // 2])
            cot_out[here, half * wide // 2:(half + 1) * wide // 2] = -view_scale * cot
        return carry

    lax.fori_loop(0, tall // STEP, step, 0)


def embed_kernel(shares, ids, plan, cols, sums, protos_t, entries, cots, *refs):
    parts, (_, duals_out, rows_out, keep, give, spread, whole) = refs[:shares], refs[shares:]
    width = protos_t.shape[0]
    rows = entries.shape[1]
    rows_out[...] = (sums[1:2, :] - added(parts)) / sums[0:1, :]
    spread[...] = jnp.broadcast_to(rows_out[...], spread.shape)
    split = rows_out.shape[1] // 2
    own_dual = jnp.concatenate((rows_out[:, 0:rows // 2], rows_out[:, split:split + rows // 2]), 1)

    def duals(index, carry):
        here = chunk(index)
        duals_out[here, :] = by_rows(plan.at[here, :], cols, here, spread)
        return carry

    lax.fori_loop(0, plan.shape[0] // STEP, duals, 0, unroll=4)
    total = jnp.zeros((width, rows), F32)
    for start in range(0, plan.shape[0], CHUNK):
        here = slice(start, start + CHUNK)
        grad = entries[here, :] * (cots[here, :] - own_dual - widened(duals_out[here, :], rows))
        total = total + mm(protos_t[:, here], grad.astype(BF16))
    whole[...] = jnp.transpose(total)
    tall = keep.shape[1]
    for place in range(shares):
        above, beside = divmod(place, shares // 2)
        to = above * shares + (ids[1] ^ (2 * beside))
        keep[place] = whole[pl.ds(pl.multiple_of(to * tall, tall), tall), :]
        give[place] = whole[pl.ds(pl.multiple_of((to ^ 1) * tall, tall), tall), :]


def proto_before_kernel(logit_scale, view_scale, ids, protos, emb_a, emb_b, view_a, view_b, after, entry_out, second_out, token):
    del after
    own, rows = entry_out.shape
    width = second_out.shape[1]
    scale = logit_scale * LOG2E
    token[...] = jnp.zeros_like(token)
    here = pl.ds(pl.multiple_of((ids[0] >> 1) * own, own), own)
    total = jnp.zeros((own, width), F32)
    for left, emb, view in ((0, emb_a, view_a), (rows // 2, emb_b, view_b)):
        for start in range(0, rows // 2, 2 * width):
            cols = slice(start, start + 2 * width)
            exact = jnp.exp2(scale * mm(protos[here, :], emb[:, cols]))
            entry_out[:, left + start:left + start + 2 * width] = logit_scale * exact
            total = total + mm((-view_scale * exact).astype(BF16), view[:, cols], NT)
    second_out[...] = total


def proto_kernel(half, ids, emb_ext, entries, cots, so_far, col_dual, row_dual, *outs):
    own, width = outs[0].shape
    here = pl.ds(pl.multiple_of((ids[0] >> 1) * own, own), own)
    column = widened(col_dual[here, :], 2 * width)
    total = so_far[...]
    some = entries.shape[1] // 2
    for start in range(0, some, 2 * width):
        cols = slice(half * some + start, half * some + start + 2 * width)
        grad = entries[:, cols] * (cots[:, cols] - row_dual[:, cols] - column)
        total = total + mm(grad.astype(BF16), emb_ext[0:width, start:start + 2 * width], NT)
    outs[0][...] = total
    for token in outs[1:]:
        token[...] = jnp.zeros_like(token)


def call(kernel, out_shape, name, scalars=0, scratch=(), aliases=None, limit=16):
    def run(*args):
        whole = pl.BlockSpec(memory_space=pltpu.VMEM)
        small = pl.BlockSpec(memory_space=pltpu.SMEM)
        return pl.pallas_call(
            kernel,
            out_shape=out_shape,
            in_specs=[small] * scalars + [whole] * (len(args) - scalars),
            out_specs=jax.tree.map(lambda _: whole, out_shape),
            scratch_shapes=[pltpu.VMEM(dims, dtype) for dtype, *dims in scratch],
            input_output_aliases=aliases or {},
            compiler_params=pltpu.CompilerParams(vmem_limit_bytes=limit << 20),
            name=name,
        )(*args)

    return run


def swap_both(value, above, beside):
    shares = lax.axis_size("proto")
    pairs = [
        (row * shares + col, (row ^ above) * shares + (col ^ beside))
        for row in range(lax.axis_size("row"))
        for col in range(shares)
    ]
    return lax.ppermute(value, ("row", "proto"), pairs)


def others():
    shares = lax.axis_size("proto")
    return [(above, beside) for above in range(2) for beside in range(0, shares, 2)]


def exchange(part):
    near = call(add_kernel, jax.ShapeDtypeStruct(part.shape, F32), "add", limit=2)(part, swap(part, "proto", 1))
    return [near if pair == (0, 0) else swap_both(near, *pair) for pair in others()]


def kept_plan(embeddings, second_view, prototypes, row_scale, col_scale):
    rows, width = embeddings.shape
    blocks, shares = lax.axis_size("row"), lax.axis_size("proto")
    all_rows = rows * blocks
    count = prototypes.shape[0] // 2
    own = 2 * count // blocks
    ids = jnp.stack((lax.axis_index("row"), lax.axis_index("proto")))
    scales = (1.0 / (0.05 * width), 1.0 / (0.1 * width))
    log_mass = math.log(64.0 * prototypes.shape[0] * shares)
    shape = lambda *dims, dtype=F32: jax.ShapeDtypeStruct(dims, dtype)
    form = lambda kernel: functools.partial(kernel, *scales)
    there = lambda value: pltpu.with_memory_space_constraint(value, pltpu.HBM)
    row_scale = row_scale.reshape(1, rows)
    col_scale = col_scale.reshape(1, 2 * count)
    half = shape(width + EXT, rows, dtype=BF16)
    send = call(functools.partial(prep_kernel, scales[0]), half, "prepare", scalars=1)(
        ids, there(embeddings), there(second_view), there(row_scale)
    )
    protos, protos_t, token = call(
        functools.partial(turn_kernel, scales[0], log_mass),
        (shape(count, 2 * width, dtype=BF16), shape(width, count, dtype=BF16), shape(8, 128)),
        "turn",
        scalars=1,
        limit=4,
    )(ids, there(prototypes), there(col_scale))
    pairs = blocks // 2
    stack = call(functools.partial(stack_kernel, pairs), shape(pairs, width + EXT, rows, dtype=BF16), "stack", limit=2)
    direct = [send] + [swap(send, "row", step) for step in range(2, blocks, 2)]
    mine_a = stack(*direct, token)
    theirs_a = swap(mine_a, "proto", 1)
    mine_b = stack(*[swap(value, "row", 1) for value in direct])
    theirs_b = swap(mine_b, "proto", 1)

    kept = pltpu.VMEM((count, all_rows), F32)
    some = all_rows // 2
    turned = (shape(2 * width, some, dtype=BF16), shape(width, some, dtype=BF16))
    work = [(F32, 8, some), (F32, 8, some)]
    plan, cols, sums, emb_a, view_a = call(
        functools.partial(plan_kernel, *scales, False),
        (kept, shape(2, count, 128), shape(2, some)) + turned,
        "plan_ours",
        scalars=1,
        scratch=work,
        limit=12,
    )(ids, protos, mine_a, theirs_a)
    plan, cols, sums, emb_b, view_b = call(
        functools.partial(plan_kernel, *scales, True),
        (kept, shape(2, count, 128), shape(2, all_rows)) + turned,
        "plan_theirs",
        scalars=1,
        scratch=work,
        aliases={4: 0},
        limit=12,
    )(ids, protos, mine_b, theirs_b, plan, cols, sums)

    work = [(F32, 8, all_rows), (F32, 8, all_rows)]
    token = shape(8, 128)
    parts = exchange(sums)
    entries, done = call(
        functools.partial(embed_before_kernel, scales[0]),
        (shape(count, 2 * rows), token),
        "embed_before",
        limit=6,
    )(protos, emb_a, emb_b, parts[0])
    plan, sums, part = call(
        functools.partial(sweep_kernel, True, shares),
        (kept, shape(2, all_rows), shape(1, all_rows)),
        "sweep",
        scratch=work,
        aliases={0: 0},
        limit=4,
    )(plan, cols, *parts, done)
    cotangent = lambda dims, block: call(
        functools.partial(cotangent_kernel, scales[1], block), (shape(*dims), token), "cotangent", scalars=1, limit=4
    )
    for sweep in range(ITERS - 2):
        parts = exchange(part)
        if sweep == ITERS - 3:
            cots, done = cotangent((count, 2 * rows), lambda ids: 0)(ids, protos, view_a, view_b, parts[0])
        if sweep == 0:
            own_entries, second, done = call(
                form(proto_before_kernel),
                (shape(own, all_rows), shape(own, width), token),
                "proto_before",
                scalars=1,
                limit=6,
            )(ids, protos, emb_a, emb_b, view_a, view_b, parts[0])
        plan, part = call(
            functools.partial(sweep_kernel, False, shares),
            (kept, shape(1, all_rows)),
            "sweep",
            scratch=work,
            aliases={0: 0},
            limit=4,
        )(plan, cols, sums, *parts, done)
    parts = exchange(part)
    own_cots, done = cotangent((own, all_rows), lambda ids: ids[0] >> 1)(ids, protos, view_a, view_b, parts[0])
    pieces = shape(shares, rows // shares, width)
    col_dual, row_dual, keep, give = call(
        functools.partial(embed_kernel, shares),
        (shape(count, 128), shape(1, all_rows), pieces, pieces),
        "embed_grad",
        scalars=1,
        scratch=work[:1] + [(F32, 2 * rows, width)],
        limit=8,
    )(ids, plan, cols, sums, protos_t, entries, cots, *parts, done)
    half = lambda number, outs: call(functools.partial(proto_kernel, number), outs, "proto_grad", scalars=1, limit=6)
    second, done = half(0, (shape(own, width), token))(ids, emb_a, own_entries, own_cots, second, col_dual, row_dual)
    near = call(add_kernel, pieces, "add", limit=2)(keep, swap(give, "proto", 1), done)
    embed_grad = near[0]
    for place, pair in list(enumerate(others()))[1:]:
        embed_grad = embed_grad + swap_both(near[place], *pair)
    proto_grad = half(1, (shape(own, width),))(ids, emb_b, own_entries, own_cots, second, col_dual, row_dual)[0]
    return embed_grad, proto_grad


def contract_rows(left, right):
    return mm(left, right, (((0,), (0,)), ((), ())))


def contract_width(left, right):
    return mm(left, right, NT)


def sum_over(value, axis):
    size = lax.axis_size(axis)
    parts = [value] + [swap(value, axis, step) for step in range(1, size)]
    return sum(parts[1:], parts[0])


def scatter_sum(value, axis):
    size = lax.axis_size(axis)
    me = lax.axis_index(axis)
    rows = value.shape[0] // size
    block = lambda owner: lax.dynamic_slice_in_dim(value, owner * rows, rows, 0)
    total = block(me)
    for step in range(1, size):
        total = total + swap(block(me ^ step), axis, step)
    return total


def split_plan(embeddings, second_view, prototypes, row_scale, col_scale):
    feat_width = embeddings.shape[1]
    proto_count = prototypes.shape[0]
    logit_scale = 1.0 / (0.05 * feat_width)
    view_scale = 1.0 / (0.1 * feat_width)
    plan_mass = 64.0 * proto_count * lax.axis_size("proto")

    logits = contract_width(embeddings, prototypes) * logit_scale
    plan = row_scale[:, None] * col_scale[None, :] * jnp.exp(logits) / plan_mass
    cotangent = -contract_width(second_view, prototypes) * view_scale
    weighted = plan * cotangent

    row_mass, row_weight = sum_over(jnp.stack((plan.sum(1), weighted.sum(1))), "proto")
    row_dual = row_weight / row_mass
    sums = jnp.stack((plan.sum(0), weighted.sum(0), (row_dual[:, None] * plan).sum(0)))
    col_mass, col_weight, product = sum_over(sums, "row")
    col_dual = (col_weight - product) / col_mass
    for sweep in range(ITERS - 1):
        product = sum_over((plan * col_dual[None, :]).sum(1), "proto")
        row_dual = (row_weight - product) / row_mass
        product = sum_over((plan * row_dual[:, None]).sum(0), "row")
        col_dual = (col_weight - product) / col_mass
    logit_grad = plan * (cotangent - row_dual[:, None] - col_dual[None, :])
    scaled_grad = (logit_scale * logit_grad).astype(jnp.bfloat16)
    scaled_plan = (-view_scale * plan).astype(jnp.bfloat16)
    embed_grad = scatter_sum(
        jnp.dot(scaled_grad, prototypes, preferred_element_type=jnp.float32), "proto"
    )
    proto_grad = scatter_sum(
        contract_rows(scaled_grad, embeddings) + contract_rows(scaled_plan, second_view), "row"
    )
    return (embed_grad, proto_grad)


def per_device(embeddings, second_view, prototypes, row_scale, col_scale):
    blocks, shares = lax.axis_size("row"), lax.axis_size("proto")
    rows, width = embeddings.shape
    count = prototypes.shape[0]
    fits = rows * blocks * count * 2 <= PLAN_BYTES
    even = all(n & (n - 1) == 0 and n > 1 for n in (blocks, shares))
    even = even and rows % (16 * shares) == 0 and rows % width == 0
    tiled = rows % 128 == 0 and width % 128 == 0 and count == blocks * CHUNK and blocks % 4 == 0
    form = kept_plan if fits and even and tiled else split_plan
    return form(embeddings, second_view, prototypes, row_scale, col_scale)


def solution(mesh):
    return jax.shard_map(
        per_device,
        mesh=mesh,
        in_specs=(P("row", None), P("row", None), P("proto", None), P("row"), P("proto")),
        out_specs=(P(("row", "proto"), None), P(("proto", "row"), None)),
        check_vma=False,
    )
```

```python
import functools
import math

import jax
import jax.numpy as jnp
from jax import lax
from jax.experimental import pallas as pl
from jax.experimental.pallas import tpu as pltpu
from jax.sharding import PartitionSpec as P

ITERS = 4
CHUNK = 512
STEP = 256
EXT = 16
PLAN_BYTES = 24 << 20
LOG2E = 1.4426950408889634
F32, BF16 = jnp.float32, jnp.bfloat16
NT = (((1,), (1,)), ((), ()))
NN = (((1,), (0,)), ((), ()))


def mm(left, right, dims=NN):
    return lax.dot_general(left, right, dims, preferred_element_type=F32)


def swap(value, axis, step):
    size = lax.axis_size(axis)
    return lax.ppermute(value, axis, [(i, i ^ step) for i in range(size)])


def lane_sums(block):
    return jnp.broadcast_to(jnp.sum(block, axis=1, keepdims=True), (block.shape[0], 128))


def widened(column, width):
    return jnp.concatenate([column] * (width // 128), 1)


def rows_of(pieces, height=EXT):
    index = lax.broadcasted_iota(jnp.int32, (height, pieces[0].shape[1]), 0)
    total = jnp.zeros(index.shape, F32)
    for place, piece in enumerate(pieces):
        total = jnp.where(index == place, piece, total)
    return total


def pieces_of(row):
    out = []
    for _ in range(3):
        out.append(row.astype(BF16).astype(F32))
        row = row - out[-1]
    return out, [jnp.ones_like(row)] * 3


def prep_kernel(logit_scale, ids, embeddings, second_view, row_scale, send_out):
    rows, width = embeddings.shape

    @pl.when(ids[1] & 1 == 0)
    def _():
        logs, ones = pieces_of(jnp.log(row_scale[...]) / logit_scale)
        send_out[0:width, :] = jnp.transpose(embeddings[...].astype(F32)).astype(BF16)
        send_out[width:width + EXT, :] = rows_of(logs + ones).astype(BF16)

    @pl.when(ids[1] & 1 != 0)
    def _():
        send_out[0:width, :] = jnp.transpose(second_view[...].astype(F32)).astype(BF16)
        send_out[width:width + EXT, :] = jnp.zeros((EXT, rows), BF16)


def turn_kernel(logit_scale, log_mass, ids, protos, col_scale, protos_out, protos_t, token):
    count = protos_out.shape[0]
    width = protos.shape[1]
    token[...] = jnp.zeros_like(token)

    def step(index, carry):
        here = pl.ds(pl.multiple_of(index * CHUNK, CHUNK), CHUNK)
        there = pl.ds(pl.multiple_of((2 * index + (ids[0] & 1)) * CHUNK, CHUNK), CHUNK)
        block = protos[there, :]
        logs, ones = pieces_of((jnp.log(col_scale[:, there]) - log_mass) / logit_scale)
        protos_out[here, 0:width] = block
        protos_out[here, width:] = jnp.transpose(rows_of(ones + logs, width)).astype(BF16)
        protos_t[:, here] = jnp.transpose(block.astype(F32)).astype(BF16)
        return carry

    lax.fori_loop(0, count // CHUNK, step, 0, unroll=True)


def stack_kernel(count, *refs):
    for place in range(count):
        refs[-1][place] = refs[place][...]


def add_kernel(left, right, *refs):
    refs[-1][...] = left[...] + right[...]


def plan_kernel(logit_scale, view_scale, second, ids, protos, mine, theirs, *refs):
    if second:
        _, cols_in, sums_in, *refs = refs
    plan_out, cols_out, sums_out, emb_ext, view_t, row_mass, row_weight = refs
    blocks, high, rows = mine.shape
    count = protos.shape[0]
    width = view_t.shape[0]
    scale = logit_scale * LOG2E
    left = blocks * rows if second else 0
    emb_ext[high:, :] = jnp.zeros((emb_ext.shape[0] - high, blocks * rows), BF16)

    def fill(emb, view):
        for block in range(blocks):
            cols = slice(block * rows, (block + 1) * rows)
            emb_ext[0:high, cols] = emb[block]
            view_t[:, cols] = view[block, 0:width, :]

    pl.when(ids[1] & 1 == 0)(lambda: fill(mine, theirs))
    pl.when(ids[1] & 1 != 0)(lambda: fill(theirs, mine))
    row_mass[...] = jnp.zeros_like(row_mass)
    row_weight[...] = jnp.zeros_like(row_weight)

    def folded(block):
        tiles = [block[:, left:left + 128] for left in range(0, block.shape[1], 128)]
        across = tiles[0]
        for tile in tiles[1:]:
            across = across + tile
        return across, jnp.sum(block.reshape(block.shape[0] // 8, 8, block.shape[1]), axis=0)

    def step(index, carry):
        here = pl.ds(pl.multiple_of(index * CHUNK, CHUNK), CHUNK)
        mass = cols_in[0, here, :] if second else jnp.zeros((CHUNK, 128), F32)
        weight = cols_in[1, here, :] if second else mass
        for block in range(blocks):
            cols = slice(block * rows, (block + 1) * rows)
            plan = jnp.exp2(scale * mm(protos[here, :], emb_ext[:, cols]))
            plan_out[here, left + block * rows:left + (block + 1) * rows] = plan
            across, down = folded(plan)
            mass = mass + across
            row_mass[:, cols] += down
            across, down = folded(plan * mm(protos[here, 0:width], view_t[:, cols]))
            weight = weight + across
            row_weight[:, cols] += down
        if second:
            mass = 1.0 / lane_sums(mass)
            weight = -view_scale * lane_sums(weight) * mass
        cols_out[0, here, :] = mass
        cols_out[1, here, :] = weight
        return carry

    lax.fori_loop(0, count // CHUNK, step, 0, unroll=True)
    if second:
        sums_out[:, 0:left] = sums_in[...]
    sums_out[0:1, left:] = jnp.sum(row_mass[...], axis=0, keepdims=True)
    sums_out[1:2, left:] = -view_scale * jnp.sum(row_weight[...], axis=0, keepdims=True)


def added(parts):
    plain, turned = parts[:len(parts) // 2], parts[len(parts) // 2:]
    total, other = plain[0][...], turned[0][...]
    for part in plain[1:]:
        total = total + part[...]
    for part in turned[1:]:
        other = other + part[...]
    half = other.shape[1] // 2
    return total + jnp.concatenate((other[:, half:], other[:, :half]), 1)


def by_rows(block, cols, here, spread):
    tall, wide = block.shape
    duals = []
    for top in range(0, tall, 64):
        group = [jnp.zeros((8, 128), F32) for _ in range(8)]
        for left in range(0, wide, 128):
            dual = spread[:, left:left + 128]
            for place in range(8):
                rows = slice(top + place * 8, top + (place + 1) * 8)
                group[place] = group[place] + block[rows, left:left + 128] * dual
        duals.append(lane_sums(jnp.concatenate(group)))
    return cols[1, here, :] - cols[0, here, :] * jnp.concatenate(duals)


def by_cols(block, column):
    tall, wide = block.shape
    sums = [jnp.zeros((8, 128), F32) for _ in range(wide // 128)]
    for top in range(0, tall, 8):
        dual = column[top:top + 8, :]
        for place in range(wide // 128):
            sums[place] = sums[place] + block[top:top + 8, place * 128:(place + 1) * 128] * dual
    return jnp.concatenate(sums, 1)


def chunk(index):
    return pl.ds(pl.multiple_of(index * STEP, STEP), STEP)


def sweep_kernel(opening, shares, plan, cols, *refs):
    if opening:
        parts, (_, _, sums_out, part_out, spread, total) = refs[:shares], refs[shares:]
        sums_out[...] = added(parts)
        row_dual = sums_out[1:2, :] / sums_out[0:1, :]
    else:
        (sums, *parts), (_, _, part_out, spread, total) = refs[:shares + 1], refs[shares + 1:]
        row_dual = (sums[1:2, :] - added(parts)) / sums[0:1, :]
    spread[...] = jnp.broadcast_to(row_dual, spread.shape)
    total[...] = jnp.zeros_like(total)
    steps = plan.shape[0] // STEP

    def duals(index):
        here = chunk(index)
        return by_rows(plan.at[here, :], cols, here, spread)

    def step(index, dual):
        product = by_cols(plan.at[chunk(index - 1), :], dual)
        dual = duals(index)
        total[...] += product
        return dual

    last = lax.fori_loop(1, steps, step, duals(0), unroll=True)
    total[...] += by_cols(plan.at[chunk(steps - 1), :], last)
    part_out[...] = jnp.sum(total[...], axis=0, keepdims=True)


def embed_before_kernel(logit_scale, protos, emb_a, emb_b, after, entry_out, token):
    del after
    scale = logit_scale * LOG2E
    token[...] = jnp.zeros_like(token)
    rows = entry_out.shape[1] // 2

    def step(index, carry):
        here = chunk(index)
        for half, emb in enumerate((emb_a, emb_b)):
            entry = jnp.exp2(scale * mm(protos[here, :], emb[:, 0:rows]))
            entry_out[here, half * rows:(half + 1) * rows] = logit_scale * entry
        return carry

    lax.fori_loop(0, protos.shape[0] // STEP, step, 0, unroll=2)


def cotangent_kernel(view_scale, block, ids, protos, view_a, view_b, after, cot_out, token):
    del after
    width = view_a.shape[0]
    tall, wide = cot_out.shape
    token[...] = jnp.zeros_like(token)
    first = pl.multiple_of(block(ids) * tall, tall)

    def step(index, carry):
        here = chunk(index)
        from_row = pl.ds(pl.multiple_of(first + index * STEP, STEP), STEP)
        for half, view in enumerate((view_a, view_b)):
            cot = mm(protos[from_row, 0:width], view[:, 0:wide // 2])
            cot_out[here, half * wide // 2:(half + 1) * wide // 2] = -view_scale * cot
        return carry

    lax.fori_loop(0, tall // STEP, step, 0, unroll=2)


def embed_kernel(shares, ids, plan, cols, sums, protos_t, entries, cots, *refs):
    parts, (_, duals_out, rows_out, keep, give, spread, whole) = refs[:shares], refs[shares:]
    width = protos_t.shape[0]
    rows = entries.shape[1]
    rows_out[...] = (sums[1:2, :] - added(parts)) / sums[0:1, :]
    spread[...] = jnp.broadcast_to(rows_out[...], spread.shape)
    split = rows_out.shape[1] // 2
    own_dual = jnp.concatenate((rows_out[:, 0:rows // 2], rows_out[:, split:split + rows // 2]), 1)

    def duals(index, carry):
        here = chunk(index)
        duals_out[here, :] = by_rows(plan.at[here, :], cols, here, spread)
        return carry

    lax.fori_loop(0, plan.shape[0] // STEP, duals, 0, unroll=4)
    total = jnp.zeros((width, rows), F32)
    for start in range(0, plan.shape[0], CHUNK):
        here = slice(start, start + CHUNK)
        grad = entries[here, :] * (cots[here, :] - own_dual - widened(duals_out[here, :], rows))
        total = total + mm(protos_t[:, here], grad.astype(BF16))
    whole[...] = jnp.transpose(total)
    tall = keep.shape[1]
    for place in range(shares):
        above, beside = divmod(place, shares // 2)
        to = above * shares + (ids[1] ^ (2 * beside))
        keep[place] = whole[pl.ds(pl.multiple_of(to * tall, tall), tall), :]
        give[place] = whole[pl.ds(pl.multiple_of((to ^ 1) * tall, tall), tall), :]


def proto_before_kernel(logit_scale, view_scale, ids, protos, emb_a, emb_b, view_a, view_b, after, entry_out, second_out, token):
    del after
    own, rows = entry_out.shape
    width = second_out.shape[1]
    scale = logit_scale * LOG2E
    token[...] = jnp.zeros_like(token)
    here = pl.ds(pl.multiple_of((ids[0] >> 1) * own, own), own)
    total = jnp.zeros((own, width), F32)
    for left, emb, view in ((0, emb_a, view_a), (rows // 2, emb_b, view_b)):
        for start in range(0, rows // 2, 2 * width):
            cols = slice(start, start + 2 * width)
            exact = jnp.exp2(scale * mm(protos[here, :], emb[:, cols]))
            entry_out[:, left + start:left + start + 2 * width] = logit_scale * exact
            total = total + mm((-view_scale * exact).astype(BF16), view[:, cols], NT)
    second_out[...] = total


def proto_kernel(half, ids, emb_ext, entries, cots, so_far, col_dual, row_dual, *outs):
    own, width = outs[0].shape
    here = pl.ds(pl.multiple_of((ids[0] >> 1) * own, own), own)
    column = widened(col_dual[here, :], 2 * width)
    total = so_far[...]
    some = entries.shape[1] // 2
    for start in range(0, some, 2 * width):
        cols = slice(half * some + start, half * some + start + 2 * width)
        grad = entries[:, cols] * (cots[:, cols] - row_dual[:, cols] - column)
        total = total + mm(grad.astype(BF16), emb_ext[0:width, start:start + 2 * width], NT)
    outs[0][...] = total
    for token in outs[1:]:
        token[...] = jnp.zeros_like(token)


def call(kernel, out_shape, name, scalars=0, scratch=(), aliases=None, limit=16):
    def run(*args):
        whole = pl.BlockSpec(memory_space=pltpu.VMEM)
        small = pl.BlockSpec(memory_space=pltpu.SMEM)
        return pl.pallas_call(
            kernel,
            out_shape=out_shape,
            in_specs=[small] * scalars + [whole] * (len(args) - scalars),
            out_specs=jax.tree.map(lambda _: whole, out_shape),
            scratch_shapes=[pltpu.VMEM(dims, dtype) for dtype, *dims in scratch],
            input_output_aliases=aliases or {},
            compiler_params=pltpu.CompilerParams(vmem_limit_bytes=limit << 20),
            name=name,
        )(*args)

    return run


def swap_both(value, above, beside):
    shares = lax.axis_size("proto")
    pairs = [
        (row * shares + col, (row ^ above) * shares + (col ^ beside))
        for row in range(lax.axis_size("row"))
        for col in range(shares)
    ]
    return lax.ppermute(value, ("row", "proto"), pairs)


def others():
    shares = lax.axis_size("proto")
    return [(above, beside) for above in range(2) for beside in range(0, shares, 2)]


def exchange(part):
    near = call(add_kernel, jax.ShapeDtypeStruct(part.shape, F32), "add", limit=2)(part, swap(part, "proto", 1))
    return [near if pair == (0, 0) else swap_both(near, *pair) for pair in others()]


def kept_plan(embeddings, second_view, prototypes, row_scale, col_scale):
    rows, width = embeddings.shape
    blocks, shares = lax.axis_size("row"), lax.axis_size("proto")
    all_rows = rows * blocks
    count = prototypes.shape[0] // 2
    own = 2 * count // blocks
    ids = jnp.stack((lax.axis_index("row"), lax.axis_index("proto")))
    scales = (1.0 / (0.05 * width), 1.0 / (0.1 * width))
    log_mass = math.log(64.0 * prototypes.shape[0] * shares)
    shape = lambda *dims, dtype=F32: jax.ShapeDtypeStruct(dims, dtype)
    form = lambda kernel: functools.partial(kernel, *scales)
    there = lambda value: pltpu.with_memory_space_constraint(value, pltpu.HBM)
    row_scale = row_scale.reshape(1, rows)
    col_scale = col_scale.reshape(1, 2 * count)
    half = shape(width + EXT, rows, dtype=BF16)
    send = call(functools.partial(prep_kernel, scales[0]), half, "prepare", scalars=1)(
        ids, there(embeddings), there(second_view), there(row_scale)
    )
    protos, protos_t, token = call(
        functools.partial(turn_kernel, scales[0], log_mass),
        (shape(count, 2 * width, dtype=BF16), shape(width, count, dtype=BF16), shape(8, 128)),
        "turn",
        scalars=1,
        limit=4,
    )(ids, there(prototypes), there(col_scale))
    pairs = blocks // 2
    stack = call(functools.partial(stack_kernel, pairs), shape(pairs, width + EXT, rows, dtype=BF16), "stack", limit=2)
    direct = [send] + [swap(send, "row", step) for step in range(2, blocks, 2)]
    mine_a = stack(*direct, token)
    theirs_a = swap(mine_a, "proto", 1)
    mine_b = stack(*[swap(value, "row", 1) for value in direct])
    theirs_b = swap(mine_b, "proto", 1)

    kept = pltpu.VMEM((count, all_rows), F32)
    some = all_rows // 2
    turned = (shape(2 * width, some, dtype=BF16), shape(width, some, dtype=BF16))
    work = [(F32, 8, some), (F32, 8, some)]
    plan, cols, sums, emb_a, view_a = call(
        functools.partial(plan_kernel, *scales, False),
        (kept, shape(2, count, 128), shape(2, some)) + turned,
        "plan_ours",
        scalars=1,
        scratch=work,
        limit=12,
    )(ids, protos, mine_a, theirs_a)
    plan, cols, sums, emb_b, view_b = call(
        functools.partial(plan_kernel, *scales, True),
        (kept, shape(2, count, 128), shape(2, all_rows)) + turned,
        "plan_theirs",
        scalars=1,
        scratch=work,
        aliases={4: 0},
        limit=12,
    )(ids, protos, mine_b, theirs_b, plan, cols, sums)

    work = [(F32, 8, all_rows), (F32, 8, all_rows)]
    token = shape(8, 128)
    parts = exchange(sums)
    entries, done = call(
        functools.partial(embed_before_kernel, scales[0]),
        (shape(count, 2 * rows), token),
        "embed_before",
        limit=6,
    )(protos, emb_a, emb_b, parts[0])
    plan, sums, part = call(
        functools.partial(sweep_kernel, True, shares),
        (kept, shape(2, all_rows), shape(1, all_rows)),
        "sweep",
        scratch=work,
        aliases={0: 0},
        limit=4,
    )(plan, cols, *parts, done)
    cotangent = lambda dims, block: call(
        functools.partial(cotangent_kernel, scales[1], block), (shape(*dims), token), "cotangent", scalars=1, limit=4
    )
    for sweep in range(ITERS - 2):
        parts = exchange(part)
        if sweep == ITERS - 3:
            cots, done = cotangent((count, 2 * rows), lambda ids: 0)(ids, protos, view_a, view_b, parts[0])
        if sweep == 0:
            own_entries, second, done = call(
                form(proto_before_kernel),
                (shape(own, all_rows), shape(own, width), token),
                "proto_before",
                scalars=1,
                limit=6,
            )(ids, protos, emb_a, emb_b, view_a, view_b, parts[0])
        plan, part = call(
            functools.partial(sweep_kernel, False, shares),
            (kept, shape(1, all_rows)),
            "sweep",
            scratch=work,
            aliases={0: 0},
            limit=4,
        )(plan, cols, sums, *parts, done)
    parts = exchange(part)
    own_cots, done = cotangent((own, all_rows), lambda ids: ids[0] >> 1)(ids, protos, view_a, view_b, parts[0])
    pieces = shape(shares, rows // shares, width)
    col_dual, row_dual, keep, give = call(
        functools.partial(embed_kernel, shares),
        (shape(count, 128), shape(1, all_rows), pieces, pieces),
        "embed_grad",
        scalars=1,
        scratch=work[:1] + [(F32, 2 * rows, width)],
        limit=8,
    )(ids, plan, cols, sums, protos_t, entries, cots, *parts, done)
    half = lambda number, outs: call(functools.partial(proto_kernel, number), outs, "proto_grad", scalars=1, limit=6)
    second, done = half(0, (shape(own, width), token))(ids, emb_a, own_entries, own_cots, second, col_dual, row_dual)
    near = call(add_kernel, pieces, "add", limit=2)(keep, swap(give, "proto", 1), done)
    embed_grad = near[0]
    for place, pair in list(enumerate(others()))[1:]:
        embed_grad = embed_grad + swap_both(near[place], *pair)
    proto_grad = half(1, (shape(own, width),))(ids, emb_b, own_entries, own_cots, second, col_dual, row_dual)[0]
    return embed_grad, proto_grad


def contract_rows(left, right):
    return mm(left, right, (((0,), (0,)), ((), ())))


def contract_width(left, right):
    return mm(left, right, NT)


def sum_over(value, axis):
    size = lax.axis_size(axis)
    parts = [value] + [swap(value, axis, step) for step in range(1, size)]
    return sum(parts[1:], parts[0])


def scatter_sum(value, axis):
    size = lax.axis_size(axis)
    me = lax.axis_index(axis)
    rows = value.shape[0] // size
    block = lambda owner: lax.dynamic_slice_in_dim(value, owner * rows, rows, 0)
    total = block(me)
    for step in range(1, size):
        total = total + swap(block(me ^ step), axis, step)
    return total


def split_plan(embeddings, second_view, prototypes, row_scale, col_scale):
    feat_width = embeddings.shape[1]
    proto_count = prototypes.shape[0]
    logit_scale = 1.0 / (0.05 * feat_width)
    view_scale = 1.0 / (0.1 * feat_width)
    plan_mass = 64.0 * proto_count * lax.axis_size("proto")

    logits = contract_width(embeddings, prototypes) * logit_scale
    plan = row_scale[:, None] * col_scale[None, :] * jnp.exp(logits) / plan_mass
    cotangent = -contract_width(second_view, prototypes) * view_scale
    weighted = plan * cotangent

    row_mass, row_weight = sum_over(jnp.stack((plan.sum(1), weighted.sum(1))), "proto")
    row_dual = row_weight / row_mass
    sums = jnp.stack((plan.sum(0), weighted.sum(0), (row_dual[:, None] * plan).sum(0)))
    col_mass, col_weight, product = sum_over(sums, "row")
    col_dual = (col_weight - product) / col_mass
    for sweep in range(ITERS - 1):
        product = sum_over((plan * col_dual[None, :]).sum(1), "proto")
        row_dual = (row_weight - product) / row_mass
        product = sum_over((plan * row_dual[:, None]).sum(0), "row")
        col_dual = (col_weight - product) / col_mass
    logit_grad = plan * (cotangent - row_dual[:, None] - col_dual[None, :])
    scaled_grad = (logit_scale * logit_grad).astype(jnp.bfloat16)
    scaled_plan = (-view_scale * plan).astype(jnp.bfloat16)
    embed_grad = scatter_sum(
        jnp.dot(scaled_grad, prototypes, preferred_element_type=jnp.float32), "proto"
    )
    proto_grad = scatter_sum(
        contract_rows(scaled_grad, embeddings) + contract_rows(scaled_plan, second_view), "row"
    )
    return (embed_grad, proto_grad)


def per_device(embeddings, second_view, prototypes, row_scale, col_scale):
    blocks, shares = lax.axis_size("row"), lax.axis_size("proto")
    rows, width = embeddings.shape
    count = prototypes.shape[0]
    fits = rows * blocks * count * 2 <= PLAN_BYTES
    even = all(n & (n - 1) == 0 and n > 1 for n in (blocks, shares))
    even = even and rows % (16 * shares) == 0 and rows % width == 0
    tiled = rows % 128 == 0 and width % 128 == 0 and count == blocks * CHUNK and blocks % 4 == 0
    form = kept_plan if fits and even and tiled else split_plan
    return form(embeddings, second_view, prototypes, row_scale, col_scale)


def solution(mesh):
    return jax.shard_map(
        per_device,
        mesh=mesh,
        in_specs=(P("row", None), P("row", None), P("proto", None), P("row"), P("proto")),
        out_specs=(P(("row", "proto"), None), P(("proto", "row"), None)),
        check_vma=False,
    )
```
